32 devices in a mesh: batch: 8 (over z, x), expert: 4 (over y, core).
Axes of the slice: x: 2, y: 2, z: 4, core: 2. Of those that a mesh axis runs over, the one named last changes fastest.
Arguments:
- emb_table: bfloat16 [524288, 16], P('batch'), may hold values from -6 to 6
- dense_feats: bfloat16 [13, 20480], P(None, ('batch', 'expert')), may hold values from -5 to 5
- dense_w: bfloat16 [13, 96], replicated, may hold values from -1.75 to 1.75
- gate_w: bfloat16 [512, 8], replicated, may hold values from -0.1796875 to 0.1796875
- hidden_w: bfloat16 [4, 512, 256], P('expert'), may hold values from -0.25 to 0.25
- hidden_b: float32 [4, 256], P('expert'), may hold values from -0.6 to 0.6
- output_w: bfloat16 [4, 256, 128], P('expert'), may hold values from -0.375 to 0.375
- output_b: float32 [4, 128], P('expert'), may hold values from -0.6 to 0.6
- tower_w: bfloat16 [128, 128], replicated, may hold values from -0.5 to 0.5
- tower_b: float32 [128], replicated, may hold values from -0.6 to 0.6
- head_w: float32 [128], replicated, may hold values from -0.75 to 0.75
- head_b: float32 [2], replicated, may hold values from -1 to 1
- row_owner: int32 [532480, 1], P(('batch', 'expert')), may hold values from 0 to 7; in each aligned block of 4160 rows (0 to 4159, 4160 to 8319, ...) at most 1040 rows name the same one
- local_row: int32 [532480], P(('batch', 'expert')), may hold values from 0 to 65535
- labels: int32 [2, 20480], P(None, ('batch', 'expert')), may hold values 0 or 1
Outputs:
- grad_table: float32 [524288, 16], P('batch')
- grad_dense: float32 [13, 20480], P(None, ('batch', 'expert'))
- grad_dense_w: float32 [13, 96], replicated
- grad_gate: float32 [512, 8], replicated
- grad_hidden_w: float32 [4, 512, 256], P('expert')
- grad_hidden_b: float32 [4, 256], P('expert')
- grad_output_w: float32 [4, 256, 128], P('expert')
- grad_output_b: float32 [4, 128], P('expert')
- grad_tower_w: float32 [128, 128], replicated
- grad_tower_b: float32 [128], replicated
- grad_head_w: float32 [128], replicated
- grad_head_b: float32 [2], replicated
The draws below stay inside these ranges and needn't reach their ends.
Inputs may be any that keep to these rules, and one draw needn't show every extreme that they name: `row_owner`: within each device's lookups of one micro-batch (aligned blocks of 4160 entries) no owner is named more than 1040 times, a bound that some block reaches.
All inputs are finite; a program needn't handle non-finite values. No bound on the sum of `labels` on one device may be relied on, other than what follows from the above.
Results may differ from the reference program's by a relative error of at most 0.017.
Values may be sent and summed in bfloat16 or wider, within the bound.
No kernel may reach another device: no remote copies, remote signals or barrier semaphores. Data moves between devices by JAX's collectives and lax.ppermute only.
A program may use at most 384 MiB of HBM per device.

```python
import math
import jax
import jax.numpy as jnp
import numpy as np
from jax import lax

FIELDS = 26
EMB = 16
DENSE = 13
BOTTOM = 96
D_IN = 512
H1 = 256
H2 = 128
TOWER = 64
TASKS = 2
MB_ROWS = 160
TAB_DEV = 65536
TOKENS = 20480
EXPERTS = 4
VOCAB = 524288
LOOKUPS = 532480
CAP = 1040
N_BATCH = 8
N_EXPERT = 4


def place_ends(result, rng, smallest, top_value):
    longest = result.shape.index(max(result.shape))
    spots = []
    for shift in (0, 1):
        where = [jax.random.randint(jax.random.fold_in(rng, axis), (), 0, length) for axis, length in enumerate(result.shape)]
        where[longest] = (where[longest] + shift) % result.shape[longest]
        spots.append(tuple(where))
    return result.at[spots[0]].set(smallest).at[spots[1]].set(top_value)


def levels(rng, dims, split, least, top_value):
    def one(dim, blocks):
        draws = jax.random.uniform(jax.random.fold_in(jax.random.fold_in(rng, 6), dim), (blocks,), jnp.float32, least / len(split), top_value / len(split))
        return jnp.repeat(jnp.exp(draws), dims[dim] // blocks).reshape((-1,) + (1,) * (len(dims) - dim - 1))

    loudness = one(*split[0])
    for cut in split[1:]:
        loudness = loudness * one(*cut)
    return loudness


def rank_table(count, lean):
    loads = [(1 << 20) // math.isqrt(grade ** lean) + 1 for grade in range(1, count + 1)]
    spread = 1 + sum(loads) // (1 << 30)
    return np.cumsum(np.array([max(1, weight // spread) for weight in loads]))


def ranked_ids(rng, dims, amount, skew):
    table = rank_table(amount, skew)
    pick = jax.random.randint(jax.random.fold_in(rng, 1), dims, 0, int(table[amount - 1]))
    standing = jnp.searchsorted(jnp.asarray(table, jnp.int32), pick, side="right")
    return jax.random.permutation(jax.random.fold_in(rng, 2), amount)[standing].astype(jnp.int32)


def routed_block(key, own, number, rows, number_of, top, limit, skew):
    sequence = jax.random.permutation(key, number_of)
    crowded, ordinary = load_shares(number_of, rows * top, limit, skew, True), load_shares(number_of, rows * top, limit, skew, False)
    places = jnp.arange(number_of)

    def named(sizes, rotation):
        used = int((sizes > 0).sum())
        fixed = max(1, used // 4)
        moved = fixed + (places - fixed + rotation * (used - fixed)) % max(1, number_of - fixed)
        return jnp.zeros((number_of,), jnp.int32).at[sequence[jnp.where(places < fixed, places, moved)]].set(jnp.asarray(sizes, jnp.int32))

    sizes = jnp.where(number % 4 == 0, named(crowded, number // 4), named(ordinary, number - number // 4 - 1))
    mixed = jax.random.permutation(jax.random.fold_in(own, 3), number_of)
    giver, sink = mixed[0:number_of // 2 * 2:2], mixed[1:number_of // 2 * 2:2]
    slack = jnp.minimum(sizes[giver] - 1, limit - sizes[sink]) // 2
    slack = jnp.where((giver == sequence[0]) | (sink == sequence[0]) | (sizes[sink] == 0), 0, jnp.maximum(slack, 0))
    moved = jax.random.randint(jax.random.fold_in(own, 4), (number_of // 2,), 0, 1 << 20) % (slack + 1)
    sizes = sizes.at[giver].add(-moved).at[sink].add(moved)
    items = jnp.searchsorted(jnp.cumsum(sizes), jnp.arange(rows * top), side="right").astype(jnp.int32)
    listing = items.reshape(top, rows).T
    listing = listing[jax.random.permutation(jax.random.fold_in(own, 1), rows)]
    rotation = jax.random.randint(jax.random.fold_in(own, 2), (rows, 1), 0, top)
    return jnp.take_along_axis(listing, (jnp.arange(top)[None, :] + rotation) % top, axis=1)


def load_shares(count, total, bound, skew, full):
    weights = [(1 << 20) // math.isqrt(rank ** skew) + 1 for rank in range(1, count + 1)]
    largest = bound if full else min(bound, max(-(-total // count), total * weights[0] // sum(weights)))
    least = 1 if total - largest >= count - 1 else 0
    counts, surplus = [largest] + [least] * (count - 1), total - largest - least * (count - 1)
    while surplus > 0:
        candidates = [i for i in range(1, count) if counts[i] < largest] or [i for i in range(1, count) if counts[i] < bound]
        whole, remaining = sum([weights[i] for i in candidates]), surplus
        for i in candidates:
            more = min(bound - counts[i], max(1, remaining * weights[i] // whole), surplus)
            counts[i] = counts[i] + more
            surplus = surplus - more
    return np.array(counts)


def gaussian(stream_key, extent, width, limit, split=(), dtype=jnp.bfloat16):
    drawn = jax.random.normal(stream_key, extent, jnp.float32) * width
    if len(split) > 0:
        drawn = levels(stream_key, extent, split, -0.22, 0.18) * drawn
    return jnp.clip(drawn, min=-limit, max=limit).astype(dtype)


def setup_inputs(seed: int = 0) -> dict:
    key_of = jax.random.split(jax.random.key(seed), 16)
    emb_table = gaussian(key_of[0], (VOCAB, EMB), 1.0, 6.0, ((0, 8),))
    dense_feats = gaussian(key_of[1], (DENSE, TOKENS), 1.0, 5.0, ((1, 32),))
    dense_w = gaussian(key_of[2], (DENSE, BOTTOM), DENSE ** -0.5, 1.75)
    gate_w = gaussian(key_of[3], (D_IN, TASKS * EXPERTS), 0.03, 0.1796875)
    hidden_w = gaussian(key_of[4], (EXPERTS, D_IN, H1), D_IN ** -0.5, 0.25, ((0, 4),))
    hidden_b = gaussian(key_of[5], (EXPERTS, H1), 0.1, 0.6, ((0, 4),), jnp.float32)
    output_w = gaussian(key_of[6], (EXPERTS, H1, H2), H1 ** -0.5, 0.375, ((0, 4),))
    output_b = gaussian(key_of[7], (EXPERTS, H2), 0.1, 0.6, ((0, 4),), jnp.float32)
    tower_w = gaussian(key_of[8], (H2, TASKS * TOWER), H2 ** -0.5, 0.5)
    tower_b = gaussian(key_of[9], (TASKS * TOWER,), 0.1, 0.6, (), jnp.float32)
    head_w = gaussian(key_of[10], (TASKS * TOWER,), TOWER ** -0.5, 0.75, (), jnp.float32)
    head_b = gaussian(key_of[11], (TASKS,), 0.3, 1.0, (), jnp.float32)
    row_owner_keys = jax.random.split(jax.random.fold_in(key_of[12], 1), LOOKUPS // (MB_ROWS * FIELDS))
    row_owner_turns = jax.random.permutation(jax.random.fold_in(key_of[12], 3), LOOKUPS // (MB_ROWS * FIELDS))
    row_owner = jax.vmap(lambda own, number: routed_block(jax.random.fold_in(key_of[12], 2), own, number, MB_ROWS * FIELDS, N_BATCH, 1, CAP, 2))(row_owner_keys, row_owner_turns).reshape((LOOKUPS, 1))
    local_row = place_ends(ranked_ids(key_of[13], (LOOKUPS,), TAB_DEV, 2), jax.random.fold_in(key_of[13], 3), 0, TAB_DEV - 1).astype(jnp.int32)
    labels = place_ends((jax.random.randint(key_of[14], (TASKS, TOKENS), 0, 4) < 1).astype(jnp.int32), jax.random.fold_in(key_of[14], 1), 0, 1)
    return {"emb_table": emb_table, "dense_feats": dense_feats, "dense_w": dense_w, "gate_w": gate_w, "hidden_w": hidden_w, "hidden_b": hidden_b, "output_w": output_w, "output_b": output_b, "tower_w": tower_w, "tower_b": tower_b, "head_w": head_w, "head_b": head_b, "row_owner": row_owner, "local_row": local_row, "labels": labels}


@jax.custom_vjp
def low(v):
    return lax.optimization_barrier(v.astype(jnp.bfloat16)).astype(jnp.float32)

@jax.custom_vjp
def low_back(v):
    return v

def low_keep(v):
    return (low(v), None)

def low_pass(kept, grad):
    return (grad,)

def back_keep(v):
    return (v, None)

def back_low(kept, grad):
    return (low(grad),)
low.defvjp(low_keep, low_pass)
low_back.defvjp(back_keep, back_low)

def forward(emb_table, dense_feats, dense_w, gate_w, hidden_w, hidden_b, output_w, output_b, tower_w, tower_b, head_w, head_b, row_ids, label_vals):
    highest = lax.Precision.HIGHEST
    block_rows = MB_ROWS * N_EXPERT
    blocks = TOKENS // block_rows
    id_blocks = row_ids.reshape(blocks, block_rows * FIELDS)
    dense_blocks = dense_feats.reshape(DENSE, blocks, block_rows).transpose(1, 0, 2)
    label_blocks = label_vals.reshape(TASKS, blocks, block_rows).transpose(1, 0, 2)
    tower_cube = tower_w.reshape(H2, TASKS, TOWER)

    def one_block(piece):
        block_ids, dense_part, label_part = piece
        embedded = jnp.take(emb_table, block_ids, axis=0).reshape(block_rows, FIELDS * EMB)
        bottom = jnp.dot(dense_part.T, dense_w, precision=highest)
        features = low(low_back(jnp.concatenate([embedded, bottom], axis=1)))
        logits = low_back(jnp.dot(features, gate_w, precision=highest)).reshape(block_rows, TASKS, EXPERTS)
        gates = jax.nn.softmax(logits, axis=-1)
        pre_hidden = low_back(jnp.einsum('rd,edh->reh', features, hidden_w, precision=highest) + hidden_b[None])
        hidden = low(jax.nn.silu(pre_hidden))
        pre_output = low_back(jnp.einsum('reh,ehf->ref', hidden, output_w, precision=highest) + output_b[None])
        outputs = jax.nn.silu(pre_output)
        mixed = jnp.einsum('rke,ref->rkf', gates, outputs, precision=highest)
        mixed_low = low(low_back(mixed))
        pre_tower = low_back(jnp.einsum('rkf,fkj->rkj', mixed_low, tower_cube, precision=highest) + tower_b.reshape(TASKS, TOWER)[None])
        tower_act = jax.nn.silu(pre_tower)
        scores = lax.optimization_barrier(jnp.sum(tower_act * head_w.reshape(TASKS, TOWER)[None], axis=-1)) + head_b[None]
        losses = jax.nn.softplus(scores) - label_part.T * scores
        return jnp.sum(losses) / jnp.sqrt(jnp.float32(TOKENS))

    def step(total, piece):
        return (total + jax.checkpoint(one_block)(piece), None)
    total, _ = lax.scan(step, jnp.zeros((), jnp.float32), (id_blocks, dense_blocks, label_blocks))
    return total

def reference(emb_table, dense_feats, dense_w, gate_w, hidden_w, hidden_b, output_w, output_b, tower_w, tower_b, head_w, head_b, row_owner, local_row, labels):
    row_ids = (row_owner[:, 0] * TAB_DEV + local_row).astype(jnp.int32)
    label_vals = labels.astype(jnp.float32)
    params = (emb_table.astype(jnp.float32), dense_feats.astype(jnp.float32), dense_w.astype(jnp.float32), gate_w.astype(jnp.float32), hidden_w.astype(jnp.float32), hidden_b.astype(jnp.float32), output_w.astype(jnp.float32), output_b.astype(jnp.float32), tower_w.astype(jnp.float32), tower_b.astype(jnp.float32), head_w.astype(jnp.float32), head_b.astype(jnp.float32))

    def loss_of(*values):
        return forward(*values, row_ids, label_vals)
    loss, pullback = jax.vjp(loss_of, *params)
    grads = pullback(jnp.ones_like(loss))
    return (grads[0], grads[1], grads[2], grads[3], grads[4], grads[5], grads[6], grads[7], grads[8], grads[9], grads[10], grads[11])
```

```python
import functools
import math

import jax
import jax.numpy as jnp
from jax import lax
from jax.experimental import pallas as pl
from jax.experimental.pallas import tpu as pltpu
from jax.sharding import PartitionSpec as P

FIELDS = 26
EMB = 16
DENSE = 13
BOTTOM = 96
D_IN = 512
H1 = 256
H2 = 128
TOWER = 64
TASKS = 2
LANES = 128
GROUPS = LANES // EMB
EMB_WIDTH = FIELDS * EMB
BIAS_ROWS = 16
WEIGHT_ROWS = 2 * D_IN + H1 + BIAS_ROWS
STREAMS = 8
PARTS = 2
CHUNK_ROWS = 64
VMEM_BYTES = 56 << 20

F32 = jnp.float32
BF16 = jnp.bfloat16
I32 = jnp.int32


def iota(shape, axis):
    return lax.broadcasted_iota(I32, shape, axis)


def matmul(a, b):
    return lax.dot_general(a, b, (((1,), (0,)), ((), ())), preferred_element_type=F32)


def matmul_nt(a, b):
    return lax.dot_general(a, b, (((1,), (1,)), ((), ())), preferred_element_type=F32)


def matmul_tn(a, b):
    return lax.dot_general(a, b, (((0,), (0,)), ((), ())), preferred_element_type=F32)


def identity():
    return (iota((LANES, LANES), 0) == iota((LANES, LANES), 1)).astype(BF16)


def aligned(value, step):
    return pl.multiple_of(value, step)


def silu_parts(values):
    sig = jax.nn.sigmoid(values)
    return values * sig, sig * (1.0 + values * (1.0 - sig))


def route_kernel(
    owners, part_lookups, packed, table_lanes, owner_ref, local_ref, request_ref, back_ref, out_ref,
    high_ref, low_ref, value_ref, total_ref
):
    rows = high_ref.shape[0]
    filled = owner_ref.shape[0]
    slot_rows = request_ref.shape[0]
    shape = (rows, LANES)
    high_ref[...] = jnp.full(shape, -1, I32)
    high_ref[0:filled, :] = owner_ref[...]
    owner = high_ref[...]
    low_ref[...] = jnp.zeros(shape, I32)
    low_ref[0:filled, :] = local_ref[...]
    local = low_ref[...]
    row_id = iota(shape, 0)
    tri = (iota((LANES, LANES), 0) <= iota((LANES, LANES), 1)).astype(BF16)
    ones = jnp.ones((LANES, LANES), BF16)
    before = (iota((rows, rows), 1) < iota((rows, rows), 0)).astype(BF16)
    part_rows = part_lookups // LANES
    rank = jnp.zeros(shape, F32)
    part_id = jnp.zeros(shape, I32)
    for part in range(1, PARTS):
        part_id = part_id + jnp.where(row_id >= part * part_rows, 1, 0)
    for part in range(PARTS):
        for one in range(owners):
            hit = (part_id == part) & (owner == one)
            hits = jnp.where(hit, 1.0, 0.0).astype(BF16)
            upto = matmul(hits, tri)
            ahead = matmul(before, matmul(hits, ones).astype(BF16))
            rank = jnp.where(hit, upto + ahead - 1.0, rank)
    rank = rank.astype(I32)
    group = jnp.zeros(shape, I32)
    for step in range(1, GROUPS):
        group = group + jnp.where(rank >= step * packed, 1, 0)
    place = rank - group * packed
    held = jnp.maximum(owner, 0)
    block = (held * PARTS + part_id) * (packed // 16) + lax.shift_right_logical(place, 4)
    inside = group * 16 + (place & 15)
    table_group = lax.shift_right_logical(local, table_lanes)
    table_row = local & ((1 << table_lanes) - 1)
    high_ref[...] = jnp.where(owner < 0, -1, block)
    low_ref[...] = inside
    value_ref[...] = table_row + (((group - table_group) & (GROUPS - 1)) << table_lanes)
    lookup = row_id * LANES + iota(shape, 1)
    quotient = jnp.floor((lookup.astype(F32) + 0.5) * (1.0 / FIELDS)).astype(I32)
    field_group = (lookup - quotient * FIELDS) & (GROUPS - 1)
    offset = 8 - (quotient & 7)
    turn = (field_group - group) & (GROUPS - 1)
    back_ref[...] = (turn * owners + held) * packed + place + offset
    out_ref[...] = block * LANES + inside + offset
    total_ref[...] = jnp.zeros_like(total_ref)

    def gather_requests(step, carry):
        base = aligned(step * 8, 8)
        high = high_ref[pl.ds(base, 8), :]
        low = low_ref[pl.ds(base, 8), :]
        values = value_ref[pl.ds(base, 8), :]
        upper = lax.shift_right_logical(values, 8).astype(F32)
        lower = (values & 255).astype(F32)
        at_high = []
        at_low = []
        for k in range(8):
            line = slice(k, k + 1)
            at_high.append(jnp.where(iota((slot_rows, LANES), 0) == high[line], 1.0, 0.0).astype(BF16))
            same = iota((LANES, LANES), 0) == low[line]
            at_low.append(
                jnp.concatenate(
                    [jnp.where(same, upper[line], 0.0), jnp.where(same, lower[line], 0.0)], axis=0
                ).astype(BF16)
            )
        total_ref[...] += matmul_nt(
            jnp.concatenate(at_high, axis=1), jnp.concatenate(at_low, axis=1)
        )
        return carry

    lax.fori_loop(0, rows // 8, gather_requests, 0, unroll=2)
    request_ref[...] = (total_ref[:, :LANES] * 256.0 + total_ref[:, LANES:]).astype(I32)


def pack_kernel(
    table_ref, hidden_w_ref, output_w_ref, hidden_b_ref, output_b_ref, packed_ref, weight_ref
):
    lines = []
    for values in (hidden_b_ref[:, :LANES], hidden_b_ref[:, LANES:], output_b_ref[...]):
        for _ in range(3):
            term = values.astype(BF16).astype(F32)
            lines.append(term)
            values = values - term
    lines.append(jnp.zeros((BIAS_ROWS - len(lines), LANES), F32))
    for half in range(H1 // LANES):
        weight_ref[half * D_IN : (half + 1) * D_IN, :] = hidden_w_ref[
            0, :, half * LANES : (half + 1) * LANES
        ]
    weight_ref[2 * D_IN : 2 * D_IN + H1, :] = output_w_ref[0]
    weight_ref[2 * D_IN + H1 :, :] = jnp.concatenate(lines, axis=0).astype(BF16)
    rows = table_ref.shape[1] // GROUPS
    eye = identity()

    def step(block, carry):
        pieces = []
        for group in range(GROUPS):
            start = aligned(group * rows + block * LANES, LANES)
            pieces.append(table_ref[:, pl.ds(start, LANES)])
        packed_ref[pl.ds(aligned(8 + block * LANES, 8), LANES), :] = matmul_nt(
            eye, jnp.concatenate(pieces, axis=0)
        )
        return carry

    packed_ref[0:8, :] = jnp.zeros((8, LANES), F32)
    packed_ref[8 + rows : 16 + rows, :] = jnp.zeros((8, LANES), F32)

    lax.fori_loop(0, rows // LANES, step, 0, unroll=8)


def masks():
    line = iota((8, LANES), 0)
    group = lax.shift_right_logical(iota((8, LANES), 1), 4)
    return [line == k for k in range(8)], [group == one for one in range(GROUPS)]


def turn_copies(rows_ref, wide_ref):
    rows = rows_ref.shape[0]
    half = GROUPS // 2
    from_lane = iota((LANES, half * LANES), 0)
    to_lane = iota((LANES, half * LANES), 1)
    turn = (lax.shift_right_logical(to_lane, 7) + half) * EMB
    turns = jnp.where(((from_lane + turn - to_lane) & (LANES - 1)) == 0, 1.0, 0.0).astype(BF16)

    def step(block, carry):
        start = aligned(block * LANES, LANES)
        piece = rows_ref[pl.ds(start, LANES), :]
        moved = matmul(piece, turns)
        piece = piece.astype(F32)
        for turn in range(GROUPS):
            if turn >= half:
                one = moved[:, (turn - half) * LANES : (turn - half + 1) * LANES]
            else:
                one = pltpu.roll(piece, turn * EMB, 1) if turn else piece
            wide_ref[pl.ds(aligned(8 + turn * rows + start, 8), LANES), :] = one
        return carry

    blocks = rows // LANES
    unroll = [count for count in (4, 3, 2, 1) if blocks % count == 0][0]
    lax.fori_loop(0, blocks, step, 0, unroll=unroll)


def assemble(wide_ref, word, groups, lines, lanes):
    block = jnp.zeros((8, LANES), F32)
    for place, group in groups:
        piece = wide_ref[pl.ds(word(0, place), 8), :]
        for k in range(1, 8):
            piece = jnp.where(lines[k], wide_ref[pl.ds(word(k, place), 8), :], piece)
        block = jnp.where(lanes[group], piece, block)
    return block


def word_stream(word_ref, buffers, sems, first, stride, count, process):
    slots = len(buffers)
    size = buffers[0].shape[0]

    def copy(at, slot):
        start = aligned(first + at * stride, LANES)
        return pltpu.make_async_copy(
            word_ref.at[pl.ds(start, size)], buffers[slot], sems.at[slot]
        )

    for slot in range(min(slots, count)):
        copy(slot, slot).start()

    def step(turn, carry):
        for slot in range(slots):
            at = turn * slots + slot
            copy(at, slot).wait()
            process(at, buffers[slot])

            @pl.when(at + slots < count)
            def _():
                copy(at + slots, slot).start()

        return carry

    lax.fori_loop(0, count // slots, step, 0)
    for slot in range(count % slots):
        at = count // slots * slots + slot
        copy(at, slot).wait()
        process(at, buffers[slot])


def slot_lines(numbers):
    own = (iota((16, LANES), 1) & 15) == iota((16, LANES), 0)
    return jnp.concatenate(
        [jnp.where(own, numbers[row : row + 1], 0.0) for row in range(numbers.shape[0])], axis=0
    ).astype(BF16)


def same_group():
    return (
        lax.shift_right_logical(iota((LANES, LANES), 0), 4)
        == lax.shift_right_logical(iota((LANES, LANES), 1), 4)
    ).astype(BF16)


def fetch_kernel(
    owners, part, packed, table_lanes, request_ref, asked_ref, table_ref, found_ref, turn_ref,
    left_ref, right_ref, sems
):
    lines, lanes = masks()
    chunks = packed // 16
    within = same_group()

    def turn_step(source, carry):
        at = (source * PARTS + part) * chunks
        numbers = lax.shift_right_logical(asked_ref[pl.ds(at, chunks), :], table_lanes)
        turn_ref[pl.ds(aligned(source * packed, 16), packed), :] = matmul(
            slot_lines(numbers.astype(F32)), within
        )
        return carry

    lax.fori_loop(0, owners, turn_step, 0)

    def process(source, words):
        for chunk in range(chunks):
            start = aligned(source * packed + chunk * 16, 16)
            turns = turn_ref[pl.ds(start, 16), :]
            halves = []
            for half in range(2):
                pieces = []
                for group in range(GROUPS):
                    base = chunk * LANES + group * 16 + half * 8
                    piece = table_ref[pl.ds(words[base], 8), :]
                    for k in range(1, 8):
                        piece = jnp.where(lines[k], table_ref[pl.ds(words[base + k], 8), :], piece)
                    pieces.append(piece)
                wanted = turns[half * 8 : (half + 1) * 8]
                block = jnp.zeros((8, LANES), F32)
                for turn in range(GROUPS):
                    mixed = pieces[turn]
                    for group in range(1, GROUPS):
                        mixed = jnp.where(lanes[group], pieces[(group + turn) % GROUPS], mixed)
                    if turn:
                        mixed = pltpu.roll(mixed, turn * EMB, 1)
                    block = jnp.where(wanted == float(turn), mixed, block)
                halves.append(block)
            found_ref[pl.ds(start, 16), :] = jnp.concatenate(halves, axis=0).astype(BF16)

    size = chunks * LANES
    word_stream(
        request_ref, (left_ref, right_ref), sems, part * size, PARTS * size, owners, process
    )


def unpermute(
    part, part_rows, back_ref, returned_ref, feature_ref, first_row, wide_ref, buffers, sems
):
    lines, lanes = masks()
    turn_copies(returned_ref, wide_ref)
    size = buffers[0].shape[0]
    chunk_rows = size // FIELDS

    def process(chunk, words):
        for block in range(chunk_rows // 16):
            start_row = aligned(first_row + chunk * chunk_rows + block * 16, 16)
            for lane_block in range(D_IN // LANES):
                fields = range(lane_block * GROUPS, min((lane_block + 1) * GROUPS, FIELDS))
                halves = [
                    assemble(
                        wide_ref,
                        lambda k, field, half=half: words[
                            (block * 16 + half * 8 + k) * FIELDS + field
                        ],
                        [(field, field % GROUPS) for field in fields],
                        lines,
                        lanes,
                    )
                    for half in range(2)
                ]
                feature_ref[
                    pl.ds(start_row, 16), lane_block * LANES : (lane_block + 1) * LANES
                ] = jnp.concatenate(halves, axis=0).astype(BF16)

    first = part * part_rows * FIELDS
    word_stream(back_ref, buffers, sems, first, size, part_rows // chunk_rows, process)


def unpermute_kernel(
    part, part_rows, back_ref, returned_ref, feature_ref, wide_ref, left_ref, right_ref, sems
):
    unpermute(
        part,
        part_rows,
        back_ref,
        returned_ref,
        feature_ref,
        0,
        wide_ref,
        (left_ref, right_ref),
        sems,
    )


def dense_kernel(
    part_rows,
    experts,
    scale,
    back_ref,
    out_ref,
    returned_ref,
    weight_ref,
    gate_ref,
    dense_ref,
    dense_w_ref,
    tower_ref,
    vector_ref,
    head_b_ref,
    label_ref,
    *refs,
):
    early = refs[: PARTS - 1]
    (
        sent_ref,
        grad_dense_ref,
        grad_weight_ref,
        grad_shared_ref,
        wide_ref,
        feature_ref,
        turned_ref,
        hidden_ref,
        hidden_slope_ref,
        output_ref,
        output_slope_ref,
        gates_ref,
        mixed_ref,
        mixed_grad_ref,
        dot_ref,
        logit_ref,
        input_ref,
        low_ref,
        tiled_ref,
        left_ref,
        right_ref,
        sems,
    ) = refs[PARTS - 1 :]
    buffers = (left_ref, right_ref)
    width = turned_ref.shape[1]
    blocks = width // LANES
    slot_blocks = sent_ref.shape[0] // 16
    eye = identity()
    lines, lanes = masks()

    def put_weight(expert, cut, value):
        grad_weight_ref[expert, cut, :] = value.astype(BF16)

    def put_shared(rows, cut, value):
        grad_shared_ref[rows, cut] = value

    whole = slice(None)
    for part in range(PARTS - 1):
        feature_ref[part * part_rows : (part + 1) * part_rows, :] = early[part][...]
    unpermute(
        PARTS - 1,
        part_rows,
        back_ref,
        returned_ref,
        feature_ref,
        (PARTS - 1) * part_rows,
        wide_ref,
        buffers,
        sems,
    )

    for lane_block in range(D_IN // LANES):
        for block in range(blocks):
            piece = feature_ref[
                block * LANES : (block + 1) * LANES, lane_block * LANES : (lane_block + 1) * LANES
            ]
            turned_ref[
                lane_block * LANES : (lane_block + 1) * LANES, block * LANES : (block + 1) * LANES
            ] = matmul_nt(eye, piece).astype(BF16)
    dense = dense_ref[...]
    dense_w = dense_w_ref[...]
    turned_ref[EMB_WIDTH:, :] = matmul_tn(dense_w, dense).astype(BF16)

    features = turned_ref[...]
    logits = matmul(gate_ref[...], features)
    for task in range(TASKS):
        part_logits = logits[task * experts : (task + 1) * experts]
        powers = jnp.exp(part_logits - jnp.max(part_logits, axis=0, keepdims=True))
        gates_ref[task * experts : (task + 1) * experts, :] = powers / jnp.sum(
            powers, axis=0, keepdims=True
        )

    mixed_ref[...] = jnp.zeros_like(mixed_ref)

    def column(line):
        tall = jnp.transpose(jnp.broadcast_to(line, (LANES, LANES)))
        return jnp.concatenate([tall] * blocks, axis=1)

    def bias_line(expert, rows):
        lines = [weight_ref[expert, 2 * D_IN + H1 :, :].astype(F32)[row : row + 1] for row in rows]
        return functools.reduce(jnp.add, lines)

    def forward(expert, carry):
        turned = turned_ref[...]
        for half in range(H1 // LANES):
            weights = weight_ref[expert, half * D_IN : (half + 1) * D_IN, :]
            bias = column(bias_line(expert, range(half * 3, half * 3 + 3)))
            value, slope = silu_parts(matmul_tn(weights, turned) + bias)
            hidden_ref[expert, half * LANES : (half + 1) * LANES, :] = value.astype(BF16)
            hidden_slope_ref[expert, half * LANES : (half + 1) * LANES, :] = slope
        weights = weight_ref[expert, 2 * D_IN : 2 * D_IN + H1, :]
        bias = column(bias_line(expert, (6, 7, 8)))
        value, slope = silu_parts(matmul_tn(weights, hidden_ref[expert]) + bias)
        output_ref[expert] = value
        output_slope_ref[expert] = slope
        for task in range(TASKS):
            mixed_ref[task * H2 : (task + 1) * H2, :] += (
                gates_ref[pl.ds(task * experts + expert, 1), :] * value
            )
        return carry

    lax.fori_loop(0, experts, forward, 0, unroll=2)

    tower_bias = column(vector_ref[0:1, :])
    head_w = column(vector_ref[1:2, :])
    tower = tower_ref[...]
    act_sums = []
    grad_sums = []
    head_sums = []
    for task in range(TASKS):
        units = slice(task * TOWER, (task + 1) * TOWER)
        outs = slice(task * H2, (task + 1) * H2)
        mixed = mixed_ref[outs, :]
        mixed_low = mixed.astype(BF16)
        tower_part = tower[:, units]
        act, slope = silu_parts(matmul_tn(tower_part, mixed_low) + tower_bias[units])
        score = jnp.sum(act * head_w[units], axis=0, keepdims=True) + head_b_ref[task]
        target = label_ref[task : task + 1, :].astype(F32)
        score_grad = (jax.nn.sigmoid(score) - target) * scale
        tower_grad = (score_grad * head_w[units] * slope).astype(BF16)
        act_sums.append(jnp.sum(score_grad * act, axis=1, keepdims=True))
        grad_sums.append(jnp.sum(tower_grad.astype(F32), axis=1, keepdims=True))
        head_sums.append(jnp.sum(score_grad, axis=1, keepdims=True))
        put_shared(slice(0, H2), units, matmul_nt(mixed_low, tower_grad))
        mixed_grad = matmul(tower_part, tower_grad).astype(BF16).astype(F32)
        mixed_grad_ref[outs, :] = mixed_grad
        dot_ref[task : task + 1, :] = jnp.sum(mixed_grad * mixed, axis=0, keepdims=True)
    column_sums = jnp.concatenate(
        [
            jnp.broadcast_to(jnp.concatenate(sums, axis=0), (LANES, LANES))
            for sums in (act_sums, grad_sums)
        ],
        axis=1,
    )
    put_shared(slice(H2, H2 + 8), whole, jnp.transpose(column_sums[:, :LANES])[0:8])
    put_shared(slice(H2 + 8, H2 + 16), whole, jnp.transpose(column_sums[:, LANES:])[0:8])
    head_line = jnp.zeros((8, LANES), F32)
    for task in range(TASKS):
        head_line = jnp.where(iota((8, LANES), 1) == task, head_sums[task], head_line)
    put_shared(slice(H2 + 16, H2 + 24), whole, head_line)

    input_ref[...] = jnp.zeros_like(input_ref)
    ones = jnp.ones((BIAS_ROWS, width), BF16)

    def backward(expert, carry):
        value = output_ref[expert]
        grad = jnp.zeros((H2, width), F32)
        for task in range(TASKS):
            mixed_grad = mixed_grad_ref[task * H2 : (task + 1) * H2, :]
            gate = gates_ref[pl.ds(task * experts + expert, 1), :]
            grad = grad + gate * mixed_grad
            along = jnp.sum(mixed_grad * value, axis=0, keepdims=True)
            logit_ref[pl.ds(task * experts + expert, 1), :] = gate * (
                along - dot_ref[task : task + 1, :]
            )
        output_grad = (grad * output_slope_ref[expert]).astype(BF16)
        hidden = hidden_ref[expert]
        put_weight(expert, slice(2 * D_IN, 2 * D_IN + H1), matmul_nt(hidden, output_grad))
        weights = weight_ref[expert, 2 * D_IN : 2 * D_IN + H1, :]
        hidden_grad = (matmul(weights, output_grad) * hidden_slope_ref[expert]).astype(BF16)
        turned = turned_ref[...]
        sums = []
        for half in range(H1 // LANES):
            half_grad = hidden_grad[half * LANES : (half + 1) * LANES]
            put_weight(
                expert, slice(half * D_IN, (half + 1) * D_IN), matmul_nt(turned, half_grad)
            )
            weights = weight_ref[expert, half * D_IN : (half + 1) * D_IN, :]
            input_ref[...] += matmul(weights, half_grad)
            sums.append(matmul_nt(ones, half_grad)[0:1])
        sums.append(matmul_nt(ones, output_grad)[0:1])
        sums.append(jnp.zeros((BIAS_ROWS - 3, LANES), F32))
        put_weight(expert, slice(2 * D_IN + H1, WEIGHT_ROWS), jnp.concatenate(sums, axis=0))
        return carry

    lax.fori_loop(0, experts, backward, 0, unroll=2)

    logit_grad = logit_ref[...].astype(BF16)
    gate_grad = matmul_nt(logit_grad, turned_ref[...])
    gate_base = H2 + 24
    pairs = TASKS * experts
    for lane_block in range(D_IN // LANES):
        put_shared(
            slice(gate_base + lane_block * pairs, gate_base + (lane_block + 1) * pairs),
            whole,
            gate_grad[:, lane_block * LANES : (lane_block + 1) * LANES],
        )
    low_ref[...] = (input_ref[...] + matmul_tn(gate_ref[...], logit_grad)).astype(BF16)
    bottom_grad = low_ref[EMB_WIDTH:, :]
    dense_base = gate_base + D_IN // LANES * pairs
    grad_dense_w = jnp.concatenate(
        [matmul_nt(dense, bottom_grad), jnp.zeros((DENSE, LANES - BOTTOM), F32)], axis=1
    )
    put_shared(
        slice(dense_base, dense_base + 16),
        whole,
        jnp.concatenate([grad_dense_w, jnp.zeros((16 - DENSE, LANES), F32)], axis=0),
    )
    grad_dense_ref[...] = matmul(dense_w, bottom_grad)

    def clear(step, carry):
        wide_ref[pl.ds(aligned(8 + step * LANES, 8), LANES), :] = jnp.zeros((LANES, LANES), F32)
        return carry

    lax.fori_loop(0, slot_blocks, clear, 0)
    chunk_rows = left_ref.shape[0] // FIELDS

    def permute(chunk, words):
        block = lax.div(chunk * chunk_rows, LANES)
        first = chunk * chunk_rows - block * LANES
        span = pl.ds(aligned(block * LANES, LANES), LANES)

        @pl.when(first == 0)
        def _():
            for field in range(FIELDS):
                piece = low_ref[field * EMB : (field + 1) * EMB, span]
                tiled_ref[field] = matmul_nt(eye, jnp.concatenate([piece] * GROUPS, axis=0))

        for step in range(chunk_rows // 8):
            start_row = aligned(first + step * 8, 8)
            for field in range(FIELDS):
                tile = tiled_ref[field, pl.ds(start_row, 8), :]
                for k in range(8):
                    start = words[(step * 8 + k) * FIELDS + field]
                    pltpu.store(wide_ref.at[pl.ds(start, 8), :], tile, mask=lines[k])

    word_stream(
        out_ref, buffers, sems, 0, chunk_rows * FIELDS, width // chunk_rows, permute
    )

    def merge(block, carry):
        halves = []
        for half in range(2):
            piece = jnp.zeros((8, LANES), F32)
            for group in range(GROUPS):
                start = aligned(block * LANES + group * 16 + (half + 1) * 8, 8)
                piece = jnp.where(lanes[group], wide_ref[pl.ds(start, 8), :], piece)
            halves.append(piece)
        start = aligned(block * 16, 16)
        sent_ref[pl.ds(start, 16), :] = jnp.concatenate(halves, axis=0).astype(BF16)
        return carry

    lax.fori_loop(0, slot_blocks, merge, 0, unroll=4 if slot_blocks % 4 == 0 else 1)


def add_kernel(
    packed,
    table_lanes,
    core_ref,
    request_ref,
    asked_ref,
    received_ref,
    total_ref,
    left_grad_ref,
    right_grad_ref,
    left_ref,
    right_ref,
    sems,
    *sums,
):
    rows = sums[0].shape[0] - 16
    core = core_ref[0]
    sources = received_ref.shape[0] // packed
    chunks = packed // 16
    lines, _ = masks()
    eye = identity()
    own_group = lax.shift_right_logical(iota((1, LANES), 1), 4)
    from_lane = iota((LANES, 2 * LANES), 0)
    to_lane = iota((LANES, 2 * LANES), 1)
    spread_names = []
    spread_grads = []
    for pair in range(GROUPS // 2):
        group = pair * 2 + lax.shift_right_logical(to_lane, 7)
        spread_names.append(
            jnp.where(lax.shift_right_logical(from_lane, 4) == group, 1.0, 0.0).astype(BF16)
        )
        wanted = group * EMB + (to_lane & (EMB - 1))
        spread_grads.append(jnp.where(from_lane == wanted, 1.0, 0.0).astype(BF16))

    def spread(source, grad_ref):
        asked = asked_ref[pl.ds(source * chunks, chunks), :]
        names = (own_group - lax.shift_right_logical(asked, table_lanes)) & (GROUPS - 1)
        names = names.astype(F32)
        for first in range(0, chunks, 8):
            count = min(8, chunks - first)
            held = slot_lines(names[first : first + count])
            start = aligned(source * packed + first * 16, 16)
            grads = received_ref[pl.ds(start, count * 16), :]
            lane_group = lax.shift_right_logical(iota((count * 16, LANES), 1), 4).astype(F32)
            for pair in range(GROUPS // 2):
                wide_names = matmul(held, spread_names[pair])
                wide_grads = matmul(grads, spread_grads[pair])
                for side in range(2):
                    half = slice(side * LANES, (side + 1) * LANES)
                    masked = jnp.where(wide_names[:, half] == lane_group, wide_grads[:, half], 0.0)
                    for chunk in range(count):
                        start = (first + chunk) * LANES + (pair * 2 + side) * 16
                        grad_ref[start : start + 16, :] = masked[chunk * 16 : (chunk + 1) * 16]

    def clear(step, carry):
        start = aligned(step * 16, 16)
        for total in sums:
            total[pl.ds(start, 16), :] = jnp.zeros((16, LANES), F32)
        return carry

    lax.fori_loop(0, (rows + 16) // 16, clear, 0)
    spread(0, left_grad_ref)

    def process(source, words):
        now, later = left_grad_ref, right_grad_ref
        if words is right_ref:
            now, later = later, now
        spread(jnp.minimum(source + 1, sources - 1), later)
        for row in range(GROUPS * packed // 8):
            grads = now[row * 8 : (row + 1) * 8, :]
            for k in range(8):
                place = pl.ds(words[row * 8 + k], 8)
                total = sums[k % STREAMS]
                pltpu.store(total.at[place, :], total[place, :] + grads, mask=lines[k])

    size = GROUPS * packed
    word_stream(request_ref, (left_ref, right_ref), sems, 0, size, sources, process)

    def finish(block, carry):
        start = aligned(8 + block * LANES, 8)
        total = functools.reduce(jnp.add, [one[pl.ds(start, LANES), :] for one in sums])
        turned = matmul_nt(eye, total.astype(BF16)).astype(BF16)
        for group in range(GROUPS):
            half, column = divmod(group, GROUPS // 2)
            column = aligned(column * rows + block * LANES, LANES)
            total_ref[half ^ core, :, pl.ds(column, LANES)] = turned[
                group * EMB : (group + 1) * EMB
            ]
        return carry

    lax.fori_loop(0, rows // LANES, finish, 0, unroll=8)


def unpack_kernel(weight_piece, shared_piece, pairs, piece_ref, *refs):
    (
        dense_w_ref,
        gate_ref,
        hidden_w_ref,
        hidden_b_ref,
        output_w_ref,
        output_b_ref,
        tower_w_ref,
        tower_b_ref,
        head_w_ref,
        head_b_ref,
        weight_ref,
        shared_ref,
    ) = refs
    for owner in range(piece_ref.shape[0]):
        weight_ref[owner * weight_piece : (owner + 1) * weight_piece, :] = piece_ref[
            owner, :weight_piece, :
        ].astype(F32)
        high = piece_ref[owner, weight_piece : weight_piece + shared_piece, :].astype(F32)
        low = piece_ref[owner, weight_piece + shared_piece :, :].astype(F32)
        shared_ref[owner * shared_piece : (owner + 1) * shared_piece, :] = high + low
    bias = 2 * D_IN + H1
    for half in range(H1 // LANES):
        span = slice(half * LANES, (half + 1) * LANES)
        hidden_w_ref[0, :, span] = weight_ref[half * D_IN : (half + 1) * D_IN, :]
        hidden_b_ref[:, span] = weight_ref[bias + half : bias + half + 1, :]
    output_w_ref[0] = weight_ref[2 * D_IN : bias, :]
    output_b_ref[...] = weight_ref[bias + 2 : bias + 3, :]
    tower_w_ref[...] = shared_ref[:H2, :]
    head_w_ref[...] = shared_ref[H2 : H2 + 1, :]
    tower_b_ref[...] = shared_ref[H2 + 8 : H2 + 9, :]
    head_b_ref[...] = shared_ref[H2 + 16 : H2 + 17, :TASKS]
    gate_base = H2 + 24
    for block in range(D_IN // LANES):
        gate_ref[:, block * LANES : (block + 1) * LANES] = shared_ref[
            gate_base + block * pairs : gate_base + (block + 1) * pairs, :
        ]
    dense_base = gate_base + D_IN // LANES * pairs
    dense_w_ref[...] = shared_ref[dense_base : dense_base + DENSE, :BOTTOM]


SMEM = pl.BlockSpec(memory_space=pltpu.SMEM)
VMEM = pl.BlockSpec(memory_space=pltpu.VMEM)
ANY = pl.BlockSpec(memory_space=pl.ANY)


def call(kernel, outs, ins, scratch, name, micros):
    return pl.pallas_call(
        kernel,
        out_shape=outs,
        in_specs=ins,
        out_specs=jax.tree.map(lambda _: VMEM, outs),
        scratch_shapes=scratch,
        name=name,
        cost_estimate=pl.CostEstimate(
            flops=int(micros * 1.15e9), bytes_accessed=int(micros * 3e6), transcendentals=0
        ),
        compiler_params=pltpu.CompilerParams(vmem_limit_bytes=VMEM_BYTES),
    )


def shards(
    emb_table,
    dense_feats,
    dense_w,
    gate_w,
    hidden_w,
    hidden_b,
    output_w,
    output_b,
    tower_w,
    tower_b,
    head_w,
    head_b,
    row_owner,
    local_row,
    labels,
):
    owners = lax.axis_size("batch")
    experts = lax.axis_size("expert")
    expert_index = lax.axis_index("expert")
    core = expert_index & 1
    row_total = dense_feats.shape[1]
    part_rows = row_total // PARTS
    lookups = row_total * FIELDS
    part_lookups = lookups // PARTS
    capacity = 2 * part_lookups // owners
    packed = -(-capacity // (GROUPS * 16)) * 16
    table_rows = emb_table.shape[0]
    table_packed = table_rows // GROUPS
    table_lanes = table_packed.bit_length() - 1
    scale = 1.0 / math.sqrt(row_total * owners * experts)
    slots = owners * PARTS * GROUPS * packed
    part_slots = owners * packed
    lookup_rows = lookups // LANES
    list_rows = -(-lookup_rows // 16) * 16

    def tie(*values):
        return lax.optimization_barrier(values)

    def exchange(values, axis):
        return lax.all_to_all(values, axis, split_axis=0, concat_axis=0, tiled=True)

    owner_list = row_owner.reshape(lookup_rows, LANES)
    local_list = local_row.reshape(lookup_rows, LANES)
    slot_rows = slots // LANES
    list_shape = jax.ShapeDtypeStruct((list_rows, LANES), I32)
    requests, back, out = call(
        functools.partial(route_kernel, owners, part_lookups, packed, table_lanes),
        (jax.ShapeDtypeStruct((slot_rows, LANES), I32), list_shape, list_shape),
        [VMEM, VMEM],
        [pltpu.VMEM((list_rows, LANES), I32)] * 3 + [pltpu.VMEM((slot_rows, 2 * LANES), F32)],
        "route",
        9,
    )(owner_list, local_list)
    asked = exchange(requests.reshape(owners, slots // owners), "batch")
    asked = asked.reshape(slot_rows, LANES)
    offset = 8 - (jnp.arange(LANES, dtype=I32) & 7)
    words = ((asked & (table_packed - 1)) + offset).reshape(-1)
    back = back.reshape(-1)
    out = out.reshape(-1)

    table, weights = call(
        pack_kernel,
        (
            jax.ShapeDtypeStruct((table_packed + 16, LANES), F32),
            jax.ShapeDtypeStruct((WEIGHT_ROWS, LANES), BF16),
        ),
        [VMEM] * 5,
        [],
        "pack",
        5,
    )(emb_table.T, hidden_w, output_w, hidden_b, output_b)
    weights = lax.all_gather(weights, "expert", axis=0, tiled=False)

    slot_words = [pltpu.SMEM((GROUPS * packed,), I32)] * 2 + [pltpu.SemaphoreType.DMA((2,))]
    row_words = [pltpu.SMEM((CHUNK_ROWS * FIELDS,), I32)] * 2 + [pltpu.SemaphoreType.DMA((2,))]
    returned = []
    for part in range(PARTS):
        found = call(
            functools.partial(fetch_kernel, owners, part, packed, table_lanes),
            jax.ShapeDtypeStruct((part_slots, LANES), BF16),
            [ANY, VMEM, VMEM],
            [pltpu.VMEM((part_slots, LANES), F32)] + slot_words,
            "fetch",
            24 // PARTS,
        )(words, asked, table)
        found = exchange(found.reshape(owners, packed, LANES), "batch")
        returned.append(found.reshape(part_slots, LANES))
    early = []
    for part in range(PARTS - 1):
        early.append(
            call(
                functools.partial(unpermute_kernel, part, part_rows),
                jax.ShapeDtypeStruct((part_rows, D_IN), BF16),
                [ANY, VMEM],
                [pltpu.VMEM((GROUPS * part_slots + 16, LANES), F32), *row_words],
                "unpermute",
                15,
            )(back, returned[part])
        )

    pairs = TASKS * experts
    shared_rows = H2 + 24 + D_IN // LANES * pairs + 16
    vectors = jnp.stack([tower_b, head_w])
    sent, grad_dense, grad_weight, grad_shared = call(
        functools.partial(dense_kernel, part_rows, experts, scale),
        (
            jax.ShapeDtypeStruct((PARTS * part_slots, LANES), BF16),
            jax.ShapeDtypeStruct((DENSE, row_total), F32),
            jax.ShapeDtypeStruct((experts, WEIGHT_ROWS, LANES), BF16),
            jax.ShapeDtypeStruct((shared_rows, LANES), F32),
        ),
        [ANY, ANY] + [VMEM] * 7 + [SMEM, VMEM] + [VMEM] * (PARTS - 1),
        [
            pltpu.VMEM((slots + 16, LANES), F32),
            pltpu.VMEM((row_total, D_IN), BF16),
            pltpu.VMEM((D_IN, row_total), BF16),
            pltpu.VMEM((experts, H1, row_total), BF16),
            pltpu.VMEM((experts, H1, row_total), F32),
            pltpu.VMEM((experts, H2, row_total), F32),
            pltpu.VMEM((experts, H2, row_total), F32),
            pltpu.VMEM((pairs, row_total), F32),
            pltpu.VMEM((TASKS * H2, row_total), F32),
            pltpu.VMEM((TASKS * H2, row_total), F32),
            pltpu.VMEM((8, row_total), F32),
            pltpu.VMEM((pairs, row_total), F32),
            pltpu.VMEM((D_IN, row_total), F32),
            pltpu.VMEM((D_IN, row_total), BF16),
            pltpu.VMEM((FIELDS, LANES, LANES), F32),
            *row_words,
        ],
        "dense",
        45,
    )(
        back,
        out,
        returned[-1],
        weights,
        gate_w.T,
        dense_feats,
        dense_w,
        tower_w,
        vectors,
        head_b,
        labels,
        *early,
    )
    received = exchange(sent.reshape(owners, PARTS * packed, LANES), "batch")
    received = received.reshape(PARTS * part_slots, LANES)

    def split(values):
        high = lax.reduce_precision(values, exponent_bits=8, mantissa_bits=7)
        return high.astype(BF16), (values - high).astype(BF16)

    weight_piece = -(-WEIGHT_ROWS // (16 * owners)) * 16
    shared_piece = -(-shared_rows // (16 * owners)) * 16
    piece_rows = weight_piece + 2 * shared_piece
    weight = jnp.pad(
        grad_weight, ((0, 0), (0, weight_piece * owners - WEIGHT_ROWS), (0, 0))
    ).reshape(experts, owners, weight_piece, LANES)
    shared = jnp.pad(grad_shared, ((0, shared_piece * owners - shared_rows), (0, 0)))
    pieces = jnp.concatenate(
        [weight.transpose(1, 0, 2, 3)]
        + [
            jnp.broadcast_to(
                one.reshape(owners, 1, shared_piece, LANES), (owners, experts, shared_piece, LANES)
            )
            for one in split(shared)
        ],
        axis=2,
    )
    received, pieces = tie(received, pieces)
    pieces = exchange(pieces.reshape(owners * experts, piece_rows, LANES), ("batch", "expert"))

    table_part = call(
        functools.partial(add_kernel, packed, table_lanes),
        jax.ShapeDtypeStruct((2, EMB, table_rows // 2), BF16),
        [SMEM, ANY, VMEM, VMEM],
        [pltpu.VMEM((GROUPS * packed, LANES), F32)] * 2
        + slot_words
        + [pltpu.VMEM((table_packed + 16, LANES), F32)] * STREAMS,
        "add",
        60,
    )(core.reshape(1), words, asked, received)

    table_part, pieces = tie(table_part, pieces)
    def swap(values, axis, bits):
        size = lax.axis_size(axis)
        return lax.ppermute(values, axis, [(one, one ^ bits) for one in range(size)])

    def add_low(left, right):
        return (left.astype(F32) + right.astype(F32)).astype(BF16)

    chunks = 2
    columns = table_rows // 2 // chunks
    kept = []
    for chunk in range(chunks):
        cut = slice(chunk * columns, (chunk + 1) * columns)
        kept.append(add_low(table_part[0, :, cut], swap(table_part[1, :, cut], "expert", 1)))
    sums = jnp.sum(pieces.astype(F32), axis=0)
    shared = sums[weight_piece : weight_piece + shared_piece] + sums[weight_piece + shared_piece :]
    piece = jnp.concatenate([sums[:weight_piece].astype(BF16), *split(shared)], axis=0)
    *kept, piece = tie(*kept, piece)
    pieces = exchange(jnp.broadcast_to(piece[None], (owners, piece_rows, LANES)), "batch")

    bit = 2
    while bit < experts:
        kept = [add_low(one, swap(one, "expert", bit)) for one in kept]
        bit *= 2
    small = call(
        functools.partial(unpack_kernel, weight_piece, shared_piece, pairs),
        tuple(
            jax.ShapeDtypeStruct(shape, F32)
            for shape in (
                (DENSE, BOTTOM),
                (pairs, D_IN),
                (1, D_IN, H1),
                (1, H1),
                (1, H1, H2),
                (1, H2),
                (H2, TASKS * TOWER),
                (1, TASKS * TOWER),
                (1, TASKS * TOWER),
                (1, TASKS),
            )
        ),
        [VMEM],
        [
            pltpu.VMEM((owners * weight_piece, LANES), F32),
            pltpu.VMEM((owners * shared_piece, LANES), F32),
        ],
        "unpack",
        3,
    )(pieces)
    *kept, small = tie(*kept, small)
    others = [swap(one, "expert", 1) for one in kept]
    lower = [jnp.where(core == 0, one, other) for one, other in zip(kept, others)]
    upper = [jnp.where(core == 0, other, one) for one, other in zip(kept, others)]
    table_total = jnp.concatenate(lower + upper, axis=1).astype(F32).T
    grad_dense_w, gate, hidden, hidden_bias, output, output_bias, tower, tower_bias, head, head_bias = (
        small
    )
    return (
        table_total,
        grad_dense,
        grad_dense_w,
        gate.T,
        hidden,
        hidden_bias,
        output,
        output_bias,
        tower,
        tower_bias.reshape(-1),
        head.reshape(-1),
        head_bias.reshape(-1),
    )


def solution(mesh):
    in_specs = (
        P("batch", None),
        P(None, ("batch", "expert")),
        P(),
        P(),
        P("expert", None, None),
        P("expert", None),
        P("expert", None, None),
        P("expert", None),
        P(),
        P(),
        P(),
        P(),
        P(("batch", "expert"), None),
        P(("batch", "expert")),
        P(None, ("batch", "expert")),
    )
    out_specs = (
        P("batch", None),
        P(None, ("batch", "expert")),
        P(),
        P(),
        P("expert", None, None),
        P("expert", None),
        P("expert", None, None),
        P("expert", None),
        P(),
        P(),
        P(),
        P(),
    )
    return jax.shard_map(shards, mesh=mesh, in_specs=in_specs, out_specs=out_specs, check_vma=False)
```

```python
import functools
import math

import jax
import jax.numpy as jnp
from jax import lax
from jax.experimental import pallas as pl
from jax.experimental.pallas import tpu as pltpu
from jax.sharding import PartitionSpec as P

FIELDS = 26
EMB = 16
DENSE = 13
BOTTOM = 96
D_IN = 512
H1 = 256
H2 = 128
TOWER = 64
TASKS = 2
LANES = 128
GROUPS = LANES // EMB
EMB_WIDTH = FIELDS * EMB
BIAS_ROWS = 16
GRAD_ROWS = 2 * D_IN + H1
WEIGHT_ROWS = GRAD_ROWS + BIAS_ROWS
STREAMS = 8
PARTS = 2
CHUNK_ROWS = 64
TABLE_CHUNKS = 2

F32 = jnp.float32
BF16 = jnp.bfloat16
I32 = jnp.int32


def iota(shape, axis):
    return lax.broadcasted_iota(I32, shape, axis)


def matmul(a, b):
    return lax.dot_general(a, b, (((1,), (0,)), ((), ())), preferred_element_type=F32)


def matmul_nt(a, b):
    return lax.dot_general(a, b, (((1,), (1,)), ((), ())), preferred_element_type=F32)


def matmul_tn(a, b):
    return lax.dot_general(a, b, (((0,), (0,)), ((), ())), preferred_element_type=F32)


def identity():
    return (iota((LANES, LANES), 0) == iota((LANES, LANES), 1)).astype(BF16)


def aligned(value, step):
    return pl.multiple_of(value, step)


def silu_parts(values):
    sig = jax.nn.sigmoid(values)
    return values * sig, sig * (1.0 + values * (1.0 - sig))


def route_kernel(
    owners, part_lookups, packed, table_lanes, batch_ref, owner_ref, local_ref, request_ref,
    back_ref, out_ref, high_ref, low_ref, value_ref, total_ref
):
    rows = high_ref.shape[0]
    part_rows = rows // PARTS
    filled = part_lookups // LANES
    slot_rows = request_ref.shape[0]
    shape = (rows, LANES)
    high_ref[...] = jnp.full(shape, -1, I32)
    low_ref[...] = jnp.zeros(shape, I32)
    for part in range(PARTS):
        lines = slice(part * part_rows, part * part_rows + filled)
        taken = slice(part * filled, (part + 1) * filled)
        high_ref[lines, :] = owner_ref[taken, :]
        low_ref[lines, :] = local_ref[taken, :]
    owner = high_ref[...]
    local = low_ref[...]
    row_id = iota(shape, 0)
    tri = (iota((LANES, LANES), 0) <= iota((LANES, LANES), 1)).astype(BF16)
    ones = jnp.ones((LANES, LANES), BF16)
    before = (iota((part_rows, part_rows), 1) < iota((part_rows, part_rows), 0)).astype(BF16)
    ranks = []
    for part in range(PARTS):
        own = owner[part * part_rows : (part + 1) * part_rows]
        rank = jnp.zeros((part_rows, LANES), F32)
        for one in range(owners):
            hit = own == one
            hits = jnp.where(hit, 1.0, 0.0).astype(BF16)
            upto = matmul(hits, tri)
            ahead = matmul(before, matmul(hits, ones).astype(BF16))
            rank = jnp.where(hit, upto + ahead - 1.0, rank)
        ranks.append(rank)
    rank = jnp.concatenate(ranks, axis=0)
    part_id = jnp.zeros(shape, I32)
    for part in range(1, PARTS):
        part_id = part_id + jnp.where(row_id >= part * part_rows, 1, 0)
    rank = rank.astype(I32)
    group = jnp.zeros(shape, I32)
    for step in range(1, GROUPS):
        group = group + jnp.where(rank >= step * packed, 1, 0)
    place = rank - group * packed
    held = jnp.maximum(owner, 0)
    chunks = packed // 16
    chunk = lax.shift_right_logical(place, 4)
    block = (held * PARTS + part_id) * chunks + chunk
    inside = group * 16 + (place & 15)
    table_group = lax.shift_right_logical(local, table_lanes)
    table_row = local & ((1 << table_lanes) - 1)
    high_ref[...] = jnp.where(owner < 0, -1, held * chunks + chunk)
    low_ref[...] = inside
    value_ref[...] = table_row + (((group - table_group) & (GROUPS - 1)) << table_lanes)
    lookup = (row_id - part_id * part_rows) * LANES + iota(shape, 1)
    quotient = jnp.floor((lookup.astype(F32) + 0.5) * (1.0 / FIELDS)).astype(I32)
    field_group = (lookup - quotient * FIELDS) & (GROUPS - 1)
    offset = 8 - (quotient & 7)
    turn = (field_group - group) & (GROUPS - 1)
    back_ref[...] = (turn * owners + held) * packed + place + offset
    away = ((held ^ batch_ref[0]) - held) * (PARTS * GROUPS * packed)
    out_ref[...] = block * LANES + inside + offset + away
    total_ref[...] = jnp.zeros_like(total_ref)
    own_rows = slot_rows // PARTS

    def gather_requests(part, step, carry):
        base = aligned(part * part_rows + step * 8, 8)
        high = high_ref[pl.ds(base, 8), :]
        low = low_ref[pl.ds(base, 8), :]
        values = value_ref[pl.ds(base, 8), :]
        upper = lax.shift_right_logical(values, 8).astype(F32)
        lower = (values & 255).astype(F32)
        at_high = []
        at_low = []
        for k in range(8):
            line = slice(k, k + 1)
            at_high.append(jnp.where(iota((own_rows, LANES), 0) == high[line], 1.0, 0.0).astype(BF16))
            same = iota((LANES, LANES), 0) == low[line]
            at_low.append(
                jnp.concatenate(
                    [jnp.where(same, upper[line], 0.0), jnp.where(same, lower[line], 0.0)], axis=0
                ).astype(BF16)
            )
        total_ref[part] += matmul_nt(
            jnp.concatenate(at_high, axis=1), jnp.concatenate(at_low, axis=1)
        )
        return carry

    for part in range(PARTS):
        lax.fori_loop(0, part_rows // 8, functools.partial(gather_requests, part), 0, unroll=3)
        total = (total_ref[part, :, :LANES] * 256.0 + total_ref[part, :, LANES:]).astype(I32)
        for one in range(owners):
            start = (one * PARTS + part) * chunks
            request_ref[start : start + chunks, :] = total[one * chunks : (one + 1) * chunks]


def pack_kernel(
    table_ref, hidden_w_ref, output_w_ref, hidden_b_ref, output_b_ref, packed_ref, weight_ref
):
    lines = []
    for values in (hidden_b_ref[:, :LANES], hidden_b_ref[:, LANES:], output_b_ref[...]):
        for _ in range(3):
            term = values.astype(BF16).astype(F32)
            lines.append(term)
            values = values - term
    lines.append(jnp.zeros((BIAS_ROWS - len(lines), LANES), F32))
    for half in range(H1 // LANES):
        weight_ref[half * D_IN : (half + 1) * D_IN, :] = hidden_w_ref[
            0, :, half * LANES : (half + 1) * LANES
        ]
    weight_ref[2 * D_IN : 2 * D_IN + H1, :] = output_w_ref[0]
    weight_ref[2 * D_IN + H1 :, :] = jnp.concatenate(lines, axis=0).astype(BF16)
    rows = table_ref.shape[1] // GROUPS
    eye = identity()

    def step(block, carry):
        pieces = []
        for group in range(GROUPS):
            start = aligned(group * rows + block * LANES, LANES)
            pieces.append(table_ref[:, pl.ds(start, LANES)])
        packed_ref[pl.ds(aligned(8 + block * LANES, 8), LANES), :] = matmul_nt(
            eye, jnp.concatenate(pieces, axis=0)
        )
        return carry

    packed_ref[0:8, :] = jnp.zeros((8, LANES), F32)
    packed_ref[8 + rows : 16 + rows, :] = jnp.zeros((8, LANES), F32)

    lax.fori_loop(0, rows // LANES, step, 0, unroll=8)


def masks():
    line = iota((8, LANES), 0)
    group = lax.shift_right_logical(iota((8, LANES), 1), 4)
    return [line == k for k in range(8)], [group == one for one in range(GROUPS)]


def turn_copies(rows_ref, wide_ref):
    rows = rows_ref.shape[0]
    half = GROUPS // 2
    from_lane = iota((LANES, half * LANES), 0)
    to_lane = iota((LANES, half * LANES), 1)
    turn = (lax.shift_right_logical(to_lane, 7) + half) * EMB
    turns = jnp.where(((from_lane + turn - to_lane) & (LANES - 1)) == 0, 1.0, 0.0).astype(BF16)

    def step(block, carry):
        start = aligned(block * LANES, LANES)
        piece = rows_ref[pl.ds(start, LANES), :]
        moved = matmul(piece, turns)
        piece = piece.astype(F32)
        for turn in range(GROUPS):
            if turn >= half:
                one = moved[:, (turn - half) * LANES : (turn - half + 1) * LANES]
            else:
                one = pltpu.roll(piece, turn * EMB, 1) if turn else piece
            wide_ref[pl.ds(aligned(8 + turn * rows + start, 8), LANES), :] = one
        return carry

    blocks = rows // LANES
    unroll = [count for count in (4, 3, 2, 1) if blocks % count == 0][0]
    lax.fori_loop(0, blocks, step, 0, unroll=unroll)


def assemble(wide_ref, word, groups, lines, lanes):
    block = jnp.zeros((8, LANES), F32)
    for place, group in groups:
        piece = wide_ref[pl.ds(word(0, place), 8), :]
        for k in range(1, 8):
            piece = jnp.where(lines[k], wide_ref[pl.ds(word(k, place), 8), :], piece)
        block = jnp.where(lanes[group], piece, block)
    return block


def word_stream(word_ref, buffers, sems, place, count, process, before=None):
    slots = len(buffers)
    size = buffers[0].shape[0]

    def copy(at, slot):
        start = aligned(place(at), LANES)
        return pltpu.make_async_copy(
            word_ref.at[pl.ds(start, size)], buffers[slot], sems.at[slot]
        )

    for slot in range(min(slots, count)):
        copy(slot, slot).start()
    if before is not None:
        before()

    def step(turn, carry):
        for slot in range(slots):
            at = turn * slots + slot
            copy(at, slot).wait()
            process(at, buffers[slot])

            @pl.when(at + slots < count)
            def _():
                copy(at + slots, slot).start()

        return carry

    lax.fori_loop(0, count // slots, step, 0)
    for slot in range(count % slots):
        at = count // slots * slots + slot
        copy(at, slot).wait()
        process(at, buffers[slot])


def slot_lines(numbers):
    own = (iota((16, LANES), 1) & 15) == iota((16, LANES), 0)
    return jnp.concatenate(
        [jnp.where(own, numbers[row : row + 1], 0.0) for row in range(numbers.shape[0])], axis=0
    ).astype(BF16)


def same_group():
    return (
        lax.shift_right_logical(iota((LANES, LANES), 0), 4)
        == lax.shift_right_logical(iota((LANES, LANES), 1), 4)
    ).astype(BF16)


def fetch_kernel(
    owners, part, packed, table_lanes, request_ref, asked_ref, table_ref, found_ref, turn_ref,
    piece_ref, left_ref, right_ref, sems
):
    lines, _ = masks()
    chunks = packed // 16
    within = same_group()
    group = lax.shift_right_logical(iota((8, LANES), 1), 4)
    bits = [(group & (1 << bit)) != 0 for bit in range(3)]

    def turn_step(source, carry):
        at = (source * PARTS + part) * chunks
        numbers = lax.shift_right_logical(asked_ref[pl.ds(at, chunks), :], table_lanes)
        turn_ref[pl.ds(aligned(source * packed, 16), packed), :] = matmul(
            slot_lines(numbers.astype(F32)), within
        )
        return carry

    def before():
        lax.fori_loop(0, owners, turn_step, 0, unroll=4)

    def process(source, words):
        for chunk in range(chunks):
            for line in range(LANES):
                base = chunk * LANES + line // 8 * 8
                pltpu.store(
                    piece_ref.at[base : base + 8, :],
                    table_ref[pl.ds(words[chunk * LANES + line], 8), :],
                    mask=lines[line % 8],
                )
            start = aligned(source * packed + chunk * 16, 16)
            turns = turn_ref[pl.ds(start, 16), :]
            halves = []
            for half in range(2):
                mixed = []
                for group in range(GROUPS):
                    base = chunk * LANES + group * 16 + half * 8
                    mixed.append(piece_ref[base : base + 8, :])
                for bit in range(3):
                    mixed = [
                        jnp.where(bits[bit], mixed[(turn + (1 << bit)) % GROUPS], mixed[turn])
                        for turn in range(GROUPS)
                    ]
                wanted = turns[half * 8 : (half + 1) * 8]
                block = mixed[0]
                for turn in range(1, GROUPS):
                    moved = pltpu.roll(mixed[turn], turn * EMB, 1)
                    block = jnp.where(wanted == float(turn), moved, block)
                halves.append(block)
            found_ref[pl.ds(start, 16), :] = jnp.concatenate(halves, axis=0).astype(BF16)

    size = chunks * LANES
    word_stream(
        request_ref,
        (left_ref, right_ref),
        sems,
        lambda at: (at * PARTS + part) * size,
        owners,
        process,
        before,
    )


def unpermute(
    part, part_rows, back_ref, returned_ref, feature_ref, first_row, wide_ref, buffers, sems
):
    lines, lanes = masks()
    size = buffers[0].shape[0]
    chunk_rows = size // FIELDS

    def process(chunk, words):
        for block in range(chunk_rows // 16):
            start_row = aligned(first_row + chunk * chunk_rows + block * 16, 16)
            for lane_block in range(D_IN // LANES):
                fields = range(lane_block * GROUPS, min((lane_block + 1) * GROUPS, FIELDS))
                halves = [
                    assemble(
                        wide_ref,
                        lambda k, field, half=half: words[
                            (block * 16 + half * 8 + k) * FIELDS + field
                        ],
                        [(field, field % GROUPS) for field in fields],
                        lines,
                        lanes,
                    )
                    for half in range(2)
                ]
                feature_ref[
                    pl.ds(start_row, 16), lane_block * LANES : (lane_block + 1) * LANES
                ] = jnp.concatenate(halves, axis=0).astype(BF16)

    first = part * back_ref.shape[0] // PARTS
    word_stream(
        back_ref,
        buffers,
        sems,
        lambda at: first + at * size,
        part_rows // chunk_rows,
        process,
        lambda: turn_copies(returned_ref, wide_ref),
    )


def gather_blocks(block_refs, whole_ref):
    rows = block_refs[0].shape[0]
    for one, block_ref in enumerate(block_refs):
        whole_ref[one * rows : (one + 1) * rows, :] = block_ref[...]


def unpermute_kernel(
    part, part_rows, back_ref, returned_ref, feature_ref, wide_ref, left_ref, right_ref, sems
):
    unpermute(
        part,
        part_rows,
        back_ref,
        returned_ref,
        feature_ref,
        0,
        wide_ref,
        (left_ref, right_ref),
        sems,
    )


def dense_kernel(
    owners,
    part_rows,
    experts,
    scale,
    back_ref,
    out_ref,
    returned_ref,
    weight_ref,
    gate_ref,
    dense_ref,
    dense_w_ref,
    tower_ref,
    vector_ref,
    head_b_ref,
    label_ref,
    *refs,
):
    early = refs[: PARTS - 1]
    refs = refs[PARTS - 1 :]
    sent_refs = refs[:owners]
    (
        grad_dense_ref,
        grad_weight_ref,
        grad_bias_ref,
        grad_shared_ref,
        wide_ref,
        feature_ref,
        turned_ref,
        hidden_ref,
        hidden_slope_ref,
        output_ref,
        output_slope_ref,
        gates_ref,
        mixed_ref,
        mixed_grad_ref,
        dot_ref,
        logit_ref,
        input_ref,
        low_ref,
        tiled_ref,
        left_ref,
        right_ref,
        sems,
        sent_ref,
    ) = refs[owners:]
    buffers = (left_ref, right_ref)
    width = turned_ref.shape[1]
    blocks = width // LANES
    slot_blocks = sent_ref.shape[0] // 16
    eye = identity()
    lines, lanes = masks()

    def put_weight(expert, cut, value):
        grad_weight_ref[expert, cut, :] = value.astype(BF16)

    def put_shared(rows, cut, value):
        grad_shared_ref[rows, cut] = value

    whole = slice(None)
    for part in range(PARTS - 1):
        feature_ref[part * part_rows : (part + 1) * part_rows, :] = early[part][...]
    unpermute(
        PARTS - 1,
        part_rows,
        back_ref,
        returned_ref,
        feature_ref,
        (PARTS - 1) * part_rows,
        wide_ref,
        buffers,
        sems,
    )

    for lane_block in range(D_IN // LANES):
        for block in range(blocks):
            piece = feature_ref[
                block * LANES : (block + 1) * LANES, lane_block * LANES : (lane_block + 1) * LANES
            ]
            turned_ref[
                lane_block * LANES : (lane_block + 1) * LANES, block * LANES : (block + 1) * LANES
            ] = matmul_nt(eye, piece).astype(BF16)
    dense = dense_ref[...]
    dense_w = dense_w_ref[...]
    turned_ref[EMB_WIDTH:, :] = matmul_tn(dense_w, dense).astype(BF16)

    features = turned_ref[...]
    logits = matmul(gate_ref[...], features)
    for task in range(TASKS):
        part_logits = logits[task * experts : (task + 1) * experts]
        powers = jnp.exp(part_logits - jnp.max(part_logits, axis=0, keepdims=True))
        gates_ref[task * experts : (task + 1) * experts, :] = powers / jnp.sum(
            powers, axis=0, keepdims=True
        )

    mixed_ref[...] = jnp.zeros_like(mixed_ref)

    def column(line):
        tall = jnp.transpose(jnp.broadcast_to(line, (LANES, LANES)))
        return jnp.concatenate([tall] * blocks, axis=1)

    def bias_line(expert, rows):
        lines = [weight_ref[expert, 2 * D_IN + H1 :, :].astype(F32)[row : row + 1] for row in rows]
        return functools.reduce(jnp.add, lines)

    def forward(expert, carry):
        turned = turned_ref[...]
        for half in range(H1 // LANES):
            weights = weight_ref[expert, half * D_IN : (half + 1) * D_IN, :]
            bias = column(bias_line(expert, range(half * 3, half * 3 + 3)))
            value, slope = silu_parts(matmul_tn(weights, turned) + bias)
            hidden_ref[expert, half * LANES : (half + 1) * LANES, :] = value.astype(BF16)
            hidden_slope_ref[expert, half * LANES : (half + 1) * LANES, :] = slope
        weights = weight_ref[expert, 2 * D_IN : 2 * D_IN + H1, :]
        bias = column(bias_line(expert, (6, 7, 8)))
        value, slope = silu_parts(matmul_tn(weights, hidden_ref[expert]) + bias)
        output_ref[expert] = value
        output_slope_ref[expert] = slope
        for task in range(TASKS):
            mixed_ref[task * H2 : (task + 1) * H2, :] += (
                gates_ref[pl.ds(task * experts + expert, 1), :] * value
            )
        return carry

    lax.fori_loop(0, experts, forward, 0, unroll=2)

    tower_bias = column(vector_ref[0:1, :])
    head_w = column(vector_ref[1:2, :])
    tower = tower_ref[...]
    act_sums = []
    grad_sums = []
    head_sums = []
    for task in range(TASKS):
        units = slice(task * TOWER, (task + 1) * TOWER)
        outs = slice(task * H2, (task + 1) * H2)
        mixed = mixed_ref[outs, :]
        mixed_low = mixed.astype(BF16)
        tower_part = tower[:, units]
        act, slope = silu_parts(matmul_tn(tower_part, mixed_low) + tower_bias[units])
        score = jnp.sum(act * head_w[units], axis=0, keepdims=True) + head_b_ref[task]
        target = label_ref[task : task + 1, :].astype(F32)
        score_grad = (jax.nn.sigmoid(score) - target) * scale
        tower_grad = (score_grad * head_w[units] * slope).astype(BF16)
        act_sums.append(jnp.sum(score_grad * act, axis=1, keepdims=True))
        grad_sums.append(jnp.sum(tower_grad.astype(F32), axis=1, keepdims=True))
        head_sums.append(jnp.sum(score_grad, axis=1, keepdims=True))
        put_shared(slice(0, H2), units, matmul_nt(mixed_low, tower_grad))
        mixed_grad = matmul(tower_part, tower_grad).astype(BF16).astype(F32)
        mixed_grad_ref[outs, :] = mixed_grad
        dot_ref[task : task + 1, :] = jnp.sum(mixed_grad * mixed, axis=0, keepdims=True)
    column_sums = jnp.concatenate(
        [
            jnp.broadcast_to(jnp.concatenate(sums, axis=0), (LANES, LANES))
            for sums in (act_sums, grad_sums)
        ],
        axis=1,
    )
    put_shared(slice(H2, H2 + 8), whole, jnp.transpose(column_sums[:, :LANES])[0:8])
    put_shared(slice(H2 + 8, H2 + 16), whole, jnp.transpose(column_sums[:, LANES:])[0:8])
    head_line = jnp.zeros((8, LANES), F32)
    for task in range(TASKS):
        head_line = jnp.where(iota((8, LANES), 1) == task, head_sums[task], head_line)
    put_shared(slice(H2 + 16, H2 + 24), whole, head_line)

    input_ref[...] = jnp.zeros_like(input_ref)
    ones = jnp.ones((BIAS_ROWS, width), BF16)

    def backward(expert, carry):
        value = output_ref[expert]
        grad = jnp.zeros((H2, width), F32)
        for task in range(TASKS):
            mixed_grad = mixed_grad_ref[task * H2 : (task + 1) * H2, :]
            gate = gates_ref[pl.ds(task * experts + expert, 1), :]
            grad = grad + gate * mixed_grad
            along = jnp.sum(mixed_grad * value, axis=0, keepdims=True)
            logit_ref[pl.ds(task * experts + expert, 1), :] = gate * (
                along - dot_ref[task : task + 1, :]
            )
        output_grad = (grad * output_slope_ref[expert]).astype(BF16)
        hidden = hidden_ref[expert]
        put_weight(expert, slice(2 * D_IN, 2 * D_IN + H1), matmul_nt(hidden, output_grad))
        weights = weight_ref[expert, 2 * D_IN : 2 * D_IN + H1, :]
        hidden_grad = (matmul(weights, output_grad) * hidden_slope_ref[expert]).astype(BF16)
        turned = turned_ref[...]
        sums = []
        for half in range(H1 // LANES):
            half_grad = hidden_grad[half * LANES : (half + 1) * LANES]
            put_weight(
                expert, slice(half * D_IN, (half + 1) * D_IN), matmul_nt(turned, half_grad)
            )
            weights = weight_ref[expert, half * D_IN : (half + 1) * D_IN, :]
            input_ref[...] += matmul(weights, half_grad)
            sums.append(matmul_nt(ones, half_grad)[0:1])
        sums.append(matmul_nt(ones, output_grad)[0:1])
        sums.append(jnp.zeros((8 - 3, LANES), F32))
        grad_bias_ref[expert] = jnp.concatenate(sums, axis=0)
        return carry

    lax.fori_loop(0, experts, backward, 0, unroll=2)

    logit_grad = logit_ref[...].astype(BF16)
    gate_grad = matmul_nt(logit_grad, turned_ref[...])
    gate_base = H2 + 24
    pairs = TASKS * experts
    for lane_block in range(D_IN // LANES):
        put_shared(
            slice(gate_base + lane_block * pairs, gate_base + (lane_block + 1) * pairs),
            whole,
            gate_grad[:, lane_block * LANES : (lane_block + 1) * LANES],
        )
    low_ref[...] = (input_ref[...] + matmul_tn(gate_ref[...], logit_grad)).astype(BF16)
    bottom_grad = low_ref[EMB_WIDTH:, :]
    dense_base = gate_base + D_IN // LANES * pairs
    grad_dense_w = jnp.concatenate(
        [matmul_nt(dense, bottom_grad), jnp.zeros((DENSE, LANES - BOTTOM), F32)], axis=1
    )
    put_shared(
        slice(dense_base, dense_base + 16),
        whole,
        jnp.concatenate([grad_dense_w, jnp.zeros((16 - DENSE, LANES), F32)], axis=0),
    )
    grad_dense_ref[...] = matmul(dense_w, bottom_grad)

    def clear(step, carry):
        wide_ref[pl.ds(aligned(8 + step * LANES, 8), LANES), :] = jnp.zeros((LANES, LANES), F32)
        return carry

    chunk_rows = left_ref.shape[0] // FIELDS

    def permute(chunk, words):
        block = lax.div(chunk * chunk_rows, LANES)
        first = chunk * chunk_rows - block * LANES
        span = pl.ds(aligned(block * LANES, LANES), LANES)

        @pl.when(first == 0)
        def _():
            for field in range(FIELDS):
                piece = low_ref[field * EMB : (field + 1) * EMB, span]
                tiled_ref[field] = matmul_nt(eye, jnp.concatenate([piece] * GROUPS, axis=0))

        for step in range(chunk_rows // 8):
            start_row = aligned(first + step * 8, 8)
            for field in range(FIELDS):
                tile = tiled_ref[field, pl.ds(start_row, 8), :]
                for k in range(8):
                    start = words[(step * 8 + k) * FIELDS + field]
                    pltpu.store(wide_ref.at[pl.ds(start, 8), :], tile, mask=lines[k])

    def permute_place(at):
        each = part_rows // chunk_rows
        part = lax.div(at, each)
        return part * (out_ref.shape[0] // PARTS) + (at - part * each) * (chunk_rows * FIELDS)

    word_stream(
        out_ref,
        buffers,
        sems,
        permute_place,
        width // chunk_rows,
        permute,
        lambda: lax.fori_loop(0, slot_blocks, clear, 0, unroll=2),
    )

    def merge(block, carry):
        halves = []
        for half in range(2):
            piece = jnp.zeros((8, LANES), F32)
            for group in range(GROUPS):
                start = aligned(block * LANES + group * 16 + (half + 1) * 8, 8)
                piece = jnp.where(lanes[group], wide_ref[pl.ds(start, 8), :], piece)
            halves.append(piece)
        start = aligned(block * 16, 16)
        sent_ref[pl.ds(start, 16), :] = jnp.concatenate(halves, axis=0).astype(BF16)
        return carry

    lax.fori_loop(0, slot_blocks, merge, 0, unroll=4 if slot_blocks % 4 == 0 else 1)
    each = sent_ref.shape[0] // owners
    for one in range(owners):
        sent_refs[one][...] = sent_ref[one * each : (one + 1) * each, :]


def add_kernel(owners, packed, table_lanes, index_ref, request_ref, asked_ref, *refs):
    received_refs = refs[:owners]
    table_refs = refs[owners : owners + 2 * TABLE_CHUNKS]
    (
        received_ref,
        left_grad_ref,
        right_grad_ref,
        left_ref,
        right_ref,
        sems,
        *sums,
    ) = refs[owners + 2 * TABLE_CHUNKS :]
    rows = sums[0].shape[0] - 16
    core, batch = index_ref[0], index_ref[1]
    sources = received_ref.shape[0] // packed
    chunks = packed // 16
    lines, _ = masks()
    eye = identity()
    own_group = lax.shift_right_logical(iota((1, LANES), 1), 4)
    from_lane = iota((LANES, 2 * LANES), 0)
    to_lane = iota((LANES, 2 * LANES), 1)
    spread_names = []
    spread_grads = []
    for pair in range(GROUPS // 2):
        group = pair * 2 + lax.shift_right_logical(to_lane, 7)
        spread_names.append(
            jnp.where(lax.shift_right_logical(from_lane, 4) == group, 1.0, 0.0).astype(BF16)
        )
        wanted = group * EMB + (to_lane & (EMB - 1))
        spread_grads.append(jnp.where(from_lane == wanted, 1.0, 0.0).astype(BF16))

    def place(source):
        distance = lax.div(source, PARTS)
        return (distance ^ batch) * PARTS + source - distance * PARTS

    def spread(source, grad_ref):
        def step(first, count, pair):
            asked = asked_ref[pl.ds(place(source) * chunks + first, count), :]
            names = (own_group - lax.shift_right_logical(asked, table_lanes)) & (GROUPS - 1)
            start = aligned(source * packed + first * 16, 16)
            grads = received_ref[pl.ds(start, count * 16), :]
            lane_group = lax.shift_right_logical(iota((count * 16, LANES), 1), 4).astype(F32)
            wide_names = matmul(slot_lines(names.astype(F32)), spread_names[pair])
            wide_grads = matmul(grads, spread_grads[pair])
            for side in range(2):
                half = slice(side * LANES, (side + 1) * LANES)
                masked = jnp.where(wide_names[:, half] == lane_group, wide_grads[:, half], 0.0)
                for chunk in range(count):
                    start = (first + chunk) * LANES + (pair * 2 + side) * 16
                    grad_ref[start : start + 16, :] = masked[chunk * 16 : (chunk + 1) * 16]

        return [
            functools.partial(step, first, min(4, chunks - first), pair)
            for first in range(0, chunks, 4)
            for pair in range(GROUPS // 2)
        ]

    def clear(step, carry):
        for total in sums:
            total[pl.ds(aligned(8 + step * LANES, 8), LANES), :] = jnp.zeros((LANES, LANES), F32)
        return carry

    def before():
        for total in sums:
            total[0:8, :] = jnp.zeros((8, LANES), F32)
            total[8 + rows : 16 + rows, :] = jnp.zeros((8, LANES), F32)
        lax.fori_loop(0, rows // LANES, clear, 0)
        gather_blocks(received_refs, received_ref)
        for one in spread(0, left_grad_ref):
            one()

    def process(source, words):
        now, later = left_grad_ref, right_grad_ref
        if words is right_ref:
            now, later = later, now
        steps = spread(jnp.minimum(source + 1, sources - 1), later)
        rows = GROUPS * packed // 8
        for row in range(rows):
            if row * len(steps) // rows != (row - 1) * len(steps) // rows:
                steps[row * len(steps) // rows]()
            grads = now[row * 8 : (row + 1) * 8, :]
            for k in range(8):
                place = pl.ds(words[row * 8 + k], 8)
                total = sums[k % STREAMS]
                pltpu.store(total.at[place, :], total[place, :] + grads, mask=lines[k])

    size = GROUPS * packed
    word_stream(
        request_ref,
        (left_ref, right_ref),
        sems,
        lambda at: place(at) * size,
        sources,
        process,
        before,
    )

    def finish(kept, block, carry):
        start = aligned(8 + block * LANES, 8)
        total = functools.reduce(jnp.add, [one[pl.ds(start, LANES), :] for one in sums])
        turned = matmul_nt(eye, total.astype(BF16)).astype(BF16)
        each = GROUPS // (2 * TABLE_CHUNKS)
        for group in range(GROUPS):
            half, column = divmod(group, GROUPS // 2)
            chunk, column = divmod(column, each)
            table_ref = table_refs[chunk + (0 if half == kept else TABLE_CHUNKS)]
            column = aligned(column * rows + block * LANES, LANES)
            table_ref[:, pl.ds(column, LANES)] = turned[group * EMB : (group + 1) * EMB]
        return carry

    for kept in range(2):

        @pl.when(core == kept)
        def _():
            lax.fori_loop(0, rows // LANES, functools.partial(finish, kept), 0, unroll=8)


def unpack_kernel(weight_piece, extra_piece, pairs, piece_ref, *refs):
    (
        dense_w_ref,
        gate_ref,
        hidden_w_ref,
        hidden_b_ref,
        output_w_ref,
        output_b_ref,
        tower_w_ref,
        tower_b_ref,
        head_w_ref,
        head_b_ref,
        weight_ref,
        extra_ref,
    ) = refs
    for owner in range(piece_ref.shape[0]):
        weight_ref[owner * weight_piece : (owner + 1) * weight_piece, :] = piece_ref[
            owner, :weight_piece, :
        ].astype(F32)
        high = piece_ref[owner, weight_piece : weight_piece + extra_piece, :].astype(F32)
        low = piece_ref[owner, weight_piece + extra_piece :, :].astype(F32)
        extra_ref[owner * extra_piece : (owner + 1) * extra_piece, :] = high + low
    gate_rows = D_IN // LANES * pairs
    small = H2 + gate_rows + 16

    def small_line(row):
        return extra_ref[small + row : small + row + 1, :] + extra_ref[small + 6 + row : small + 7 + row, :]

    for half in range(H1 // LANES):
        span = slice(half * LANES, (half + 1) * LANES)
        hidden_w_ref[0, :, span] = weight_ref[half * D_IN : (half + 1) * D_IN, :]
        hidden_b_ref[:, span] = small_line(3 + half)
    output_w_ref[0] = weight_ref[2 * D_IN : GRAD_ROWS, :]
    output_b_ref[...] = small_line(5)
    tower_w_ref[...] = extra_ref[:H2, :]
    head_w_ref[...] = small_line(0)
    tower_b_ref[...] = small_line(1)
    head_b_ref[...] = small_line(2)[:, :TASKS]
    for block in range(D_IN // LANES):
        gate_ref[:, block * LANES : (block + 1) * LANES] = extra_ref[
            H2 + block * pairs : H2 + (block + 1) * pairs, :
        ]
    dense_w_ref[...] = extra_ref[H2 + gate_rows : H2 + gate_rows + DENSE, :BOTTOM]


SMEM = pl.BlockSpec(memory_space=pltpu.SMEM)
VMEM = pl.BlockSpec(memory_space=pltpu.VMEM)
ANY = pl.BlockSpec(memory_space=pl.ANY)


def call(kernel, outs, ins, scratch, name, micros, vmem=16):
    return pl.pallas_call(
        kernel,
        out_shape=outs,
        in_specs=ins,
        out_specs=jax.tree.map(lambda _: VMEM, outs),
        scratch_shapes=scratch,
        name=name,
        cost_estimate=pl.CostEstimate(
            flops=int(micros * 1.15e9), bytes_accessed=int(micros * 3e6), transcendentals=0
        ),
        compiler_params=pltpu.CompilerParams(vmem_limit_bytes=vmem << 20),
    )


def shards(
    emb_table,
    dense_feats,
    dense_w,
    gate_w,
    hidden_w,
    hidden_b,
    output_w,
    output_b,
    tower_w,
    tower_b,
    head_w,
    head_b,
    row_owner,
    local_row,
    labels,
):
    owners = lax.axis_size("batch")
    experts = lax.axis_size("expert")
    expert_index = lax.axis_index("expert")
    core = expert_index & 1
    row_total = dense_feats.shape[1]
    part_rows = row_total // PARTS
    lookups = row_total * FIELDS
    part_lookups = lookups // PARTS
    capacity = 2 * part_lookups // owners
    packed = -(-capacity // (GROUPS * 16)) * 16
    table_rows = emb_table.shape[0]
    table_packed = table_rows // GROUPS
    table_lanes = table_packed.bit_length() - 1
    scale = 1.0 / math.sqrt(row_total * owners * experts)
    slots = owners * PARTS * GROUPS * packed
    part_slots = owners * packed
    lookup_rows = lookups // LANES
    list_part = -(-lookup_rows // (PARTS * 24)) * 24
    list_rows = list_part * PARTS

    def tie(*values):
        return lax.optimization_barrier(values)

    def exchange(values, axis):
        return lax.all_to_all(values, axis, split_axis=0, concat_axis=0, tiled=True)

    def swap(values, axis, bits):
        size = lax.axis_size(axis)
        return lax.ppermute(values, axis, [(one, one ^ bits) for one in range(size)])

    def swap_all(blocks):
        order = sorted(range(1, owners), key=lambda bits: (-bits.bit_length(), bits))
        moved = {bits: swap(blocks[bits], "batch", bits) for bits in order}
        return [blocks[0]] + [moved[bits] for bits in range(1, owners)]

    owner_list = row_owner.reshape(lookup_rows, LANES)
    local_list = local_row.reshape(lookup_rows, LANES)
    slot_rows = slots // LANES
    list_shape = jax.ShapeDtypeStruct((list_rows, LANES), I32)
    batch_index = lax.axis_index("batch").reshape(1)
    requests, back, out = call(
        functools.partial(route_kernel, owners, part_lookups, packed, table_lanes),
        (jax.ShapeDtypeStruct((slot_rows, LANES), I32), list_shape, list_shape),
        [SMEM, VMEM, VMEM],
        [pltpu.VMEM((list_rows, LANES), I32)] * 3 + [pltpu.VMEM((PARTS, slot_rows // PARTS, 2 * LANES), F32)],
        "route",
        9,
    )(batch_index, owner_list, local_list)
    asked = exchange(requests.reshape(owners, slots // owners), "batch")
    asked = asked.reshape(slot_rows, LANES)
    offset = 8 - (jnp.arange(LANES, dtype=I32) & 7)
    words = ((asked & (table_packed - 1)) + offset).reshape(-1)
    back = back.reshape(-1)
    out = out.reshape(-1)

    hidden_b, out = tie(hidden_b, out)
    table, weights = call(
        pack_kernel,
        (
            pltpu.VMEM((table_packed + 16, LANES), F32),
            jax.ShapeDtypeStruct((WEIGHT_ROWS, LANES), BF16),
        ),
        [VMEM] * 5,
        [],
        "pack",
        5,
    )(emb_table.T, hidden_w, output_w, hidden_b, output_b)
    table = pltpu.with_memory_space_constraint(table, pltpu.VMEM)
    weights = lax.all_gather(weights, "expert", axis=0, tiled=False)

    slot_words = [pltpu.SMEM((GROUPS * packed,), I32)] * 2 + [pltpu.SemaphoreType.DMA((2,))]
    row_words = [pltpu.SMEM((CHUNK_ROWS * FIELDS,), I32)] * 2 + [pltpu.SemaphoreType.DMA((2,))]
    returned = []
    for part in range(PARTS):
        found = call(
            functools.partial(fetch_kernel, owners, part, packed, table_lanes),
            jax.ShapeDtypeStruct((part_slots, LANES), BF16),
            [ANY, VMEM, VMEM],
            [
                pltpu.VMEM((part_slots, LANES), F32),
                pltpu.VMEM((GROUPS * packed, LANES), F32),
            ]
            + slot_words,
            "fetch",
            24 // PARTS,
        )(words, asked, table)
        found = exchange(found.reshape(owners, packed, LANES), "batch")
        returned.append(found.reshape(part_slots, LANES))
    early = []
    for part in range(PARTS - 1):
        early.append(
            call(
                functools.partial(unpermute_kernel, part, part_rows),
                jax.ShapeDtypeStruct((part_rows, D_IN), BF16),
                [ANY, VMEM],
                [pltpu.VMEM((GROUPS * part_slots + 16, LANES), F32), *row_words],
                "unpermute",
                15,
            )(back, returned[part])
        )

    pairs = TASKS * experts
    shared_rows = H2 + 24 + D_IN // LANES * pairs + 16
    vectors = jnp.stack([tower_b, head_w])
    *sent, grad_dense, grad_weight, grad_bias, grad_shared = call(
        functools.partial(dense_kernel, owners, part_rows, experts, scale),
        (
            *[jax.ShapeDtypeStruct((PARTS * packed, LANES), BF16)] * owners,
            jax.ShapeDtypeStruct((DENSE, row_total), F32),
            jax.ShapeDtypeStruct((experts, GRAD_ROWS, LANES), BF16),
            jax.ShapeDtypeStruct((experts, 8, LANES), F32),
            jax.ShapeDtypeStruct((shared_rows, LANES), F32),
        ),
        [ANY, ANY] + [VMEM] * 7 + [SMEM] + [VMEM] * PARTS,
        [
            pltpu.VMEM((slots + 16, LANES), F32),
            pltpu.VMEM((row_total, D_IN), BF16),
            pltpu.VMEM((D_IN, row_total), BF16),
            pltpu.VMEM((experts, H1, row_total), BF16),
            pltpu.VMEM((experts, H1, row_total), F32),
            pltpu.VMEM((experts, H2, row_total), F32),
            pltpu.VMEM((experts, H2, row_total), F32),
            pltpu.VMEM((pairs, row_total), F32),
            pltpu.VMEM((TASKS * H2, row_total), F32),
            pltpu.VMEM((TASKS * H2, row_total), F32),
            pltpu.VMEM((8, row_total), F32),
            pltpu.VMEM((pairs, row_total), F32),
            pltpu.VMEM((D_IN, row_total), F32),
            pltpu.VMEM((D_IN, row_total), BF16),
            pltpu.VMEM((FIELDS, LANES, LANES), F32),
            *row_words,
            pltpu.VMEM((PARTS * part_slots, LANES), BF16),
        ],
        "dense",
        45,
        56,
    )(
        back,
        out,
        returned[-1],
        weights,
        gate_w.T,
        dense_feats,
        dense_w,
        tower_w,
        vectors,
        head_b,
        labels,
        *early,
    )
    received = swap_all(sent)

    def split(values):
        high = lax.reduce_precision(values, exponent_bits=8, mantissa_bits=7)
        return high.astype(BF16), (values - high).astype(BF16)

    received[1], grad_weight, grad_bias, grad_shared = tie(
        received[1], grad_weight, grad_bias, grad_shared
    )

    def spread_rows(values, piece):
        rows = values.shape[1]
        values = jnp.pad(values, ((0, 0), (0, piece * owners - rows), (0, 0)))
        return values.reshape(experts, owners, piece, LANES).transpose(1, 0, 2, 3)

    large = jnp.concatenate([grad_shared[:H2], grad_shared[H2 + 24 :]], axis=0).astype(BF16)
    small = jnp.concatenate([grad_shared[H2 + 8 * row : H2 + 8 * row + 1] for row in range(3)])
    small = jnp.concatenate(
        [jnp.broadcast_to(small[None], (experts, 3, LANES)), grad_bias[:, :3]], axis=1
    )
    extra = jnp.concatenate(
        [jnp.broadcast_to(large[None], (experts, *large.shape)), *split(small)], axis=1
    )
    weight_piece = -(-GRAD_ROWS // (16 * owners)) * 16
    extra_piece = -(-extra.shape[1] // (16 * owners)) * 16
    piece_rows = weight_piece + extra_piece
    pieces = jnp.concatenate(
        [spread_rows(grad_weight, weight_piece), spread_rows(extra, extra_piece)], axis=2
    )
    late = owners - 2
    *received[:late], pieces = tie(*received[:late], pieces)
    pieces = exchange(pieces.reshape(owners * experts, piece_rows, LANES), ("batch", "expert"))

    columns = table_rows // 2 // TABLE_CHUNKS
    table_part = call(
        functools.partial(add_kernel, owners, packed, table_lanes),
        (jax.ShapeDtypeStruct((EMB, columns), BF16),) * (2 * TABLE_CHUNKS),
        [SMEM, ANY, VMEM] + [VMEM] * owners,
        [pltpu.VMEM((PARTS * part_slots, LANES), BF16)]
        + [pltpu.VMEM((GROUPS * packed, LANES), F32)] * 2
        + slot_words
        + [pltpu.VMEM((table_packed + 16, LANES), F32)] * STREAMS,
        "add",
        60,
        48,
    )(jnp.concatenate([core.reshape(1), batch_index]), words, asked, *received)

    def add_low(left, right):
        return (left.astype(F32) + right.astype(F32)).astype(BF16)

    *table_part, pieces = tie(*table_part, pieces)
    kept = [
        add_low(one, swap(other, "expert", 1))
        for one, other in zip(table_part[:TABLE_CHUNKS], table_part[TABLE_CHUNKS:])
    ]
    sums = jnp.sum(pieces.astype(F32), axis=0)
    piece = jnp.concatenate([sums[:weight_piece].astype(BF16), *split(sums[weight_piece:])], axis=0)
    *kept, piece = tie(*kept, piece)
    pieces = exchange(jnp.broadcast_to(piece[None], (owners, *piece.shape)), "batch")

    bit = 2
    while bit < experts:
        kept = [add_low(one, swap(one, "expert", bit)) for one in kept]
        bit *= 2
    small = call(
        functools.partial(unpack_kernel, weight_piece, extra_piece, pairs),
        tuple(
            jax.ShapeDtypeStruct(shape, F32)
            for shape in (
                (DENSE, BOTTOM),
                (pairs, D_IN),
                (1, D_IN, H1),
                (1, H1),
                (1, H1, H2),
                (1, H2),
                (H2, TASKS * TOWER),
                (1, TASKS * TOWER),
                (1, TASKS * TOWER),
                (1, TASKS),
            )
        ),
        [VMEM],
        [
            pltpu.VMEM((owners * weight_piece, LANES), F32),
            pltpu.VMEM((owners * extra_piece, LANES), F32),
        ],
        "unpack",
        3,
    )(pieces)
    others = [swap(one, "expert", 1) for one in kept]
    *others, small = tie(*others, small)
    lower = [jnp.where(core == 0, one, other) for one, other in zip(kept, others)]
    upper = [jnp.where(core == 0, other, one) for one, other in zip(kept, others)]
    table_total = jnp.concatenate(lower + upper, axis=1).astype(F32).T
    grad_dense_w, gate, hidden, hidden_bias, output, output_bias, tower, tower_bias, head, head_bias = (
        small
    )
    return (
        table_total,
        grad_dense,
        grad_dense_w,
        gate.T,
        hidden,
        hidden_bias,
        output,
        output_bias,
        tower,
        tower_bias.reshape(-1),
        head.reshape(-1),
        head_bias.reshape(-1),
    )


def solution(mesh):
    in_specs = (
        P("batch", None),
        P(None, ("batch", "expert")),
        P(),
        P(),
        P("expert", None, None),
        P("expert", None),
        P("expert", None, None),
        P("expert", None),
        P(),
        P(),
        P(),
        P(),
        P(("batch", "expert"), None),
        P(("batch", "expert")),
        P(None, ("batch", "expert")),
    )
    out_specs = (
        P("batch", None),
        P(None, ("batch", "expert")),
        P(),
        P(),
        P("expert", None, None),
        P("expert", None),
        P("expert", None, None),
        P("expert", None),
        P(),
        P(),
        P(),
        P(),
    )
    return jax.shard_map(shards, mesh=mesh, in_specs=in_specs, out_specs=out_specs, check_vma=False)
```

```python
import functools
import math

import jax
import jax.numpy as jnp
from jax import lax
from jax.experimental import pallas as pl
from jax.experimental.pallas import tpu as pltpu
from jax.sharding import PartitionSpec as P

FIELDS = 26
EMB = 16
DENSE = 13
BOTTOM = 96
D_IN = 512
H1 = 256
H2 = 128
TOWER = 64
TASKS = 2
LANES = 128
GROUPS = LANES // EMB
EMB_WIDTH = FIELDS * EMB
BIAS_ROWS = 16
GRAD_ROWS = 2 * D_IN + H1
WEIGHT_ROWS = GRAD_ROWS + BIAS_ROWS
STREAMS = 8
PARTS = 2
CHUNK_ROWS = 64
TABLE_CHUNKS = 2

F32 = jnp.float32
BF16 = jnp.bfloat16
I32 = jnp.int32


def iota(shape, axis):
    return lax.broadcasted_iota(I32, shape, axis)


def matmul(a, b):
    return lax.dot_general(a, b, (((1,), (0,)), ((), ())), preferred_element_type=F32)


def matmul_nt(a, b):
    return lax.dot_general(a, b, (((1,), (1,)), ((), ())), preferred_element_type=F32)


def matmul_tn(a, b):
    return lax.dot_general(a, b, (((0,), (0,)), ((), ())), preferred_element_type=F32)


def identity():
    return (iota((LANES, LANES), 0) == iota((LANES, LANES), 1)).astype(BF16)


def aligned(value, step):
    return pl.multiple_of(value, step)


def silu_parts(values):
    sig = jax.nn.sigmoid(values)
    return values * sig, sig * (1.0 + values * (1.0 - sig))


def route_kernel(
    owners, part_lookups, packed, table_lanes, batch_ref, owner_ref, local_ref, request_ref,
    back_ref, out_ref, high_ref, low_ref, value_ref, total_ref
):
    rows = high_ref.shape[0]
    part_rows = rows // PARTS
    filled = part_lookups // LANES
    slot_rows = request_ref.shape[0]
    shape = (rows, LANES)
    high_ref[...] = jnp.full(shape, -1, I32)
    low_ref[...] = jnp.zeros(shape, I32)
    for part in range(PARTS):
        lines = slice(part * part_rows, part * part_rows + filled)
        taken = slice(part * filled, (part + 1) * filled)
        for line in range(filled):
            start = (part * filled + line) * LANES
            high_ref[part * part_rows + line : part * part_rows + line + 1, :] = owner_ref[
                :, start : start + LANES
            ]
        low_ref[lines, :] = local_ref[taken, :]
    owner = high_ref[...]
    local = low_ref[...]
    row_id = iota(shape, 0)
    tri = (iota((LANES, LANES), 0) <= iota((LANES, LANES), 1)).astype(BF16)
    ones = jnp.ones((LANES, LANES), BF16)
    before = (iota((part_rows, part_rows), 1) < iota((part_rows, part_rows), 0)).astype(BF16)
    ranks = []
    for part in range(PARTS):
        own = owner[part * part_rows : (part + 1) * part_rows]
        rank = jnp.zeros((part_rows, LANES), F32)
        for one in range(owners):
            hit = own == one
            hits = jnp.where(hit, 1.0, 0.0).astype(BF16)
            upto = matmul(hits, tri)
            ahead = matmul(before, matmul(hits, ones).astype(BF16))
            rank = jnp.where(hit, upto + ahead - 1.0, rank)
        ranks.append(rank)
    rank = jnp.concatenate(ranks, axis=0)
    part_id = jnp.zeros(shape, I32)
    for part in range(1, PARTS):
        part_id = part_id + jnp.where(row_id >= part * part_rows, 1, 0)
    rank = rank.astype(I32)
    group = jnp.zeros(shape, I32)
    for step in range(1, GROUPS):
        group = group + jnp.where(rank >= step * packed, 1, 0)
    place = rank - group * packed
    held = jnp.maximum(owner, 0)
    chunks = packed // 16
    chunk = lax.shift_right_logical(place, 4)
    block = (held * PARTS + part_id) * chunks + chunk
    inside = group * 16 + (place & 15)
    table_group = lax.shift_right_logical(local, table_lanes)
    table_row = local & ((1 << table_lanes) - 1)
    high_ref[...] = jnp.where(owner < 0, -1, held * chunks + chunk)
    low_ref[...] = inside
    value_ref[...] = table_row + (((group - table_group) & (GROUPS - 1)) << table_lanes)
    lookup = (row_id - part_id * part_rows) * LANES + iota(shape, 1)
    quotient = jnp.floor((lookup.astype(F32) + 0.5) * (1.0 / FIELDS)).astype(I32)
    field_group = (lookup - quotient * FIELDS) & (GROUPS - 1)
    offset = 8 - (quotient & 7)
    turn = (field_group - group) & (GROUPS - 1)
    back_ref[...] = (turn * owners + held) * packed + place + offset
    away = ((held ^ batch_ref[0]) - held) * (PARTS * GROUPS * packed)
    out_ref[...] = block * LANES + inside + offset + away
    total_ref[...] = jnp.zeros_like(total_ref)
    own_rows = slot_rows // PARTS

    def gather_requests(part, step, carry):
        base = aligned(part * part_rows + step * 8, 8)
        high = high_ref[pl.ds(base, 8), :]
        low = low_ref[pl.ds(base, 8), :]
        values = value_ref[pl.ds(base, 8), :]
        upper = lax.shift_right_logical(values, 8).astype(F32)
        lower = (values & 255).astype(F32)
        at_high = []
        at_low = []
        for k in range(8):
            line = slice(k, k + 1)
            at_high.append(jnp.where(iota((own_rows, LANES), 0) == high[line], 1.0, 0.0).astype(BF16))
            same = iota((LANES, LANES), 0) == low[line]
            at_low.append(
                jnp.concatenate(
                    [jnp.where(same, upper[line], 0.0), jnp.where(same, lower[line], 0.0)], axis=0
                ).astype(BF16)
            )
        total_ref[part] += matmul_nt(
            jnp.concatenate(at_high, axis=1), jnp.concatenate(at_low, axis=1)
        )
        return carry

    for part in range(PARTS):
        lax.fori_loop(0, part_rows // 8, functools.partial(gather_requests, part), 0, unroll=3)
        total = (total_ref[part, :, :LANES] * 256.0 + total_ref[part, :, LANES:]).astype(I32)
        for one in range(owners):
            start = (one * PARTS + part) * chunks
            request_ref[start : start + chunks, :] = total[one * chunks : (one + 1) * chunks]


def pack_kernel(
    table_ref, hidden_w_ref, output_w_ref, hidden_b_ref, output_b_ref, packed_ref, weight_ref
):
    lines = []
    for values in (hidden_b_ref[:, :LANES], hidden_b_ref[:, LANES:], output_b_ref[...]):
        for _ in range(3):
            term = values.astype(BF16).astype(F32)
            lines.append(term)
            values = values - term
    lines.append(jnp.zeros((BIAS_ROWS - len(lines), LANES), F32))
    for half in range(H1 // LANES):
        weight_ref[half * D_IN : (half + 1) * D_IN, :] = hidden_w_ref[
            0, :, half * LANES : (half + 1) * LANES
        ]
    weight_ref[2 * D_IN : 2 * D_IN + H1, :] = output_w_ref[0]
    weight_ref[2 * D_IN + H1 :, :] = jnp.concatenate(lines, axis=0).astype(BF16)
    rows = table_ref.shape[1] // GROUPS
    eye = identity()

    def step(block, carry):
        pieces = []
        for group in range(GROUPS):
            start = aligned(group * rows + block * LANES, LANES)
            pieces.append(table_ref[:, pl.ds(start, LANES)])
        packed_ref[pl.ds(aligned(8 + block * LANES, 8), LANES), :] = matmul_nt(
            eye, jnp.concatenate(pieces, axis=0)
        )
        return carry

    packed_ref[0:8, :] = jnp.zeros((8, LANES), F32)
    packed_ref[8 + rows : 16 + rows, :] = jnp.zeros((8, LANES), F32)

    lax.fori_loop(0, rows // LANES, step, 0, unroll=8)


def masks():
    line = iota((8, LANES), 0)
    group = lax.shift_right_logical(iota((8, LANES), 1), 4)
    return [line == k for k in range(8)], [group == one for one in range(GROUPS)]


def turn_copies(rows_ref, wide_ref):
    rows = rows_ref.shape[0]
    half = GROUPS // 2
    from_lane = iota((LANES, half * LANES), 0)
    to_lane = iota((LANES, half * LANES), 1)
    turn = (lax.shift_right_logical(to_lane, 7) + half) * EMB
    turns = jnp.where(((from_lane + turn - to_lane) & (LANES - 1)) == 0, 1.0, 0.0).astype(BF16)

    def step(block, carry):
        start = aligned(block * LANES, LANES)
        piece = rows_ref[pl.ds(start, LANES), :]
        moved = matmul(piece, turns)
        piece = piece.astype(F32)
        for turn in range(GROUPS):
            if turn >= half:
                one = moved[:, (turn - half) * LANES : (turn - half + 1) * LANES]
            else:
                one = pltpu.roll(piece, turn * EMB, 1) if turn else piece
            wide_ref[pl.ds(aligned(8 + turn * rows + start, 8), LANES), :] = one
        return carry

    blocks = rows // LANES
    unroll = [count for count in (4, 3, 2, 1) if blocks % count == 0][0]
    lax.fori_loop(0, blocks, step, 0, unroll=unroll)


def assemble(wide_ref, word, groups, lines, lanes):
    block = jnp.zeros((8, LANES), F32)
    for place, group in groups:
        piece = wide_ref[pl.ds(word(0, place), 8), :]
        for k in range(1, 8):
            piece = jnp.where(lines[k], wide_ref[pl.ds(word(k, place), 8), :], piece)
        block = jnp.where(lanes[group], piece, block)
    return block


def word_stream(word_ref, buffers, sems, place, count, process, before=None):
    slots = len(buffers)
    size = buffers[0].shape[0]

    def copy(at, slot):
        start = aligned(place(at), LANES)
        return pltpu.make_async_copy(
            word_ref.at[pl.ds(start, size)], buffers[slot], sems.at[slot]
        )

    for slot in range(min(slots, count)):
        copy(slot, slot).start()
    if before is not None:
        before()

    def step(turn, carry):
        for slot in range(slots):
            at = turn * slots + slot
            copy(at, slot).wait()
            process(at, buffers[slot])

            @pl.when(at + slots < count)
            def _():
                copy(at + slots, slot).start()

        return carry

    lax.fori_loop(0, count // slots, step, 0)
    for slot in range(count % slots):
        at = count // slots * slots + slot
        copy(at, slot).wait()
        process(at, buffers[slot])


def slot_lines(numbers):
    own = (iota((16, LANES), 1) & 15) == iota((16, LANES), 0)
    return jnp.concatenate(
        [jnp.where(own, numbers[row : row + 1], 0.0) for row in range(numbers.shape[0])], axis=0
    ).astype(BF16)


def same_group():
    return (
        lax.shift_right_logical(iota((LANES, LANES), 0), 4)
        == lax.shift_right_logical(iota((LANES, LANES), 1), 4)
    ).astype(BF16)


def fetch_kernel(
    owners, part, packed, table_lanes, request_ref, asked_ref, table_ref, found_ref, turn_ref,
    piece_ref, left_ref, right_ref, sems
):
    lines, _ = masks()
    chunks = packed // 16
    within = same_group()
    group = lax.shift_right_logical(iota((8, LANES), 1), 4)
    bits = [(group & (1 << bit)) != 0 for bit in range(3)]

    def turn_step(source, carry):
        at = (source * PARTS + part) * chunks
        numbers = lax.shift_right_logical(asked_ref[pl.ds(at, chunks), :], table_lanes)
        turn_ref[pl.ds(aligned(source * packed, 16), packed), :] = matmul(
            slot_lines(numbers.astype(F32)), within
        )
        return carry

    def before():
        lax.fori_loop(0, owners, turn_step, 0, unroll=4)

    def process(source, words):
        for chunk in range(chunks):
            for line in range(LANES):
                base = chunk * LANES + line // 8 * 8
                pltpu.store(
                    piece_ref.at[base : base + 8, :],
                    table_ref[pl.ds(words[chunk * LANES + line], 8), :],
                    mask=lines[line % 8],
                )
            start = aligned(source * packed + chunk * 16, 16)
            turns = turn_ref[pl.ds(start, 16), :]
            halves = []
            for half in range(2):
                mixed = []
                for group in range(GROUPS):
                    base = chunk * LANES + group * 16 + half * 8
                    mixed.append(piece_ref[base : base + 8, :])
                for bit in range(3):
                    mixed = [
                        jnp.where(bits[bit], mixed[(turn + (1 << bit)) % GROUPS], mixed[turn])
                        for turn in range(GROUPS)
                    ]
                wanted = turns[half * 8 : (half + 1) * 8]
                block = mixed[0]
                for turn in range(1, GROUPS):
                    moved = pltpu.roll(mixed[turn], turn * EMB, 1)
                    block = jnp.where(wanted == float(turn), moved, block)
                halves.append(block)
            found_ref[pl.ds(start, 16), :] = jnp.concatenate(halves, axis=0).astype(BF16)

    size = chunks * LANES
    word_stream(
        request_ref,
        (left_ref, right_ref),
        sems,
        lambda at: (at * PARTS + part) * size,
        owners,
        process,
        before,
    )


def unpermute(
    part, part_rows, back_ref, returned_ref, feature_ref, first_row, wide_ref, buffers, sems
):
    lines, lanes = masks()
    size = buffers[0].shape[0]
    chunk_rows = size // FIELDS

    def process(chunk, words):
        for block in range(chunk_rows // 16):
            start_row = aligned(first_row + chunk * chunk_rows + block * 16, 16)
            for lane_block in range(D_IN // LANES):
                fields = range(lane_block * GROUPS, min((lane_block + 1) * GROUPS, FIELDS))
                halves = [
                    assemble(
                        wide_ref,
                        lambda k, field, half=half: words[
                            (block * 16 + half * 8 + k) * FIELDS + field
                        ],
                        [(field, field % GROUPS) for field in fields],
                        lines,
                        lanes,
                    )
                    for half in range(2)
                ]
                feature_ref[
                    pl.ds(start_row, 16), lane_block * LANES : (lane_block + 1) * LANES
                ] = jnp.concatenate(halves, axis=0).astype(BF16)

    first = part * back_ref.shape[0] // PARTS
    word_stream(
        back_ref,
        buffers,
        sems,
        lambda at: first + at * size,
        part_rows // chunk_rows,
        process,
        lambda: turn_copies(returned_ref, wide_ref),
    )


def gather_blocks(block_refs, whole_ref):
    rows = block_refs[0].shape[0]
    for one, block_ref in enumerate(block_refs):
        whole_ref[one * rows : (one + 1) * rows, :] = block_ref[...]


def unpermute_kernel(
    part, part_rows, back_ref, returned_ref, feature_ref, wide_ref, left_ref, right_ref, sems
):
    unpermute(
        part,
        part_rows,
        back_ref,
        returned_ref,
        feature_ref,
        0,
        wide_ref,
        (left_ref, right_ref),
        sems,
    )


def dense_kernel(
    order,
    part_rows,
    experts,
    scale,
    back_ref,
    out_ref,
    returned_ref,
    weight_ref,
    gate_ref,
    dense_ref,
    dense_w_ref,
    tower_ref,
    vector_ref,
    head_b_ref,
    label_ref,
    *refs,
):
    early = refs[: PARTS - 1]
    refs = refs[PARTS - 1 :]
    owners = len(order)
    sent_refs = refs[:owners]
    (
        grad_dense_ref,
        grad_weight_ref,
        grad_bias_ref,
        grad_shared_ref,
        wide_ref,
        feature_ref,
        turned_ref,
        hidden_ref,
        hidden_slope_ref,
        output_ref,
        output_slope_ref,
        gates_ref,
        mixed_ref,
        mixed_grad_ref,
        dot_ref,
        logit_ref,
        input_ref,
        low_ref,
        tiled_ref,
        left_ref,
        right_ref,
        sems,
        sent_ref,
    ) = refs[owners:]
    buffers = (left_ref, right_ref)
    width = turned_ref.shape[1]
    blocks = width // LANES
    slot_blocks = sent_ref.shape[0] // 16
    eye = identity()
    lines, lanes = masks()

    def put_weight(expert, cut, value):
        grad_weight_ref[expert, cut, :] = value.astype(BF16)

    def put_shared(rows, cut, value):
        grad_shared_ref[rows, cut] = value

    whole = slice(None)
    for part in range(PARTS - 1):
        feature_ref[part * part_rows : (part + 1) * part_rows, :] = early[part][...]
    unpermute(
        PARTS - 1,
        part_rows,
        back_ref,
        returned_ref,
        feature_ref,
        (PARTS - 1) * part_rows,
        wide_ref,
        buffers,
        sems,
    )

    for lane_block in range(D_IN // LANES):
        for block in range(blocks):
            piece = feature_ref[
                block * LANES : (block + 1) * LANES, lane_block * LANES : (lane_block + 1) * LANES
            ]
            turned_ref[
                lane_block * LANES : (lane_block + 1) * LANES, block * LANES : (block + 1) * LANES
            ] = matmul_nt(eye, piece).astype(BF16)
    dense = dense_ref[...]
    dense_w = dense_w_ref[...]
    turned_ref[EMB_WIDTH:, :] = matmul_tn(dense_w, dense).astype(BF16)

    features = turned_ref[...]
    logits = matmul(gate_ref[...], features)
    for task in range(TASKS):
        part_logits = logits[task * experts : (task + 1) * experts]
        powers = jnp.exp(part_logits - jnp.max(part_logits, axis=0, keepdims=True))
        gates_ref[task * experts : (task + 1) * experts, :] = powers / jnp.sum(
            powers, axis=0, keepdims=True
        )

    mixed_ref[...] = jnp.zeros_like(mixed_ref)

    def column(line):
        tall = jnp.transpose(jnp.broadcast_to(line, (LANES, LANES)))
        return jnp.concatenate([tall] * blocks, axis=1)

    def hidden_weights(expert):
        return jnp.concatenate(
            [weight_ref[expert, half * D_IN : (half + 1) * D_IN, :] for half in range(2)], axis=1
        )

    def bias_line(expert, rows):
        lines = [weight_ref[expert, 2 * D_IN + H1 :, :].astype(F32)[row : row + 1] for row in rows]
        return functools.reduce(jnp.add, lines)

    def forward(expert, carry):
        turned = turned_ref[...]
        bias = jnp.concatenate(
            [column(bias_line(expert, range(half * 3, half * 3 + 3))) for half in range(2)], axis=0
        )
        value, slope = silu_parts(matmul_tn(hidden_weights(expert), turned) + bias)
        hidden_ref[expert] = value.astype(BF16)
        hidden_slope_ref[expert] = slope
        weights = weight_ref[expert, 2 * D_IN : 2 * D_IN + H1, :]
        bias = column(bias_line(expert, (6, 7, 8)))
        value, slope = silu_parts(matmul_tn(weights, hidden_ref[expert]) + bias)
        output_ref[expert] = value
        output_slope_ref[expert] = slope
        for task in range(TASKS):
            mixed_ref[task * H2 : (task + 1) * H2, :] += (
                gates_ref[pl.ds(task * experts + expert, 1), :] * value
            )
        return carry

    lax.fori_loop(0, experts, forward, 0, unroll=2)

    tower_bias = column(vector_ref[0:1, :])
    head_w = column(vector_ref[1:2, :])
    tower = tower_ref[...]
    act_sums = []
    grad_sums = []
    head_sums = []
    for task in range(TASKS):
        units = slice(task * TOWER, (task + 1) * TOWER)
        outs = slice(task * H2, (task + 1) * H2)
        mixed = mixed_ref[outs, :]
        mixed_low = mixed.astype(BF16)
        tower_part = tower[:, units]
        act, slope = silu_parts(matmul_tn(tower_part, mixed_low) + tower_bias[units])
        score = jnp.sum(act * head_w[units], axis=0, keepdims=True) + head_b_ref[task]
        target = label_ref[task : task + 1, :].astype(F32)
        score_grad = (jax.nn.sigmoid(score) - target) * scale
        tower_grad = (score_grad * head_w[units] * slope).astype(BF16)
        act_sums.append(jnp.sum(score_grad * act, axis=1, keepdims=True))
        grad_sums.append(jnp.sum(tower_grad.astype(F32), axis=1, keepdims=True))
        head_sums.append(jnp.sum(score_grad, axis=1, keepdims=True))
        put_shared(slice(0, H2), units, matmul_nt(mixed_low, tower_grad))
        mixed_grad = matmul(tower_part, tower_grad).astype(BF16).astype(F32)
        mixed_grad_ref[outs, :] = mixed_grad
        dot_ref[task : task + 1, :] = jnp.sum(mixed_grad * mixed, axis=0, keepdims=True)
    column_sums = jnp.concatenate(
        [
            jnp.broadcast_to(jnp.concatenate(sums, axis=0), (LANES, LANES))
            for sums in (act_sums, grad_sums)
        ],
        axis=1,
    )
    put_shared(slice(H2, H2 + 8), whole, jnp.transpose(column_sums[:, :LANES])[0:8])
    put_shared(slice(H2 + 8, H2 + 16), whole, jnp.transpose(column_sums[:, LANES:])[0:8])
    head_line = jnp.zeros((8, LANES), F32)
    for task in range(TASKS):
        head_line = jnp.where(iota((8, LANES), 1) == task, head_sums[task], head_line)
    put_shared(slice(H2 + 16, H2 + 24), whole, head_line)

    input_ref[...] = jnp.zeros_like(input_ref)
    ones = jnp.ones((BIAS_ROWS, width), BF16)

    def backward(expert, carry):
        value = output_ref[expert]
        grad = jnp.zeros((H2, width), F32)
        for task in range(TASKS):
            mixed_grad = mixed_grad_ref[task * H2 : (task + 1) * H2, :]
            gate = gates_ref[pl.ds(task * experts + expert, 1), :]
            grad = grad + gate * mixed_grad
            along = jnp.sum(mixed_grad * value, axis=0, keepdims=True)
            logit_ref[pl.ds(task * experts + expert, 1), :] = gate * (
                along - dot_ref[task : task + 1, :]
            )
        output_grad = (grad * output_slope_ref[expert]).astype(BF16)
        hidden = hidden_ref[expert]
        put_weight(expert, slice(2 * D_IN, 2 * D_IN + H1), matmul_nt(hidden, output_grad))
        weights = weight_ref[expert, 2 * D_IN : 2 * D_IN + H1, :]
        hidden_grad = (matmul(weights, output_grad) * hidden_slope_ref[expert]).astype(BF16)
        weight_grad = matmul_nt(turned_ref[...], hidden_grad)
        for half in range(2):
            put_weight(
                expert,
                slice(half * D_IN, (half + 1) * D_IN),
                weight_grad[:, half * LANES : (half + 1) * LANES],
            )
        input_ref[...] += matmul(hidden_weights(expert), hidden_grad)
        hidden_sum = matmul_nt(ones, hidden_grad)[0:1]
        sums = [hidden_sum[:, half * LANES : (half + 1) * LANES] for half in range(2)]
        sums.append(matmul_nt(ones, output_grad)[0:1])
        sums.append(jnp.zeros((8 - 3, LANES), F32))
        grad_bias_ref[expert] = jnp.concatenate(sums, axis=0)
        return carry

    lax.fori_loop(0, experts, backward, 0, unroll=2)

    logit_grad = logit_ref[...].astype(BF16)
    gate_grad = matmul_nt(logit_grad, turned_ref[...])
    gate_base = H2 + 24
    pairs = TASKS * experts
    for lane_block in range(D_IN // LANES):
        put_shared(
            slice(gate_base + lane_block * pairs, gate_base + (lane_block + 1) * pairs),
            whole,
            gate_grad[:, lane_block * LANES : (lane_block + 1) * LANES],
        )
    low_ref[...] = (input_ref[...] + matmul_tn(gate_ref[...], logit_grad)).astype(BF16)
    bottom_grad = low_ref[EMB_WIDTH:, :]
    dense_base = gate_base + D_IN // LANES * pairs
    grad_dense_w = jnp.concatenate(
        [matmul_nt(dense, bottom_grad), jnp.zeros((DENSE, LANES - BOTTOM), F32)], axis=1
    )
    put_shared(
        slice(dense_base, dense_base + 16),
        whole,
        jnp.concatenate([grad_dense_w, jnp.zeros((16 - DENSE, LANES), F32)], axis=0),
    )
    grad_dense_ref[...] = matmul(dense_w, bottom_grad)

    def clear(step, carry):
        wide_ref[pl.ds(aligned(8 + step * LANES, 8), LANES), :] = jnp.zeros((LANES, LANES), F32)
        return carry

    chunk_rows = left_ref.shape[0] // FIELDS

    def make_tile(block, field):
        span = pl.ds(aligned(block * LANES, LANES), LANES)
        piece = low_ref[field * EMB : (field + 1) * EMB, span]
        tiled_ref[block & 1, field] = matmul_nt(eye, jnp.concatenate([piece] * GROUPS, axis=0))

    def permute(chunk, words):
        block = lax.div(chunk * chunk_rows, LANES)
        first = 0 if words is left_ref else chunk_rows
        ahead = list(range(FIELDS))[first * FIELDS // LANES : (first + chunk_rows) * FIELDS // LANES]
        later = jnp.minimum(block + 1, blocks - 1)
        for step in range(chunk_rows // 8):
            start_row = first + step * 8
            for field in range(FIELDS):
                place = step * FIELDS + field
                total = chunk_rows // 8 * FIELDS
                if place * len(ahead) // total != (place - 1) * len(ahead) // total:
                    made = ahead[place * len(ahead) // total]
                    make_tile(later, made)
                tile = tiled_ref[block & 1, field, start_row : start_row + 8, :]
                for k in range(8):
                    start = words[(step * 8 + k) * FIELDS + field]
                    pltpu.store(wide_ref.at[pl.ds(start, 8), :], tile, mask=lines[k])

    def permute_before():
        lax.fori_loop(0, slot_blocks, clear, 0, unroll=2)
        for field in range(FIELDS):
            make_tile(0, field)

    def permute_place(at):
        each = part_rows // chunk_rows
        part = lax.div(at, each)
        return part * (out_ref.shape[0] // PARTS) + (at - part * each) * (chunk_rows * FIELDS)

    word_stream(
        out_ref,
        buffers,
        sems,
        permute_place,
        width // chunk_rows,
        permute,
        permute_before,
    )

    def merge(block, carry):
        halves = []
        for half in range(2):
            piece = jnp.zeros((8, LANES), F32)
            for group in range(GROUPS):
                start = aligned(block * LANES + group * 16 + (half + 1) * 8, 8)
                piece = jnp.where(lanes[group], wide_ref[pl.ds(start, 8), :], piece)
            halves.append(piece)
        start = aligned(block * 16, 16)
        sent_ref[pl.ds(start, 16), :] = jnp.concatenate(halves, axis=0).astype(BF16)
        return carry

    lax.fori_loop(0, slot_blocks, merge, 0, unroll=4 if slot_blocks % 4 == 0 else 1)
    each = sent_ref.shape[0] // owners
    for one, held in enumerate(order):
        sent_refs[one][...] = sent_ref[held * each : (held + 1) * each, :]


def add_kernel(owners, packed, table_lanes, index_ref, request_ref, asked_ref, *refs):
    received_refs = refs[:owners]
    table_refs = refs[owners : owners + 2 * TABLE_CHUNKS]
    (
        received_ref,
        left_grad_ref,
        right_grad_ref,
        left_ref,
        right_ref,
        sems,
        *sums,
    ) = refs[owners + 2 * TABLE_CHUNKS :]
    rows = sums[0].shape[0] - 16
    core, batch = index_ref[0], index_ref[1]
    sources = received_ref.shape[0] // packed
    chunks = packed // 16
    lines, _ = masks()
    eye = identity()
    own_group = lax.shift_right_logical(iota((1, LANES), 1), 4)
    from_lane = iota((LANES, 2 * LANES), 0)
    to_lane = iota((LANES, 2 * LANES), 1)
    spread_names = []
    spread_grads = []
    for pair in range(GROUPS // 2):
        group = pair * 2 + lax.shift_right_logical(to_lane, 7)
        spread_names.append(
            jnp.where(lax.shift_right_logical(from_lane, 4) == group, 1.0, 0.0).astype(BF16)
        )
        wanted = group * EMB + (to_lane & (EMB - 1))
        spread_grads.append(jnp.where(from_lane == wanted, 1.0, 0.0).astype(BF16))

    def place(source):
        distance = lax.div(source, PARTS)
        return (distance ^ batch) * PARTS + source - distance * PARTS

    def spread(source, grad_ref):
        def step(first, count, pair):
            asked = asked_ref[pl.ds(place(source) * chunks + first, count), :]
            names = (own_group - lax.shift_right_logical(asked, table_lanes)) & (GROUPS - 1)
            start = aligned(source * packed + first * 16, 16)
            grads = received_ref[pl.ds(start, count * 16), :]
            lane_group = lax.shift_right_logical(iota((count * 16, LANES), 1), 4).astype(F32)
            wide_names = matmul(slot_lines(names.astype(F32)), spread_names[pair])
            wide_grads = matmul(grads, spread_grads[pair])
            for side in range(2):
                half = slice(side * LANES, (side + 1) * LANES)
                masked = jnp.where(wide_names[:, half] == lane_group, wide_grads[:, half], 0.0)
                for chunk in range(count):
                    start = (first + chunk) * LANES + (pair * 2 + side) * 16
                    grad_ref[start : start + 16, :] = masked[chunk * 16 : (chunk + 1) * 16]

        return [
            functools.partial(step, first, min(4, chunks - first), pair)
            for first in range(0, chunks, 4)
            for pair in range(GROUPS // 2)
        ]

    def clear(step, carry):
        for total in sums:
            total[pl.ds(aligned(8 + step * LANES, 8), LANES), :] = jnp.zeros((LANES, LANES), F32)
        return carry

    def before():
        for total in sums:
            total[0:8, :] = jnp.zeros((8, LANES), F32)
            total[8 + rows : 16 + rows, :] = jnp.zeros((8, LANES), F32)
        lax.fori_loop(0, rows // LANES, clear, 0)
        gather_blocks(received_refs, received_ref)
        for one in spread(0, left_grad_ref):
            one()

    def process(source, words):
        now, later = left_grad_ref, right_grad_ref
        if words is right_ref:
            now, later = later, now
        steps = spread(jnp.minimum(source + 1, sources - 1), later)
        rows = GROUPS * packed // 8
        for row in range(rows):
            if row * len(steps) // rows != (row - 1) * len(steps) // rows:
                steps[row * len(steps) // rows]()
            grads = now[row * 8 : (row + 1) * 8, :]
            for k in range(8):
                place = pl.ds(words[row * 8 + k], 8)
                total = sums[k % STREAMS]
                pltpu.store(total.at[place, :], total[place, :] + grads, mask=lines[k])

    size = GROUPS * packed
    word_stream(
        request_ref,
        (left_ref, right_ref),
        sems,
        lambda at: place(at) * size,
        sources,
        process,
        before,
    )

    def finish(kept, block, carry):
        start = aligned(8 + block * LANES, 8)
        total = functools.reduce(jnp.add, [one[pl.ds(start, LANES), :] for one in sums])
        turned = matmul_nt(eye, total.astype(BF16)).astype(BF16)
        each = GROUPS // (2 * TABLE_CHUNKS)
        for group in range(GROUPS):
            half, column = divmod(group, GROUPS // 2)
            chunk, column = divmod(column, each)
            table_ref = table_refs[chunk + (0 if half == kept else TABLE_CHUNKS)]
            column = aligned(column * rows + block * LANES, LANES)
            table_ref[:, pl.ds(column, LANES)] = turned[group * EMB : (group + 1) * EMB]
        return carry

    for kept in range(2):

        @pl.when(core == kept)
        def _():
            lax.fori_loop(0, rows // LANES, functools.partial(finish, kept), 0, unroll=8)


def unpack_kernel(weight_piece, extra_piece, pairs, piece_ref, *refs):
    (
        dense_w_ref,
        gate_ref,
        hidden_w_ref,
        hidden_b_ref,
        output_w_ref,
        output_b_ref,
        tower_w_ref,
        tower_b_ref,
        head_w_ref,
        head_b_ref,
        weight_ref,
        extra_ref,
    ) = refs
    for owner in range(piece_ref.shape[0]):
        weight_ref[owner * weight_piece : (owner + 1) * weight_piece, :] = piece_ref[
            owner, :weight_piece, :
        ].astype(F32)
        high = piece_ref[owner, weight_piece : weight_piece + extra_piece, :].astype(F32)
        low = piece_ref[owner, weight_piece + extra_piece :, :].astype(F32)
        extra_ref[owner * extra_piece : (owner + 1) * extra_piece, :] = high + low
    gate_rows = D_IN // LANES * pairs
    small = H2 + gate_rows + 16

    def small_line(row):
        return extra_ref[small + row : small + row + 1, :] + extra_ref[small + 6 + row : small + 7 + row, :]

    for half in range(H1 // LANES):
        span = slice(half * LANES, (half + 1) * LANES)
        hidden_w_ref[0, :, span] = weight_ref[half * D_IN : (half + 1) * D_IN, :]
        hidden_b_ref[:, span] = small_line(3 + half)
    output_w_ref[0] = weight_ref[2 * D_IN : GRAD_ROWS, :]
    output_b_ref[...] = small_line(5)
    tower_w_ref[...] = extra_ref[:H2, :]
    head_w_ref[...] = small_line(0)
    tower_b_ref[...] = small_line(1)
    head_b_ref[...] = small_line(2)[:, :TASKS]
    for block in range(D_IN // LANES):
        gate_ref[:, block * LANES : (block + 1) * LANES] = extra_ref[
            H2 + block * pairs : H2 + (block + 1) * pairs, :
        ]
    dense_w_ref[...] = extra_ref[H2 + gate_rows : H2 + gate_rows + DENSE, :BOTTOM]


SMEM = pl.BlockSpec(memory_space=pltpu.SMEM)
VMEM = pl.BlockSpec(memory_space=pltpu.VMEM)
ANY = pl.BlockSpec(memory_space=pl.ANY)


def call(kernel, outs, ins, scratch, name, micros, vmem=16):
    return pl.pallas_call(
        kernel,
        out_shape=outs,
        in_specs=ins,
        out_specs=jax.tree.map(lambda _: VMEM, outs),
        scratch_shapes=scratch,
        name=name,
        cost_estimate=pl.CostEstimate(
            flops=int(micros * 1.15e9), bytes_accessed=int(micros * 3e6), transcendentals=0
        ),
        compiler_params=pltpu.CompilerParams(vmem_limit_bytes=vmem << 20),
    )


def shards(
    emb_table,
    dense_feats,
    dense_w,
    gate_w,
    hidden_w,
    hidden_b,
    output_w,
    output_b,
    tower_w,
    tower_b,
    head_w,
    head_b,
    row_owner,
    local_row,
    labels,
):
    owners = lax.axis_size("batch")
    experts = lax.axis_size("expert")
    expert_index = lax.axis_index("expert")
    core = expert_index & 1
    row_total = dense_feats.shape[1]
    part_rows = row_total // PARTS
    lookups = row_total * FIELDS
    part_lookups = lookups // PARTS
    capacity = 2 * part_lookups // owners
    packed = -(-capacity // (GROUPS * 16)) * 16
    table_rows = emb_table.shape[0]
    table_packed = table_rows // GROUPS
    table_lanes = table_packed.bit_length() - 1
    scale = 1.0 / math.sqrt(row_total * owners * experts)
    slots = owners * PARTS * GROUPS * packed
    part_slots = owners * packed
    lookup_rows = lookups // LANES
    list_part = -(-lookup_rows // (PARTS * 24)) * 24
    list_rows = list_part * PARTS

    def tie(*values):
        return lax.optimization_barrier(values)

    def exchange(values, axis):
        return lax.all_to_all(values, axis, split_axis=0, concat_axis=0, tiled=True)

    def swap(values, axis, bits):
        size = lax.axis_size(axis)
        return lax.ppermute(values, axis, [(one, one ^ bits) for one in range(size)])

    order = sorted(range(owners), key=lambda bits: (-bits.bit_length(), bits))

    owner_list = row_owner.T
    local_list = local_row.reshape(lookup_rows, LANES)
    slot_rows = slots // LANES
    list_shape = jax.ShapeDtypeStruct((list_rows, LANES), I32)
    batch_index = lax.axis_index("batch").reshape(1)
    requests, back, out = call(
        functools.partial(route_kernel, owners, part_lookups, packed, table_lanes),
        (jax.ShapeDtypeStruct((slot_rows, LANES), I32), list_shape, list_shape),
        [SMEM, VMEM, VMEM],
        [pltpu.VMEM((list_rows, LANES), I32)] * 3 + [pltpu.VMEM((PARTS, slot_rows // PARTS, 2 * LANES), F32)],
        "route",
        9,
    )(batch_index, owner_list, local_list)
    asked = exchange(requests.reshape(owners, slots // owners), "batch")
    asked = asked.reshape(slot_rows, LANES)
    offset = 8 - (jnp.arange(LANES, dtype=I32) & 7)
    words = ((asked & (table_packed - 1)) + offset).reshape(-1)
    back = back.reshape(-1)
    out = out.reshape(-1)

    hidden_b, out = tie(hidden_b, out)
    table, weights = call(
        pack_kernel,
        (
            pltpu.VMEM((table_packed + 16, LANES), F32),
            jax.ShapeDtypeStruct((WEIGHT_ROWS, LANES), BF16),
        ),
        [VMEM] * 5,
        [],
        "pack",
        5,
    )(emb_table.T, hidden_w, output_w, hidden_b, output_b)
    table = pltpu.with_memory_space_constraint(table, pltpu.VMEM)
    weights = lax.all_gather(weights, "expert", axis=0, tiled=False)

    slot_words = [pltpu.SMEM((GROUPS * packed,), I32)] * 2 + [pltpu.SemaphoreType.DMA((2,))]
    row_words = [pltpu.SMEM((CHUNK_ROWS * FIELDS,), I32)] * 2 + [pltpu.SemaphoreType.DMA((2,))]
    returned = []
    for part in range(PARTS):
        found = call(
            functools.partial(fetch_kernel, owners, part, packed, table_lanes),
            jax.ShapeDtypeStruct((part_slots, LANES), BF16),
            [ANY, VMEM, VMEM],
            [
                pltpu.VMEM((part_slots, LANES), F32),
                pltpu.VMEM((GROUPS * packed, LANES), F32),
            ]
            + slot_words,
            "fetch",
            24 // PARTS,
        )(words, asked, table)
        found = exchange(found.reshape(owners, packed, LANES), "batch")
        returned.append(found.reshape(part_slots, LANES))
    early = []
    for part in range(PARTS - 1):
        early.append(
            call(
                functools.partial(unpermute_kernel, part, part_rows),
                jax.ShapeDtypeStruct((part_rows, D_IN), BF16),
                [ANY, VMEM],
                [pltpu.VMEM((GROUPS * part_slots + 16, LANES), F32), *row_words],
                "unpermute",
                15,
            )(back, returned[part])
        )

    pairs = TASKS * experts
    shared_rows = H2 + 24 + D_IN // LANES * pairs + 16
    vectors = jnp.stack([tower_b, head_w])
    *sent, grad_dense, grad_weight, grad_bias, grad_shared = call(
        functools.partial(dense_kernel, order, part_rows, experts, scale),
        (
            *[jax.ShapeDtypeStruct((PARTS * packed, LANES), BF16)] * owners,
            jax.ShapeDtypeStruct((DENSE, row_total), F32),
            jax.ShapeDtypeStruct((experts, GRAD_ROWS, LANES), BF16),
            jax.ShapeDtypeStruct((experts, 8, LANES), F32),
            jax.ShapeDtypeStruct((shared_rows, LANES), F32),
        ),
        [ANY, ANY] + [VMEM] * 7 + [SMEM] + [VMEM] * PARTS,
        [
            pltpu.VMEM((slots + 16, LANES), F32),
            pltpu.VMEM((row_total, D_IN), BF16),
            pltpu.VMEM((D_IN, row_total), BF16),
            pltpu.VMEM((experts, H1, row_total), BF16),
            pltpu.VMEM((experts, H1, row_total), F32),
            pltpu.VMEM((experts, H2, row_total), F32),
            pltpu.VMEM((experts, H2, row_total), F32),
            pltpu.VMEM((pairs, row_total), F32),
            pltpu.VMEM((TASKS * H2, row_total), F32),
            pltpu.VMEM((TASKS * H2, row_total), F32),
            pltpu.VMEM((8, row_total), F32),
            pltpu.VMEM((pairs, row_total), F32),
            pltpu.VMEM((D_IN, row_total), F32),
            pltpu.VMEM((D_IN, row_total), BF16),
            pltpu.VMEM((2, FIELDS, LANES, LANES), F32),
            *row_words,
            pltpu.VMEM((PARTS * part_slots, LANES), BF16),
        ],
        "dense",
        45,
        min(60, 30 + 4 * experts),
    )(
        back,
        out,
        returned[-1],
        weights,
        gate_w.T,
        dense_feats,
        dense_w,
        tower_w,
        vectors,
        head_b,
        labels,
        *early,
    )
    moved = {bits: swap(one, "batch", bits) if bits else one for bits, one in zip(order, sent)}
    received = [moved[bits] for bits in range(owners)]

    def split(values):
        high = lax.reduce_precision(values, exponent_bits=8, mantissa_bits=7)
        return high.astype(BF16), (values - high).astype(BF16)

    received[1], grad_weight, grad_bias, grad_shared = tie(
        received[1], grad_weight, grad_bias, grad_shared
    )

    def spread_rows(values, piece):
        rows = values.shape[1]
        values = jnp.pad(values, ((0, 0), (0, piece * owners - rows), (0, 0)))
        return values.reshape(experts, owners, piece, LANES).transpose(1, 0, 2, 3)

    large = jnp.concatenate([grad_shared[:H2], grad_shared[H2 + 24 :]], axis=0).astype(BF16)
    small = jnp.concatenate([grad_shared[H2 + 8 * row : H2 + 8 * row + 1] for row in range(3)])
    small = jnp.concatenate(
        [jnp.broadcast_to(small[None], (experts, 3, LANES)), grad_bias[:, :3]], axis=1
    )
    extra = jnp.concatenate(
        [jnp.broadcast_to(large[None], (experts, *large.shape)), *split(small)], axis=1
    )
    weight_piece = -(-GRAD_ROWS // (16 * owners)) * 16
    extra_piece = -(-extra.shape[1] // (16 * owners)) * 16
    piece_rows = weight_piece + extra_piece
    pieces = jnp.concatenate(
        [spread_rows(grad_weight, weight_piece), spread_rows(extra, extra_piece)], axis=2
    )
    late = owners - 2
    *received[:late], pieces = tie(*received[:late], pieces)
    pieces = exchange(pieces.reshape(owners * experts, piece_rows, LANES), ("batch", "expert"))

    columns = table_rows // 2 // TABLE_CHUNKS
    table_part = call(
        functools.partial(add_kernel, owners, packed, table_lanes),
        (jax.ShapeDtypeStruct((EMB, columns), BF16),) * (2 * TABLE_CHUNKS),
        [SMEM, ANY, VMEM] + [VMEM] * owners,
        [pltpu.VMEM((PARTS * part_slots, LANES), BF16)]
        + [pltpu.VMEM((GROUPS * packed, LANES), F32)] * 2
        + slot_words
        + [pltpu.VMEM((table_packed + 16, LANES), F32)] * STREAMS,
        "add",
        60,
        48,
    )(jnp.concatenate([core.reshape(1), batch_index]), words, asked, *received)

    def add_low(left, right):
        return (left.astype(F32) + right.astype(F32)).astype(BF16)

    *table_part, pieces = tie(*table_part, pieces)
    kept = [
        add_low(one, swap(other, "expert", 1))
        for one, other in zip(table_part[:TABLE_CHUNKS], table_part[TABLE_CHUNKS:])
    ]
    sums = jnp.sum(pieces.astype(F32), axis=0)
    piece = jnp.concatenate([sums[:weight_piece].astype(BF16), *split(sums[weight_piece:])], axis=0)
    *kept, piece = tie(*kept, piece)
    bit = 2
    over = [swap(one, "expert", bit) for one in kept]
    pieces = exchange(jnp.broadcast_to(piece[None], (owners, *piece.shape)), "batch")
    while bit < experts:
        kept = [add_low(one, other) for one, other in zip(kept, over)]
        bit *= 2
        if bit < experts:
            over = [swap(one, "expert", bit) for one in kept]
    small = call(
        functools.partial(unpack_kernel, weight_piece, extra_piece, pairs),
        tuple(
            jax.ShapeDtypeStruct(shape, F32)
            for shape in (
                (DENSE, BOTTOM),
                (pairs, D_IN),
                (1, D_IN, H1),
                (1, H1),
                (1, H1, H2),
                (1, H2),
                (H2, TASKS * TOWER),
                (1, TASKS * TOWER),
                (1, TASKS * TOWER),
                (1, TASKS),
            )
        ),
        [VMEM],
        [
            pltpu.VMEM((owners * weight_piece, LANES), F32),
            pltpu.VMEM((owners * extra_piece, LANES), F32),
        ],
        "unpack",
        3,
    )(pieces)
    others = [swap(one, "expert", 1) for one in kept]
    *others, small = tie(*others, small)
    lower = [jnp.where(core == 0, one, other) for one, other in zip(kept, others)]
    upper = [jnp.where(core == 0, other, one) for one, other in zip(kept, others)]
    table_total = jnp.concatenate(lower + upper, axis=1).astype(F32).T
    grad_dense_w, gate, hidden, hidden_bias, output, output_bias, tower, tower_bias, head, head_bias = (
        small
    )
    return (
        table_total,
        grad_dense,
        grad_dense_w,
        gate.T,
        hidden,
        hidden_bias,
        output,
        output_bias,
        tower,
        tower_bias.reshape(-1),
        head.reshape(-1),
        head_bias.reshape(-1),
    )


def solution(mesh):
    in_specs = (
        P("batch", None),
        P(None, ("batch", "expert")),
        P(),
        P(),
        P("expert", None, None),
        P("expert", None),
        P("expert", None, None),
        P("expert", None),
        P(),
        P(),
        P(),
        P(),
        P(("batch", "expert"), None),
        P(("batch", "expert")),
        P(None, ("batch", "expert")),
    )
    out_specs = (
        P("batch", None),
        P(None, ("batch", "expert")),
        P(),
        P(),
        P("expert", None, None),
        P("expert", None),
        P("expert", None, None),
        P("expert", None),
        P(),
        P(),
        P(),
        P(),
    )
    return jax.shard_map(shards, mesh=mesh, in_specs=in_specs, out_specs=out_specs, check_vma=False)
```

```python
import functools
import math

import jax
import jax.numpy as jnp
from jax import lax
from jax.experimental import pallas as pl
from jax.experimental.pallas import tpu as pltpu
from jax.sharding import PartitionSpec as P

FIELDS = 26
EMB = 16
DENSE = 13
BOTTOM = 96
D_IN = 512
H1 = 256
H2 = 128
TOWER = 64
TASKS = 2
LANES = 128
GROUPS = LANES // EMB
EMB_WIDTH = FIELDS * EMB
BIAS_ROWS = 16
GRAD_ROWS = 2 * D_IN + H1
WEIGHT_ROWS = GRAD_ROWS + BIAS_ROWS
STREAMS = 8
PARTS = 2
CHUNK_ROWS = 64
TABLE_CHUNKS = 1

F32 = jnp.float32
BF16 = jnp.bfloat16
I32 = jnp.int32


def iota(shape, axis):
    return lax.broadcasted_iota(I32, shape, axis)


def matmul(a, b):
    return lax.dot_general(a, b, (((1,), (0,)), ((), ())), preferred_element_type=F32)


def matmul_nt(a, b):
    return lax.dot_general(a, b, (((1,), (1,)), ((), ())), preferred_element_type=F32)


def matmul_tn(a, b):
    return lax.dot_general(a, b, (((0,), (0,)), ((), ())), preferred_element_type=F32)


def identity():
    return (iota((LANES, LANES), 0) == iota((LANES, LANES), 1)).astype(BF16)


def aligned(value, step):
    return pl.multiple_of(value, step)


def silu_parts(values):
    sig = jax.nn.sigmoid(values)
    return values * sig, sig * (1.0 + values * (1.0 - sig))


def route_kernel(
    owners, part_lookups, packed, table_lanes, batch_ref, owner_ref, local_ref, request_ref,
    back_ref, out_ref, high_ref, low_ref, value_ref, total_ref
):
    rows = high_ref.shape[0]
    part_rows = rows // PARTS
    filled = part_lookups // LANES
    slot_rows = request_ref.shape[0]
    shape = (rows, LANES)
    high_ref[...] = jnp.full(shape, -1, I32)
    low_ref[...] = jnp.zeros(shape, I32)
    for part in range(PARTS):
        lines = slice(part * part_rows, part * part_rows + filled)
        taken = slice(part * filled, (part + 1) * filled)
        high_ref[lines, :] = owner_ref[taken, :]
        low_ref[lines, :] = local_ref[taken, :]
    owner = high_ref[...]
    local = low_ref[...]
    row_id = iota(shape, 0)
    tri = (iota((LANES, LANES), 0) <= iota((LANES, LANES), 1)).astype(BF16)
    ones = jnp.ones((LANES, LANES), BF16)
    before = (iota((part_rows, part_rows), 1) < iota((part_rows, part_rows), 0)).astype(BF16)
    ranks = []
    for part in range(PARTS):
        own = owner[part * part_rows : (part + 1) * part_rows]
        rank = jnp.zeros((part_rows, LANES), F32)
        for one in range(owners):
            hit = own == one
            hits = jnp.where(hit, 1.0, 0.0).astype(BF16)
            upto = matmul(hits, tri)
            ahead = matmul(before, matmul(hits, ones).astype(BF16))
            rank = jnp.where(hit, upto + ahead - 1.0, rank)
        ranks.append(rank)
    rank = jnp.concatenate(ranks, axis=0)
    part_id = jnp.zeros(shape, I32)
    for part in range(1, PARTS):
        part_id = part_id + jnp.where(row_id >= part * part_rows, 1, 0)
    rank = rank.astype(I32)
    group = jnp.zeros(shape, I32)
    for step in range(1, GROUPS):
        group = group + jnp.where(rank >= step * packed, 1, 0)
    place = rank - group * packed
    held = jnp.maximum(owner, 0)
    chunks = packed // 16
    chunk = lax.shift_right_logical(place, 4)
    block = (held * PARTS + part_id) * chunks + chunk
    inside = group * 16 + (place & 15)
    table_group = lax.shift_right_logical(local, table_lanes)
    table_row = local & ((1 << table_lanes) - 1)
    high_ref[...] = jnp.where(owner < 0, -1, held * chunks + chunk)
    low_ref[...] = inside
    value_ref[...] = table_row + (((group - table_group) & (GROUPS - 1)) << table_lanes)
    lookup = (row_id - part_id * part_rows) * LANES + iota(shape, 1)
    quotient = jnp.floor((lookup.astype(F32) + 0.5) * (1.0 / FIELDS)).astype(I32)
    field_group = (lookup - quotient * FIELDS) & (GROUPS - 1)
    offset = 8 - (quotient & 7)
    turn = (field_group - group) & (GROUPS - 1)
    back_ref[...] = (turn * owners + held) * packed + place + offset
    away = ((held ^ batch_ref[0]) - held) * (PARTS * GROUPS * packed)
    out_ref[...] = block * LANES + inside + offset + away
    total_ref[...] = jnp.zeros_like(total_ref)
    own_rows = slot_rows // PARTS

    def gather_requests(part, step, carry):
        base = aligned(part * part_rows + step * 8, 8)
        high = high_ref[pl.ds(base, 8), :]
        low = low_ref[pl.ds(base, 8), :]
        values = value_ref[pl.ds(base, 8), :]
        upper = lax.shift_right_logical(values, 8).astype(F32)
        lower = (values & 255).astype(F32)
        at_high = []
        at_low = []
        for k in range(8):
            line = slice(k, k + 1)
            at_high.append(jnp.where(iota((own_rows, LANES), 0) == high[line], 1.0, 0.0).astype(BF16))
            same = iota((LANES, LANES), 0) == low[line]
            at_low.append(
                jnp.concatenate(
                    [jnp.where(same, upper[line], 0.0), jnp.where(same, lower[line], 0.0)], axis=0
                ).astype(BF16)
            )
        total_ref[part] += matmul_nt(
            jnp.concatenate(at_high, axis=1), jnp.concatenate(at_low, axis=1)
        )
        return carry

    for part in range(PARTS):
        lax.fori_loop(0, part_rows // 8, functools.partial(gather_requests, part), 0, unroll=3)
        total = (total_ref[part, :, :LANES] * 256.0 + total_ref[part, :, LANES:]).astype(I32)
        for one in range(owners):
            start = (one * PARTS + part) * chunks
            request_ref[start : start + chunks, :] = total[one * chunks : (one + 1) * chunks]


def pack_kernel(
    table_ref, hidden_w_ref, output_w_ref, hidden_b_ref, output_b_ref, packed_ref, weight_ref
):
    lines = []
    for values in (hidden_b_ref[:, :LANES], hidden_b_ref[:, LANES:], output_b_ref[...]):
        for _ in range(3):
            term = values.astype(BF16).astype(F32)
            lines.append(term)
            values = values - term
    lines.append(jnp.zeros((BIAS_ROWS - len(lines), LANES), F32))
    for half in range(H1 // LANES):
        weight_ref[half * D_IN : (half + 1) * D_IN, :] = hidden_w_ref[
            0, :, half * LANES : (half + 1) * LANES
        ]
    weight_ref[2 * D_IN : 2 * D_IN + H1, :] = output_w_ref[0]
    weight_ref[2 * D_IN + H1 :, :] = jnp.concatenate(lines, axis=0).astype(BF16)
    rows = table_ref.shape[1] // GROUPS
    eye = identity()

    def step(block, carry):
        pieces = []
        for group in range(GROUPS):
            start = aligned(group * rows + block * LANES, LANES)
            pieces.append(table_ref[:, pl.ds(start, LANES)])
        packed_ref[pl.ds(aligned(8 + block * LANES, 8), LANES), :] = matmul_nt(
            eye, jnp.concatenate(pieces, axis=0)
        )
        return carry

    packed_ref[0:8, :] = jnp.zeros((8, LANES), F32)
    packed_ref[8 + rows : 16 + rows, :] = jnp.zeros((8, LANES), F32)

    lax.fori_loop(0, rows // LANES, step, 0, unroll=8)


def masks():
    line = iota((8, LANES), 0)
    group = lax.shift_right_logical(iota((8, LANES), 1), 4)
    return [line == k for k in range(8)], [group == one for one in range(GROUPS)]


def turn_copies(rows_ref, wide_ref):
    rows = rows_ref.shape[0]
    half = GROUPS // 2
    from_lane = iota((LANES, half * LANES), 0)
    to_lane = iota((LANES, half * LANES), 1)
    turn = (lax.shift_right_logical(to_lane, 7) + half) * EMB
    turns = jnp.where(((from_lane + turn - to_lane) & (LANES - 1)) == 0, 1.0, 0.0).astype(BF16)

    def step(block, carry):
        start = aligned(block * LANES, LANES)
        piece = rows_ref[pl.ds(start, LANES), :]
        moved = matmul(piece, turns)
        piece = piece.astype(F32)
        for turn in range(GROUPS):
            if turn >= half:
                one = moved[:, (turn - half) * LANES : (turn - half + 1) * LANES]
            else:
                one = pltpu.roll(piece, turn * EMB, 1) if turn else piece
            wide_ref[pl.ds(aligned(8 + turn * rows + start, 8), LANES), :] = one
        return carry

    blocks = rows // LANES
    unroll = [count for count in (4, 3, 2, 1) if blocks % count == 0][0]
    lax.fori_loop(0, blocks, step, 0, unroll=unroll)


def assemble(wide_ref, word, groups, lines, lanes):
    block = jnp.zeros((8, LANES), F32)
    for place, group in groups:
        piece = wide_ref[pl.ds(word(0, place), 8), :]
        for k in range(1, 8):
            piece = jnp.where(lines[k], wide_ref[pl.ds(word(k, place), 8), :], piece)
        block = jnp.where(lanes[group], piece, block)
    return block


def word_stream(word_ref, buffers, sems, place, count, process, before=None):
    slots = len(buffers)
    size = buffers[0].shape[0]

    def copy(at, slot):
        start = aligned(place(at), LANES)
        return pltpu.make_async_copy(
            word_ref.at[pl.ds(start, size)], buffers[slot], sems.at[slot]
        )

    for slot in range(min(slots, count)):
        copy(slot, slot).start()
    if before is not None:
        before()

    def step(turn, carry):
        for slot in range(slots):
            at = turn * slots + slot
            copy(at, slot).wait()
            process(at, buffers[slot])

            @pl.when(at + slots < count)
            def _():
                copy(at + slots, slot).start()

        return carry

    lax.fori_loop(0, count // slots, step, 0)
    for slot in range(count % slots):
        at = count // slots * slots + slot
        copy(at, slot).wait()
        process(at, buffers[slot])


def slot_lines(numbers):
    own = (iota((16, LANES), 1) & 15) == iota((16, LANES), 0)
    return jnp.concatenate(
        [jnp.where(own, numbers[row : row + 1], 0.0) for row in range(numbers.shape[0])], axis=0
    ).astype(BF16)


def same_group():
    return (
        lax.shift_right_logical(iota((LANES, LANES), 0), 4)
        == lax.shift_right_logical(iota((LANES, LANES), 1), 4)
    ).astype(BF16)


def fetch_kernel(
    owners, part, packed, table_lanes, request_ref, asked_ref, far_table_ref, found_ref, table_ref,
    turn_ref, piece_ref, left_ref, right_ref, sems, table_sem
):
    table_copy = pltpu.make_async_copy(far_table_ref, table_ref, table_sem)
    table_copy.start()
    lines, _ = masks()
    chunks = packed // 16
    within = same_group()
    group = lax.shift_right_logical(iota((8, LANES), 1), 4)
    bits = [(group & (1 << bit)) != 0 for bit in range(3)]

    def turn_step(source, carry):
        at = (source * PARTS + part) * chunks
        numbers = lax.shift_right_logical(asked_ref[pl.ds(at, chunks), :], table_lanes)
        turn_ref[pl.ds(aligned(source * packed, 16), packed), :] = matmul(
            slot_lines(numbers.astype(F32)), within
        )
        return carry

    def before():
        lax.fori_loop(0, owners, turn_step, 0, unroll=4)
        table_copy.wait()

    def process(source, words):
        for chunk in range(chunks):
            for line in range(LANES):
                base = chunk * LANES + line // 8 * 8
                pltpu.store(
                    piece_ref.at[base : base + 8, :],
                    table_ref[pl.ds(words[chunk * LANES + line], 8), :],
                    mask=lines[line % 8],
                )
            start = aligned(source * packed + chunk * 16, 16)
            turns = turn_ref[pl.ds(start, 16), :]
            halves = []
            for half in range(2):
                mixed = []
                for group in range(GROUPS):
                    base = chunk * LANES + group * 16 + half * 8
                    mixed.append(piece_ref[base : base + 8, :])
                for bit in range(3):
                    mixed = [
                        jnp.where(bits[bit], mixed[(turn + (1 << bit)) % GROUPS], mixed[turn])
                        for turn in range(GROUPS)
                    ]
                wanted = turns[half * 8 : (half + 1) * 8]
                block = mixed[0]
                for turn in range(1, GROUPS):
                    moved = pltpu.roll(mixed[turn], turn * EMB, 1)
                    block = jnp.where(wanted == float(turn), moved, block)
                halves.append(block)
            found_ref[pl.ds(start, 16), :] = jnp.concatenate(halves, axis=0).astype(BF16)

    size = chunks * LANES
    word_stream(
        request_ref,
        (left_ref, right_ref),
        sems,
        lambda at: (at * PARTS + part) * size,
        owners,
        process,
        before,
    )


def unpermute(
    part, part_rows, back_ref, returned_ref, feature_ref, first_row, wide_ref, buffers, sems
):
    lines, lanes = masks()
    size = buffers[0].shape[0]
    chunk_rows = size // FIELDS

    def process(chunk, words):
        for block in range(chunk_rows // 16):
            start_row = aligned(first_row + chunk * chunk_rows + block * 16, 16)
            for lane_block in range(D_IN // LANES):
                fields = range(lane_block * GROUPS, min((lane_block + 1) * GROUPS, FIELDS))
                halves = [
                    assemble(
                        wide_ref,
                        lambda k, field, half=half: words[
                            (block * 16 + half * 8 + k) * FIELDS + field
                        ],
                        [(field, field % GROUPS) for field in fields],
                        lines,
                        lanes,
                    )
                    for half in range(2)
                ]
                feature_ref[
                    pl.ds(start_row, 16), lane_block * LANES : (lane_block + 1) * LANES
                ] = jnp.concatenate(halves, axis=0).astype(BF16)

    first = part * back_ref.shape[0] // PARTS
    word_stream(
        back_ref,
        buffers,
        sems,
        lambda at: first + at * size,
        part_rows // chunk_rows,
        process,
        lambda: turn_copies(returned_ref, wide_ref),
    )


def gather_blocks(order, block_refs, whole_ref):
    rows = block_refs[0].shape[0]
    for held, block_ref in zip(order, block_refs):
        whole_ref[held * rows : (held + 1) * rows, :] = block_ref[...]


def unpermute_kernel(
    part, part_rows, back_ref, returned_ref, feature_ref, wide_ref, left_ref, right_ref, sems
):
    unpermute(
        part,
        part_rows,
        back_ref,
        returned_ref,
        feature_ref,
        0,
        wide_ref,
        (left_ref, right_ref),
        sems,
    )


def dense_kernel(
    order,
    part_rows,
    experts,
    scale,
    back_ref,
    out_ref,
    returned_ref,
    weight_ref,
    gate_ref,
    dense_ref,
    dense_w_ref,
    tower_ref,
    vector_ref,
    head_b_ref,
    label_ref,
    *refs,
):
    early = refs[: PARTS - 1]
    refs = refs[PARTS - 1 :]
    owners = len(order)
    sent_refs = refs[:owners]
    (
        grad_dense_ref,
        grad_weight_ref,
        grad_bias_ref,
        grad_shared_ref,
        wide_ref,
        feature_ref,
        turned_ref,
        hidden_ref,
        hidden_slope_ref,
        output_ref,
        output_slope_ref,
        gates_ref,
        mixed_ref,
        mixed_grad_ref,
        dot_ref,
        logit_ref,
        input_ref,
        low_ref,
        tiled_ref,
        left_ref,
        right_ref,
        sems,
        sent_ref,
    ) = refs[owners:]
    buffers = (left_ref, right_ref)
    width = turned_ref.shape[1]
    blocks = width // LANES
    slot_blocks = sent_ref.shape[0] // 16
    eye = identity()
    lines, lanes = masks()

    def put_weight(expert, cut, value):
        grad_weight_ref[expert, cut, :] = value.astype(BF16)

    def put_shared(rows, cut, value):
        grad_shared_ref[rows, cut] = value

    whole = slice(None)
    for part in range(PARTS - 1):
        feature_ref[part * part_rows : (part + 1) * part_rows, :] = early[part][...]
    unpermute(
        PARTS - 1,
        part_rows,
        back_ref,
        returned_ref,
        feature_ref,
        (PARTS - 1) * part_rows,
        wide_ref,
        buffers,
        sems,
    )

    for lane_block in range(D_IN // LANES):
        for block in range(blocks):
            piece = feature_ref[
                block * LANES : (block + 1) * LANES, lane_block * LANES : (lane_block + 1) * LANES
            ]
            turned_ref[
                lane_block * LANES : (lane_block + 1) * LANES, block * LANES : (block + 1) * LANES
            ] = matmul_nt(eye, piece).astype(BF16)
    dense = dense_ref[...]
    dense_w = dense_w_ref[...]
    turned_ref[EMB_WIDTH:, :] = matmul_tn(dense_w, dense).astype(BF16)

    features = turned_ref[...]
    logits = matmul(gate_ref[...], features)
    for task in range(TASKS):
        part_logits = logits[task * experts : (task + 1) * experts]
        powers = jnp.exp(part_logits - jnp.max(part_logits, axis=0, keepdims=True))
        gates_ref[task * experts : (task + 1) * experts, :] = powers / jnp.sum(
            powers, axis=0, keepdims=True
        )

    mixed_ref[...] = jnp.zeros_like(mixed_ref)

    def column(line):
        tall = jnp.transpose(jnp.broadcast_to(line, (LANES, LANES)))
        return jnp.concatenate([tall] * blocks, axis=1)

    def bias_line(expert, rows):
        lines = [weight_ref[expert, 2 * D_IN + H1 :, :].astype(F32)[row : row + 1] for row in rows]
        return functools.reduce(jnp.add, lines)

    def forward(expert, carry):
        turned = turned_ref[...]
        for half in range(H1 // LANES):
            weights = weight_ref[expert, half * D_IN : (half + 1) * D_IN, :]
            bias = column(bias_line(expert, range(half * 3, half * 3 + 3)))
            value, slope = silu_parts(matmul_tn(weights, turned) + bias)
            hidden_ref[expert, half * LANES : (half + 1) * LANES, :] = value.astype(BF16)
            hidden_slope_ref[expert, half * LANES : (half + 1) * LANES, :] = slope
        weights = weight_ref[expert, 2 * D_IN : 2 * D_IN + H1, :]
        bias = column(bias_line(expert, (6, 7, 8)))
        value, slope = silu_parts(matmul_tn(weights, hidden_ref[expert]) + bias)
        output_ref[expert] = value
        output_slope_ref[expert] = slope
        for task in range(TASKS):
            mixed_ref[task * H2 : (task + 1) * H2, :] += (
                gates_ref[pl.ds(task * experts + expert, 1), :] * value
            )
        return carry

    lax.fori_loop(0, experts, forward, 0, unroll=2)

    tower_bias = column(vector_ref[0:1, :])
    head_w = column(vector_ref[1:2, :])
    tower = tower_ref[...]
    act_sums = []
    grad_sums = []
    head_sums = []
    for task in range(TASKS):
        units = slice(task * TOWER, (task + 1) * TOWER)
        outs = slice(task * H2, (task + 1) * H2)
        mixed = mixed_ref[outs, :]
        mixed_low = mixed.astype(BF16)
        tower_part = tower[:, units]
        act, slope = silu_parts(matmul_tn(tower_part, mixed_low) + tower_bias[units])
        score = jnp.sum(act * head_w[units], axis=0, keepdims=True) + head_b_ref[task]
        target = label_ref[task : task + 1, :].astype(F32)
        score_grad = (jax.nn.sigmoid(score) - target) * scale
        tower_grad = (score_grad * head_w[units] * slope).astype(BF16)
        act_sums.append(jnp.sum(score_grad * act, axis=1, keepdims=True))
        grad_sums.append(jnp.sum(tower_grad.astype(F32), axis=1, keepdims=True))
        head_sums.append(jnp.sum(score_grad, axis=1, keepdims=True))
        put_shared(slice(0, H2), units, matmul_nt(mixed_low, tower_grad))
        mixed_grad = matmul(tower_part, tower_grad).astype(BF16).astype(F32)
        mixed_grad_ref[outs, :] = mixed_grad
        dot_ref[task : task + 1, :] = jnp.sum(mixed_grad * mixed, axis=0, keepdims=True)
    column_sums = jnp.concatenate(
        [
            jnp.broadcast_to(jnp.concatenate(sums, axis=0), (LANES, LANES))
            for sums in (act_sums, grad_sums)
        ],
        axis=1,
    )
    put_shared(slice(H2, H2 + 8), whole, jnp.transpose(column_sums[:, :LANES])[0:8])
    put_shared(slice(H2 + 8, H2 + 16), whole, jnp.transpose(column_sums[:, LANES:])[0:8])
    head_line = jnp.zeros((8, LANES), F32)
    for task in range(TASKS):
        head_line = jnp.where(iota((8, LANES), 1) == task, head_sums[task], head_line)
    put_shared(slice(H2 + 16, H2 + 24), whole, head_line)

    input_ref[...] = jnp.zeros_like(input_ref)
    ones = jnp.ones((BIAS_ROWS, width), BF16)

    def backward(expert, carry):
        value = output_ref[expert]
        grad = jnp.zeros((H2, width), F32)
        for task in range(TASKS):
            mixed_grad = mixed_grad_ref[task * H2 : (task + 1) * H2, :]
            gate = gates_ref[pl.ds(task * experts + expert, 1), :]
            grad = grad + gate * mixed_grad
            along = jnp.sum(mixed_grad * value, axis=0, keepdims=True)
            logit_ref[pl.ds(task * experts + expert, 1), :] = gate * (
                along - dot_ref[task : task + 1, :]
            )
        output_grad = (grad * output_slope_ref[expert]).astype(BF16)
        hidden = hidden_ref[expert]
        put_weight(expert, slice(2 * D_IN, 2 * D_IN + H1), matmul_nt(hidden, output_grad))
        weights = weight_ref[expert, 2 * D_IN : 2 * D_IN + H1, :]
        hidden_grad = (matmul(weights, output_grad) * hidden_slope_ref[expert]).astype(BF16)
        turned = turned_ref[...]
        sums = []
        for half in range(H1 // LANES):
            half_grad = hidden_grad[half * LANES : (half + 1) * LANES]
            put_weight(
                expert, slice(half * D_IN, (half + 1) * D_IN), matmul_nt(turned, half_grad)
            )
            weights = weight_ref[expert, half * D_IN : (half + 1) * D_IN, :]
            input_ref[...] += matmul(weights, half_grad)
            sums.append(matmul_nt(ones, half_grad)[0:1])
        sums.append(matmul_nt(ones, output_grad)[0:1])
        sums.append(jnp.zeros((8 - 3, LANES), F32))
        grad_bias_ref[expert] = jnp.concatenate(sums, axis=0)
        return carry

    lax.fori_loop(0, experts, backward, 0, unroll=2)

    logit_grad = logit_ref[...].astype(BF16)
    gate_grad = matmul_nt(logit_grad, turned_ref[...])
    gate_base = H2 + 24
    pairs = TASKS * experts
    for lane_block in range(D_IN // LANES):
        put_shared(
            slice(gate_base + lane_block * pairs, gate_base + (lane_block + 1) * pairs),
            whole,
            gate_grad[:, lane_block * LANES : (lane_block + 1) * LANES],
        )
    low_ref[...] = (input_ref[...] + matmul_tn(gate_ref[...], logit_grad)).astype(BF16)
    bottom_grad = low_ref[EMB_WIDTH:, :]
    dense_base = gate_base + D_IN // LANES * pairs
    grad_dense_w = jnp.concatenate(
        [matmul_nt(dense, bottom_grad), jnp.zeros((DENSE, LANES - BOTTOM), F32)], axis=1
    )
    put_shared(
        slice(dense_base, dense_base + 16),
        whole,
        jnp.concatenate([grad_dense_w, jnp.zeros((16 - DENSE, LANES), F32)], axis=0),
    )
    grad_dense_ref[...] = matmul(dense_w, bottom_grad)

    def clear(step, carry):
        wide_ref[pl.ds(aligned(8 + step * LANES, 8), LANES), :] = jnp.zeros((LANES, LANES), F32)
        return carry

    chunk_rows = left_ref.shape[0] // FIELDS

    def permute(chunk, words):
        block = lax.div(chunk * chunk_rows, LANES)
        first = chunk * chunk_rows - block * LANES
        span = pl.ds(aligned(block * LANES, LANES), LANES)

        @pl.when(first == 0)
        def _():
            for field in range(FIELDS):
                piece = low_ref[field * EMB : (field + 1) * EMB, span]
                tiled_ref[field] = matmul_nt(eye, jnp.concatenate([piece] * GROUPS, axis=0))

        for step in range(chunk_rows // 8):
            start_row = aligned(first + step * 8, 8)
            for field in range(FIELDS):
                tile = tiled_ref[field, pl.ds(start_row, 8), :]
                for k in range(8):
                    start = words[(step * 8 + k) * FIELDS + field]
                    pltpu.store(wide_ref.at[pl.ds(start, 8), :], tile, mask=lines[k])

    def permute_place(at):
        each = part_rows // chunk_rows
        part = lax.div(at, each)
        return part * (out_ref.shape[0] // PARTS) + (at - part * each) * (chunk_rows * FIELDS)

    word_stream(
        out_ref,
        buffers,
        sems,
        permute_place,
        width // chunk_rows,
        permute,
        lambda: lax.fori_loop(0, slot_blocks, clear, 0, unroll=2),
    )

    def merge(block, carry):
        halves = []
        for half in range(2):
            piece = jnp.zeros((8, LANES), F32)
            for group in range(GROUPS):
                start = aligned(block * LANES + group * 16 + (half + 1) * 8, 8)
                piece = jnp.where(lanes[group], wide_ref[pl.ds(start, 8), :], piece)
            halves.append(piece)
        start = aligned(block * 16, 16)
        sent_ref[pl.ds(start, 16), :] = jnp.concatenate(halves, axis=0).astype(BF16)
        return carry

    lax.fori_loop(0, slot_blocks, merge, 0, unroll=4 if slot_blocks % 4 == 0 else 1)
    each = sent_ref.shape[0] // owners
    for one, held in enumerate(order):
        sent_refs[one][...] = sent_ref[held * each : (held + 1) * each, :]


def add_kernel(order, packed, table_lanes, index_ref, request_ref, asked_ref, *refs):
    owners = len(order)
    received_refs = refs[:owners]
    table_refs = refs[owners : owners + 2 * TABLE_CHUNKS]
    (
        received_ref,
        left_grad_ref,
        right_grad_ref,
        left_ref,
        right_ref,
        sems,
        *sums,
    ) = refs[owners + 2 * TABLE_CHUNKS :]
    rows = sums[0].shape[0] - 16
    core, batch = index_ref[0], index_ref[1]
    sources = received_ref.shape[0] // packed
    chunks = packed // 16
    lines, _ = masks()
    eye = identity()
    own_group = lax.shift_right_logical(iota((1, LANES), 1), 4)
    from_lane = iota((LANES, 2 * LANES), 0)
    to_lane = iota((LANES, 2 * LANES), 1)
    spread_names = []
    spread_grads = []
    for pair in range(GROUPS // 2):
        group = pair * 2 + lax.shift_right_logical(to_lane, 7)
        spread_names.append(
            jnp.where(lax.shift_right_logical(from_lane, 4) == group, 1.0, 0.0).astype(BF16)
        )
        wanted = group * EMB + (to_lane & (EMB - 1))
        spread_grads.append(jnp.where(from_lane == wanted, 1.0, 0.0).astype(BF16))

    def place(source):
        distance = lax.div(source, PARTS)
        return (distance ^ batch) * PARTS + source - distance * PARTS

    def spread(source, grad_ref):
        def step(first, count, pair):
            asked = asked_ref[pl.ds(place(source) * chunks + first, count), :]
            names = (own_group - lax.shift_right_logical(asked, table_lanes)) & (GROUPS - 1)
            start = aligned(source * packed + first * 16, 16)
            grads = received_ref[pl.ds(start, count * 16), :]
            lane_group = lax.shift_right_logical(iota((count * 16, LANES), 1), 4).astype(F32)
            wide_names = matmul(slot_lines(names.astype(F32)), spread_names[pair])
            wide_grads = matmul(grads, spread_grads[pair])
            for side in range(2):
                half = slice(side * LANES, (side + 1) * LANES)
                masked = jnp.where(wide_names[:, half] == lane_group, wide_grads[:, half], 0.0)
                for chunk in range(count):
                    start = (first + chunk) * LANES + (pair * 2 + side) * 16
                    grad_ref[start : start + 16, :] = masked[chunk * 16 : (chunk + 1) * 16]

        return [
            functools.partial(step, first, min(4, chunks - first), pair)
            for first in range(0, chunks, 4)
            for pair in range(GROUPS // 2)
        ]

    def clear(step, carry):
        for total in sums:
            total[pl.ds(aligned(8 + step * LANES, 8), LANES), :] = jnp.zeros((LANES, LANES), F32)
        return carry

    def before():
        for total in sums:
            total[0:8, :] = jnp.zeros((8, LANES), F32)
            total[8 + rows : 16 + rows, :] = jnp.zeros((8, LANES), F32)
        lax.fori_loop(0, rows // LANES, clear, 0)
        gather_blocks(order, received_refs, received_ref)
        for one in spread(0, left_grad_ref):
            one()

    def process(source, words):
        now, later = left_grad_ref, right_grad_ref
        if words is right_ref:
            now, later = later, now
        steps = spread(jnp.minimum(source + 1, sources - 1), later)
        rows = GROUPS * packed // 8
        for row in range(rows):
            if row * len(steps) // rows != (row - 1) * len(steps) // rows:
                steps[row * len(steps) // rows]()
            grads = now[row * 8 : (row + 1) * 8, :]
            for k in range(8):
                place = pl.ds(words[row * 8 + k], 8)
                total = sums[k % STREAMS]
                pltpu.store(total.at[place, :], total[place, :] + grads, mask=lines[k])

    size = GROUPS * packed
    word_stream(
        request_ref,
        (left_ref, right_ref),
        sems,
        lambda at: place(at) * size,
        sources,
        process,
        before,
    )

    def finish(kept, block, carry):
        start = aligned(8 + block * LANES, 8)
        total = functools.reduce(jnp.add, [one[pl.ds(start, LANES), :] for one in sums])
        turned = matmul_nt(eye, total.astype(BF16)).astype(BF16)
        each = GROUPS // (2 * TABLE_CHUNKS)
        for group in range(GROUPS):
            half, column = divmod(group, GROUPS // 2)
            chunk, column = divmod(column, each)
            table_ref = table_refs[chunk + (0 if half == kept else TABLE_CHUNKS)]
            column = aligned(column * rows + block * LANES, LANES)
            table_ref[:, pl.ds(column, LANES)] = turned[group * EMB : (group + 1) * EMB]
        return carry

    for kept in range(2):

        @pl.when(core == kept)
        def _():
            lax.fori_loop(0, rows // LANES, functools.partial(finish, kept), 0, unroll=8)


def unpack_kernel(weight_piece, extra_piece, pairs, piece_ref, *refs):
    (
        dense_w_ref,
        gate_ref,
        hidden_w_ref,
        hidden_b_ref,
        output_w_ref,
        output_b_ref,
        tower_w_ref,
        tower_b_ref,
        head_w_ref,
        head_b_ref,
        weight_ref,
        extra_ref,
    ) = refs
    for owner in range(piece_ref.shape[0]):
        weight_ref[owner * weight_piece : (owner + 1) * weight_piece, :] = piece_ref[
            owner, :weight_piece, :
        ].astype(F32)
        high = piece_ref[owner, weight_piece : weight_piece + extra_piece, :].astype(F32)
        low = piece_ref[owner, weight_piece + extra_piece :, :].astype(F32)
        extra_ref[owner * extra_piece : (owner + 1) * extra_piece, :] = high + low
    gate_rows = D_IN // LANES * pairs
    small = H2 + gate_rows + 16

    def small_line(row):
        return extra_ref[small + row : small + row + 1, :] + extra_ref[small + 6 + row : small + 7 + row, :]

    for half in range(H1 // LANES):
        span = slice(half * LANES, (half + 1) * LANES)
        hidden_w_ref[0, :, span] = weight_ref[half * D_IN : (half + 1) * D_IN, :]
        hidden_b_ref[:, span] = small_line(3 + half)
    output_w_ref[0] = weight_ref[2 * D_IN : GRAD_ROWS, :]
    output_b_ref[...] = small_line(5)
    tower_w_ref[...] = extra_ref[:H2, :]
    head_w_ref[...] = small_line(0)
    tower_b_ref[...] = small_line(1)
    head_b_ref[...] = small_line(2)[:, :TASKS]
    for block in range(D_IN // LANES):
        gate_ref[:, block * LANES : (block + 1) * LANES] = extra_ref[
            H2 + block * pairs : H2 + (block + 1) * pairs, :
        ]
    dense_w_ref[...] = extra_ref[H2 + gate_rows : H2 + gate_rows + DENSE, :BOTTOM]


SMEM = pl.BlockSpec(memory_space=pltpu.SMEM)
VMEM = pl.BlockSpec(memory_space=pltpu.VMEM)
ANY = pl.BlockSpec(memory_space=pl.ANY)


def call(kernel, outs, ins, scratch, name, micros, vmem=16):
    return pl.pallas_call(
        kernel,
        out_shape=outs,
        in_specs=ins,
        out_specs=jax.tree.map(lambda _: VMEM, outs),
        scratch_shapes=scratch,
        name=name,
        cost_estimate=pl.CostEstimate(
            flops=int(micros * 1.15e9), bytes_accessed=int(micros * 3e6), transcendentals=0
        ),
        compiler_params=pltpu.CompilerParams(vmem_limit_bytes=vmem << 20),
    )


def shards(
    emb_table,
    dense_feats,
    dense_w,
    gate_w,
    hidden_w,
    hidden_b,
    output_w,
    output_b,
    tower_w,
    tower_b,
    head_w,
    head_b,
    row_owner,
    local_row,
    labels,
):
    owners = lax.axis_size("batch")
    experts = lax.axis_size("expert")
    expert_index = lax.axis_index("expert")
    core = expert_index & 1
    row_total = dense_feats.shape[1]
    part_rows = row_total // PARTS
    lookups = row_total * FIELDS
    part_lookups = lookups // PARTS
    capacity = 2 * part_lookups // owners
    packed = -(-capacity // (GROUPS * 16)) * 16
    table_rows = emb_table.shape[0]
    table_packed = table_rows // GROUPS
    table_lanes = table_packed.bit_length() - 1
    scale = 1.0 / math.sqrt(row_total * owners * experts)
    slots = owners * PARTS * GROUPS * packed
    part_slots = owners * packed
    lookup_rows = lookups // LANES
    list_part = -(-lookup_rows // (PARTS * 24)) * 24
    list_rows = list_part * PARTS

    def tie(*values):
        return lax.optimization_barrier(values)

    def exchange(values, axis):
        return lax.all_to_all(values, axis, split_axis=0, concat_axis=0, tiled=True)

    def swap(values, axis, bits):
        size = lax.axis_size(axis)
        return lax.ppermute(values, axis, [(one, one ^ bits) for one in range(size)])

    order = sorted(range(owners), key=lambda bits: (-bits.bit_length(), bits))

    owner_list = row_owner.reshape(lookup_rows, LANES)
    local_list = local_row.reshape(lookup_rows, LANES)
    slot_rows = slots // LANES
    list_shape = jax.ShapeDtypeStruct((list_rows, LANES), I32)
    batch_index = lax.axis_index("batch").reshape(1)
    requests, back, out = call(
        functools.partial(route_kernel, owners, part_lookups, packed, table_lanes),
        (jax.ShapeDtypeStruct((slot_rows, LANES), I32), list_shape, list_shape),
        [SMEM, VMEM, VMEM],
        [pltpu.VMEM((list_rows, LANES), I32)] * 3 + [pltpu.VMEM((PARTS, slot_rows // PARTS, 2 * LANES), F32)],
        "route",
        9,
    )(batch_index, owner_list, local_list)
    asked = exchange(requests.reshape(owners, slots // owners), "batch")
    asked = asked.reshape(slot_rows, LANES)
    offset = 8 - (jnp.arange(LANES, dtype=I32) & 7)
    words = ((asked & (table_packed - 1)) + offset).reshape(-1)
    back = back.reshape(-1)
    out = out.reshape(-1)

    hidden_b, out = tie(hidden_b, out)
    table, weights = call(
        pack_kernel,
        (
            jax.ShapeDtypeStruct((table_packed + 16, LANES), F32),
            jax.ShapeDtypeStruct((WEIGHT_ROWS, LANES), BF16),
        ),
        [VMEM] * 5,
        [],
        "pack",
        5,
    )(emb_table.T, hidden_w, output_w, hidden_b, output_b)
    weights = lax.all_gather(weights, "expert", axis=0, tiled=False)

    slot_words = [pltpu.SMEM((GROUPS * packed,), I32)] * 2 + [pltpu.SemaphoreType.DMA((2,))]
    row_words = [pltpu.SMEM((CHUNK_ROWS * FIELDS,), I32)] * 2 + [pltpu.SemaphoreType.DMA((2,))]
    returned = []
    for part in range(PARTS):
        found = call(
            functools.partial(fetch_kernel, owners, part, packed, table_lanes),
            jax.ShapeDtypeStruct((part_slots, LANES), BF16),
            [ANY, VMEM, ANY],
            [
                pltpu.VMEM((table_packed + 16, LANES), F32),
                pltpu.VMEM((part_slots, LANES), F32),
                pltpu.VMEM((GROUPS * packed, LANES), F32),
            ]
            + slot_words
            + [pltpu.SemaphoreType.DMA],
            "fetch",
            24 // PARTS,
        )(words, asked, table)
        found = exchange(found.reshape(owners, packed, LANES), "batch")
        returned.append(found.reshape(part_slots, LANES))
    early = []
    for part in range(PARTS - 1):
        early.append(
            call(
                functools.partial(unpermute_kernel, part, part_rows),
                jax.ShapeDtypeStruct((part_rows, D_IN), BF16),
                [ANY, VMEM],
                [pltpu.VMEM((GROUPS * part_slots + 16, LANES), F32), *row_words],
                "unpermute",
                15,
            )(back, returned[part])
        )

    pairs = TASKS * experts
    shared_rows = H2 + 24 + D_IN // LANES * pairs + 16
    vectors = jnp.stack([tower_b, head_w])
    *sent, grad_dense, grad_weight, grad_bias, grad_shared = call(
        functools.partial(dense_kernel, order, part_rows, experts, scale),
        (
            *[jax.ShapeDtypeStruct((PARTS * packed, LANES), BF16)] * owners,
            jax.ShapeDtypeStruct((DENSE, row_total), F32),
            jax.ShapeDtypeStruct((experts, GRAD_ROWS, LANES), BF16),
            jax.ShapeDtypeStruct((experts, 8, LANES), F32),
            jax.ShapeDtypeStruct((shared_rows, LANES), F32),
        ),
        [ANY, ANY] + [VMEM] * 7 + [SMEM] + [VMEM] * PARTS,
        [
            pltpu.VMEM((slots + 16, LANES), F32),
            pltpu.VMEM((row_total, D_IN), BF16),
            pltpu.VMEM((D_IN, row_total), BF16),
            pltpu.VMEM((experts, H1, row_total), BF16),
            pltpu.VMEM((experts, H1, row_total), F32),
            pltpu.VMEM((experts, H2, row_total), F32),
            pltpu.VMEM((experts, H2, row_total), F32),
            pltpu.VMEM((pairs, row_total), F32),
            pltpu.VMEM((TASKS * H2, row_total), F32),
            pltpu.VMEM((TASKS * H2, row_total), F32),
            pltpu.VMEM((8, row_total), F32),
            pltpu.VMEM((pairs, row_total), F32),
            pltpu.VMEM((D_IN, row_total), F32),
            pltpu.VMEM((D_IN, row_total), BF16),
            pltpu.VMEM((FIELDS, LANES, LANES), F32),
            *row_words,
            pltpu.VMEM((PARTS * part_slots, LANES), BF16),
        ],
        "dense",
        45,
        56,
    )(
        back,
        out,
        returned[-1],
        weights,
        gate_w.T,
        dense_feats,
        dense_w,
        tower_w,
        vectors,
        head_b,
        labels,
        *early,
    )
    received = [swap(one, "batch", bits) if bits else one for bits, one in zip(order, sent)]

    def split(values):
        high = lax.reduce_precision(values, exponent_bits=8, mantissa_bits=7)
        return high.astype(BF16), (values - high).astype(BF16)

    near = owners - 2
    received[near], grad_weight, grad_bias, grad_shared = tie(
        received[near], grad_weight, grad_bias, grad_shared
    )

    def spread_rows(values, piece):
        rows = values.shape[1]
        values = jnp.pad(values, ((0, 0), (0, piece * owners - rows), (0, 0)))
        return values.reshape(experts, owners, piece, LANES).transpose(1, 0, 2, 3)

    large = jnp.concatenate([grad_shared[:H2], grad_shared[H2 + 24 :]], axis=0).astype(BF16)
    small = jnp.concatenate([grad_shared[H2 + 8 * row : H2 + 8 * row + 1] for row in range(3)])
    small = jnp.concatenate(
        [jnp.broadcast_to(small[None], (experts, 3, LANES)), grad_bias[:, :3]], axis=1
    )
    extra = jnp.concatenate(
        [jnp.broadcast_to(large[None], (experts, *large.shape)), *split(small)], axis=1
    )
    weight_piece = -(-GRAD_ROWS // (16 * owners)) * 16
    extra_piece = -(-extra.shape[1] // (16 * owners)) * 16
    piece_rows = weight_piece + extra_piece
    pieces = jnp.concatenate(
        [spread_rows(grad_weight, weight_piece), spread_rows(extra, extra_piece)], axis=2
    )
    *received[2:], pieces = tie(*received[2:], pieces)
    pieces = exchange(pieces.reshape(owners * experts, piece_rows, LANES), ("batch", "expert"))

    columns = table_rows // 2 // TABLE_CHUNKS
    table_part = call(
        functools.partial(add_kernel, order, packed, table_lanes),
        (jax.ShapeDtypeStruct((EMB, columns), BF16),) * (2 * TABLE_CHUNKS),
        [SMEM, ANY, VMEM] + [VMEM] * owners,
        [pltpu.VMEM((PARTS * part_slots, LANES), BF16)]
        + [pltpu.VMEM((GROUPS * packed, LANES), F32)] * 2
        + slot_words
        + [pltpu.VMEM((table_packed + 16, LANES), F32)] * STREAMS,
        "add",
        60,
        48,
    )(jnp.concatenate([core.reshape(1), batch_index]), words, asked, *received)

    def add_low(left, right):
        return (left.astype(F32) + right.astype(F32)).astype(BF16)

    *table_part, pieces = tie(*table_part, pieces)
    kept = [
        add_low(one, swap(other, "expert", 1))
        for one, other in zip(table_part[:TABLE_CHUNKS], table_part[TABLE_CHUNKS:])
    ]
    *kept, pieces = tie(*kept, pieces)
    over = [swap(one, "expert", 2) for one in kept]
    sums = jnp.sum(pieces.astype(F32), axis=0)
    piece = jnp.concatenate([sums[:weight_piece].astype(BF16), *split(sums[weight_piece:])], axis=0)
    pieces = exchange(jnp.broadcast_to(piece[None], (owners, *piece.shape)), "batch")
    bit = 2
    while bit < experts:
        kept = [add_low(one, other) for one, other in zip(kept, over)]
        bit *= 2
        if bit < experts:
            over = [swap(one, "expert", bit) for one in kept]
    small = call(
        functools.partial(unpack_kernel, weight_piece, extra_piece, pairs),
        tuple(
            jax.ShapeDtypeStruct(shape, F32)
            for shape in (
                (DENSE, BOTTOM),
                (pairs, D_IN),
                (1, D_IN, H1),
                (1, H1),
                (1, H1, H2),
                (1, H2),
                (H2, TASKS * TOWER),
                (1, TASKS * TOWER),
                (1, TASKS * TOWER),
                (1, TASKS),
            )
        ),
        [VMEM],
        [
            pltpu.VMEM((owners * weight_piece, LANES), F32),
            pltpu.VMEM((owners * extra_piece, LANES), F32),
        ],
        "unpack",
        3,
    )(pieces)
    others = [swap(one, "expert", 1) for one in kept]
    *others, small = tie(*others, small)
    lower = [jnp.where(core == 0, one, other) for one, other in zip(kept, others)]
    upper = [jnp.where(core == 0, other, one) for one, other in zip(kept, others)]
    table_total = jnp.concatenate(lower + upper, axis=1).astype(F32).T
    grad_dense_w, gate, hidden, hidden_bias, output, output_bias, tower, tower_bias, head, head_bias = (
        small
    )
    return (
        table_total,
        grad_dense,
        grad_dense_w,
        gate.T,
        hidden,
        hidden_bias,
        output,
        output_bias,
        tower,
        tower_bias.reshape(-1),
        head.reshape(-1),
        head_bias.reshape(-1),
    )


def solution(mesh):
    in_specs = (
        P("batch", None),
        P(None, ("batch", "expert")),
        P(),
        P(),
        P("expert", None, None),
        P("expert", None),
        P("expert", None, None),
        P("expert", None),
        P(),
        P(),
        P(),
        P(),
        P(("batch", "expert"), None),
        P(("batch", "expert")),
        P(None, ("batch", "expert")),
    )
    out_specs = (
        P("batch", None),
        P(None, ("batch", "expert")),
        P(),
        P(),
        P("expert", None, None),
        P("expert", None),
        P("expert", None, None),
        P("expert", None),
        P(),
        P(),
        P(),
        P(),
    )
    return jax.shard_map(shards, mesh=mesh, in_specs=in_specs, out_specs=out_specs, check_vma=False)
```

```python
import functools
import math

import jax
import jax.numpy as jnp
from jax import lax
from jax.experimental import pallas as pl
from jax.experimental.pallas import tpu as pltpu
from jax.sharding import PartitionSpec as P

FIELDS = 26
EMB = 16
DENSE = 13
BOTTOM = 96
D_IN = 512
H1 = 256
H2 = 128
TOWER = 64
TASKS = 2
LANES = 128
GROUPS = LANES // EMB
EMB_WIDTH = FIELDS * EMB
BIAS_ROWS = 16
GRAD_ROWS = 2 * D_IN + H1
WEIGHT_ROWS = GRAD_ROWS + BIAS_ROWS
STREAMS = 8
PARTS = 2
CHUNK_ROWS = 64
TABLE_CHUNKS = 2

F32 = jnp.float32
BF16 = jnp.bfloat16
I32 = jnp.int32


def iota(shape, axis):
    return lax.broadcasted_iota(I32, shape, axis)


def matmul(a, b):
    return lax.dot_general(a, b, (((1,), (0,)), ((), ())), preferred_element_type=F32)


def matmul_nt(a, b):
    return lax.dot_general(a, b, (((1,), (1,)), ((), ())), preferred_element_type=F32)


def matmul_tn(a, b):
    return lax.dot_general(a, b, (((0,), (0,)), ((), ())), preferred_element_type=F32)


def identity():
    return (iota((LANES, LANES), 0) == iota((LANES, LANES), 1)).astype(BF16)


def aligned(value, step):
    return pl.multiple_of(value, step)


def silu_parts(values):
    sig = jax.nn.sigmoid(values)
    return values * sig, sig * (1.0 + values * (1.0 - sig))


def route_kernel(
    owners, part_lookups, packed, table_lanes, batch_ref, owner_ref, local_ref, request_ref,
    back_ref, out_ref, high_ref, low_ref, value_ref, total_ref
):
    rows = high_ref.shape[0]
    part_rows = rows // PARTS
    filled = part_lookups // LANES
    slot_rows = request_ref.shape[0]
    shape = (rows, LANES)
    high_ref[...] = jnp.full(shape, -1, I32)
    low_ref[...] = jnp.zeros(shape, I32)
    for part in range(PARTS):
        lines = slice(part * part_rows, part * part_rows + filled)
        taken = slice(part * filled, (part + 1) * filled)
        high_ref[lines, :] = owner_ref[taken, :]
        low_ref[lines, :] = local_ref[taken, :]
    owner = high_ref[...]
    local = low_ref[...]
    row_id = iota(shape, 0)
    tri = (iota((LANES, LANES), 0) <= iota((LANES, LANES), 1)).astype(BF16)
    ones = jnp.ones((LANES, LANES), BF16)
    before = (iota((part_rows, part_rows), 1) < iota((part_rows, part_rows), 0)).astype(BF16)
    ranks = []
    for part in range(PARTS):
        own = owner[part * part_rows : (part + 1) * part_rows]
        rank = jnp.zeros((part_rows, LANES), F32)
        for one in range(owners):
            hit = own == one
            hits = jnp.where(hit, 1.0, 0.0).astype(BF16)
            upto = matmul(hits, tri)
            ahead = matmul(before, matmul(hits, ones).astype(BF16))
            rank = jnp.where(hit, upto + ahead - 1.0, rank)
        ranks.append(rank)
    rank = jnp.concatenate(ranks, axis=0)
    part_id = jnp.zeros(shape, I32)
    for part in range(1, PARTS):
        part_id = part_id + jnp.where(row_id >= part * part_rows, 1, 0)
    rank = rank.astype(I32)
    group = jnp.zeros(shape, I32)
    for step in range(1, GROUPS):
        group = group + jnp.where(rank >= step * packed, 1, 0)
    place = rank - group * packed
    held = jnp.maximum(owner, 0)
    chunks = packed // 16
    chunk = lax.shift_right_logical(place, 4)
    block = (held * PARTS + part_id) * chunks + chunk
    inside = group * 16 + (place & 15)
    table_group = lax.shift_right_logical(local, table_lanes)
    table_row = local & ((1 << table_lanes) - 1)
    high_ref[...] = jnp.where(owner < 0, -1, held * chunks + chunk)
    low_ref[...] = inside
    value_ref[...] = table_row + (((group - table_group) & (GROUPS - 1)) << table_lanes)
    lookup = (row_id - part_id * part_rows) * LANES + iota(shape, 1)
    quotient = jnp.floor((lookup.astype(F32) + 0.5) * (1.0 / FIELDS)).astype(I32)
    field_group = (lookup - quotient * FIELDS) & (GROUPS - 1)
    offset = 8 - (quotient & 7)
    turn = (field_group - group) & (GROUPS - 1)
    back_ref[...] = (turn * owners + held) * packed + place + offset
    away = ((held ^ batch_ref[0]) - held) * (PARTS * GROUPS * packed)
    out_ref[...] = block * LANES + inside + offset + away
    total_ref[...] = jnp.zeros_like(total_ref)
    own_rows = slot_rows // PARTS

    def gather_requests(part, step, carry):
        base = aligned(part * part_rows + step * 8, 8)
        high = high_ref[pl.ds(base, 8), :]
        low = low_ref[pl.ds(base, 8), :]
        values = value_ref[pl.ds(base, 8), :]
        upper = lax.shift_right_logical(values, 8).astype(F32)
        lower = (values & 255).astype(F32)
        at_high = []
        at_low = []
        for k in range(8):
            line = slice(k, k + 1)
            at_high.append(jnp.where(iota((own_rows, LANES), 0) == high[line], 1.0, 0.0).astype(BF16))
            same = iota((LANES, LANES), 0) == low[line]
            at_low.append(
                jnp.concatenate(
                    [jnp.where(same, upper[line], 0.0), jnp.where(same, lower[line], 0.0)], axis=0
                ).astype(BF16)
            )
        total_ref[part] += matmul_nt(
            jnp.concatenate(at_high, axis=1), jnp.concatenate(at_low, axis=1)
        )
        return carry

    for part in range(PARTS):
        lax.fori_loop(0, part_rows // 8, functools.partial(gather_requests, part), 0, unroll=3)
        total = (total_ref[part, :, :LANES] * 256.0 + total_ref[part, :, LANES:]).astype(I32)
        for one in range(owners):
            start = (one * PARTS + part) * chunks
            request_ref[start : start + chunks, :] = total[one * chunks : (one + 1) * chunks]


def pack_kernel(
    table_ref, hidden_w_ref, output_w_ref, hidden_b_ref, output_b_ref, packed_ref, weight_ref
):
    lines = []
    for values in (hidden_b_ref[:, :LANES], hidden_b_ref[:, LANES:], output_b_ref[...]):
        for _ in range(3):
            term = values.astype(BF16).astype(F32)
            lines.append(term)
            values = values - term
    lines.append(jnp.zeros((BIAS_ROWS - len(lines), LANES), F32))
    for half in range(H1 // LANES):
        weight_ref[half * D_IN : (half + 1) * D_IN, :] = hidden_w_ref[
            0, :, half * LANES : (half + 1) * LANES
        ]
    weight_ref[2 * D_IN : 2 * D_IN + H1, :] = output_w_ref[0]
    weight_ref[2 * D_IN + H1 :, :] = jnp.concatenate(lines, axis=0).astype(BF16)
    rows = table_ref.shape[1] // GROUPS
    eye = identity()

    def step(block, carry):
        pieces = []
        for group in range(GROUPS):
            start = aligned(group * rows + block * LANES, LANES)
            pieces.append(table_ref[:, pl.ds(start, LANES)])
        packed_ref[pl.ds(aligned(8 + block * LANES, 8), LANES), :] = matmul_nt(
            eye, jnp.concatenate(pieces, axis=0)
        )
        return carry

    packed_ref[0:8, :] = jnp.zeros((8, LANES), F32)
    packed_ref[8 + rows : 16 + rows, :] = jnp.zeros((8, LANES), F32)

    lax.fori_loop(0, rows // LANES, step, 0, unroll=8)


def masks():
    line = iota((8, LANES), 0)
    group = lax.shift_right_logical(iota((8, LANES), 1), 4)
    return [line == k for k in range(8)], [group == one for one in range(GROUPS)]


def turn_copies(rows_ref, wide_ref):
    rows = rows_ref.shape[0]
    half = GROUPS // 2
    from_lane = iota((LANES, half * LANES), 0)
    to_lane = iota((LANES, half * LANES), 1)
    turn = (lax.shift_right_logical(to_lane, 7) + half) * EMB
    turns = jnp.where(((from_lane + turn - to_lane) & (LANES - 1)) == 0, 1.0, 0.0).astype(BF16)

    def step(block, carry):
        start = aligned(block * LANES, LANES)
        piece = rows_ref[pl.ds(start, LANES), :]
        moved = matmul(piece, turns)
        piece = piece.astype(F32)
        for turn in range(GROUPS):
            if turn >= half:
                one = moved[:, (turn - half) * LANES : (turn - half + 1) * LANES]
            else:
                one = pltpu.roll(piece, turn * EMB, 1) if turn else piece
            wide_ref[pl.ds(aligned(8 + turn * rows + start, 8), LANES), :] = one
        return carry

    blocks = rows // LANES
    unroll = [count for count in (4, 3, 2, 1) if blocks % count == 0][0]
    lax.fori_loop(0, blocks, step, 0, unroll=unroll)


def assemble(wide_ref, word, groups, lines, lanes):
    block = jnp.zeros((8, LANES), F32)
    for place, group in groups:
        piece = wide_ref[pl.ds(word(0, place), 8), :]
        for k in range(1, 8):
            piece = jnp.where(lines[k], wide_ref[pl.ds(word(k, place), 8), :], piece)
        block = jnp.where(lanes[group], piece, block)
    return block


def word_stream(word_ref, buffers, sems, place, count, process, before=None):
    slots = len(buffers)
    size = buffers[0].shape[0]

    def copy(at, slot):
        start = aligned(place(at), LANES)
        return pltpu.make_async_copy(
            word_ref.at[pl.ds(start, size)], buffers[slot], sems.at[slot]
        )

    for slot in range(min(slots, count)):
        copy(slot, slot).start()
    if before is not None:
        before()

    def step(turn, carry):
        for slot in range(slots):
            at = turn * slots + slot
            copy(at, slot).wait()
            process(at, buffers[slot])

            @pl.when(at + slots < count)
            def _():
                copy(at + slots, slot).start()

        return carry

    lax.fori_loop(0, count // slots, step, 0)
    for slot in range(count % slots):
        at = count // slots * slots + slot
        copy(at, slot).wait()
        process(at, buffers[slot])


def slot_lines(numbers):
    own = (iota((16, LANES), 1) & 15) == iota((16, LANES), 0)
    return jnp.concatenate(
        [jnp.where(own, numbers[row : row + 1], 0.0) for row in range(numbers.shape[0])], axis=0
    ).astype(BF16)


def same_group():
    return (
        lax.shift_right_logical(iota((LANES, LANES), 0), 4)
        == lax.shift_right_logical(iota((LANES, LANES), 1), 4)
    ).astype(BF16)


def fetch_kernel(
    owners, part, packed, table_lanes, request_ref, asked_ref, far_table_ref, found_ref, table_ref,
    turn_ref, piece_ref, left_ref, right_ref, sems, table_sem
):
    table_copy = pltpu.make_async_copy(far_table_ref, table_ref, table_sem)
    table_copy.start()
    lines, _ = masks()
    chunks = packed // 16
    within = same_group()
    group = lax.shift_right_logical(iota((8, LANES), 1), 4)
    bits = [(group & (1 << bit)) != 0 for bit in range(3)]

    def turn_step(source, carry):
        at = (source * PARTS + part) * chunks
        numbers = lax.shift_right_logical(asked_ref[pl.ds(at, chunks), :], table_lanes)
        turn_ref[pl.ds(aligned(source * packed, 16), packed), :] = matmul(
            slot_lines(numbers.astype(F32)), within
        )
        return carry

    def before():
        lax.fori_loop(0, owners, turn_step, 0, unroll=4)
        table_copy.wait()

    def process(source, words):
        for chunk in range(chunks):
            for line in range(LANES):
                base = chunk * LANES + line // 8 * 8
                pltpu.store(
                    piece_ref.at[base : base + 8, :],
                    table_ref[pl.ds(words[chunk * LANES + line], 8), :],
                    mask=lines[line % 8],
                )
            start = aligned(source * packed + chunk * 16, 16)
            turns = turn_ref[pl.ds(start, 16), :]
            halves = []
            for half in range(2):
                mixed = []
                for group in range(GROUPS):
                    base = chunk * LANES + group * 16 + half * 8
                    mixed.append(piece_ref[base : base + 8, :])
                for bit in range(3):
                    mixed = [
                        jnp.where(bits[bit], mixed[(turn + (1 << bit)) % GROUPS], mixed[turn])
                        for turn in range(GROUPS)
                    ]
                wanted = turns[half * 8 : (half + 1) * 8]
                block = mixed[0]
                for turn in range(1, GROUPS):
                    moved = pltpu.roll(mixed[turn], turn * EMB, 1)
                    block = jnp.where(wanted == float(turn), moved, block)
                halves.append(block)
            found_ref[pl.ds(start, 16), :] = jnp.concatenate(halves, axis=0).astype(BF16)

    size = chunks * LANES
    word_stream(
        request_ref,
        (left_ref, right_ref),
        sems,
        lambda at: (at * PARTS + part) * size,
        owners,
        process,
        before,
    )


def unpermute(
    part, part_rows, back_ref, returned_ref, feature_ref, first_row, wide_ref, buffers, sems
):
    lines, lanes = masks()
    size = buffers[0].shape[0]
    chunk_rows = size // FIELDS

    def process(chunk, words):
        for block in range(chunk_rows // 16):
            start_row = aligned(first_row + chunk * chunk_rows + block * 16, 16)
            for lane_block in range(D_IN // LANES):
                fields = range(lane_block * GROUPS, min((lane_block + 1) * GROUPS, FIELDS))
                halves = [
                    assemble(
                        wide_ref,
                        lambda k, field, half=half: words[
                            (block * 16 + half * 8 + k) * FIELDS + field
                        ],
                        [(field, field % GROUPS) for field in fields],
                        lines,
                        lanes,
                    )
                    for half in range(2)
                ]
                feature_ref[
                    pl.ds(start_row, 16), lane_block * LANES : (lane_block + 1) * LANES
                ] = jnp.concatenate(halves, axis=0).astype(BF16)

    first = part * back_ref.shape[0] // PARTS
    word_stream(
        back_ref,
        buffers,
        sems,
        lambda at: first + at * size,
        part_rows // chunk_rows,
        process,
        lambda: turn_copies(returned_ref, wide_ref),
    )


def gather_blocks(block_refs, whole_ref):
    rows = block_refs[0].shape[0]
    for one, block_ref in enumerate(block_refs):
        whole_ref[one * rows : (one + 1) * rows, :] = block_ref[...]


def unpermute_kernel(
    part, part_rows, back_ref, returned_ref, feature_ref, wide_ref, left_ref, right_ref, sems
):
    unpermute(
        part,
        part_rows,
        back_ref,
        returned_ref,
        feature_ref,
        0,
        wide_ref,
        (left_ref, right_ref),
        sems,
    )


def dense_kernel(
    owners,
    part_rows,
    experts,
    scale,
    back_ref,
    out_ref,
    returned_ref,
    weight_ref,
    gate_ref,
    dense_ref,
    dense_w_ref,
    tower_ref,
    vector_ref,
    head_b_ref,
    label_ref,
    *refs,
):
    early = refs[: PARTS - 1]
    refs = refs[PARTS - 1 :]
    sent_refs = refs[:owners]
    (
        grad_dense_ref,
        grad_weight_ref,
        grad_bias_ref,
        grad_shared_ref,
        wide_ref,
        feature_ref,
        turned_ref,
        hidden_ref,
        hidden_slope_ref,
        output_ref,
        output_slope_ref,
        gates_ref,
        mixed_ref,
        mixed_grad_ref,
        dot_ref,
        logit_ref,
        input_ref,
        low_ref,
        tiled_ref,
        left_ref,
        right_ref,
        sems,
        sent_ref,
    ) = refs[owners:]
    buffers = (left_ref, right_ref)
    width = turned_ref.shape[1]
    blocks = width // LANES
    slot_blocks = sent_ref.shape[0] // 16
    eye = identity()
    lines, lanes = masks()

    def put_weight(expert, cut, value):
        grad_weight_ref[expert, cut, :] = value.astype(BF16)

    def put_shared(rows, cut, value):
        grad_shared_ref[rows, cut] = value

    whole = slice(None)
    for part in range(PARTS - 1):
        feature_ref[part * part_rows : (part + 1) * part_rows, :] = early[part][...]
    unpermute(
        PARTS - 1,
        part_rows,
        back_ref,
        returned_ref,
        feature_ref,
        (PARTS - 1) * part_rows,
        wide_ref,
        buffers,
        sems,
    )

    for lane_block in range(D_IN // LANES):
        for block in range(blocks):
            piece = feature_ref[
                block * LANES : (block + 1) * LANES, lane_block * LANES : (lane_block + 1) * LANES
            ]
            turned_ref[
                lane_block * LANES : (lane_block + 1) * LANES, block * LANES : (block + 1) * LANES
            ] = matmul_nt(eye, piece).astype(BF16)
    dense = dense_ref[...]
    dense_w = dense_w_ref[...]
    turned_ref[EMB_WIDTH:, :] = matmul_tn(dense_w, dense).astype(BF16)

    features = turned_ref[...]
    logits = matmul(gate_ref[...], features)
    for task in range(TASKS):
        part_logits = logits[task * experts : (task + 1) * experts]
        powers = jnp.exp(part_logits - jnp.max(part_logits, axis=0, keepdims=True))
        gates_ref[task * experts : (task + 1) * experts, :] = powers / jnp.sum(
            powers, axis=0, keepdims=True
        )

    mixed_ref[...] = jnp.zeros_like(mixed_ref)

    def column(line):
        tall = jnp.transpose(jnp.broadcast_to(line, (LANES, LANES)))
        return jnp.concatenate([tall] * blocks, axis=1)

    def bias_line(expert, rows):
        lines = [weight_ref[expert, 2 * D_IN + H1 :, :].astype(F32)[row : row + 1] for row in rows]
        return functools.reduce(jnp.add, lines)

    def forward(expert, carry):
        turned = turned_ref[...]
        for half in range(H1 // LANES):
            weights = weight_ref[expert, half * D_IN : (half + 1) * D_IN, :]
            bias = column(bias_line(expert, range(half * 3, half * 3 + 3)))
            value, slope = silu_parts(matmul_tn(weights, turned) + bias)
            hidden_ref[expert, half * LANES : (half + 1) * LANES, :] = value.astype(BF16)
            hidden_slope_ref[expert, half * LANES : (half + 1) * LANES, :] = slope
        weights = weight_ref[expert, 2 * D_IN : 2 * D_IN + H1, :]
        bias = column(bias_line(expert, (6, 7, 8)))
        value, slope = silu_parts(matmul_tn(weights, hidden_ref[expert]) + bias)
        output_ref[expert] = value
        output_slope_ref[expert] = slope
        for task in range(TASKS):
            mixed_ref[task * H2 : (task + 1) * H2, :] += (
                gates_ref[pl.ds(task * experts + expert, 1), :] * value
            )
        return carry

    lax.fori_loop(0, experts, forward, 0, unroll=2)

    tower_bias = column(vector_ref[0:1, :])
    head_w = column(vector_ref[1:2, :])
    tower = tower_ref[...]
    act_sums = []
    grad_sums = []
    head_sums = []
    for task in range(TASKS):
        units = slice(task * TOWER, (task + 1) * TOWER)
        outs = slice(task * H2, (task + 1) * H2)
        mixed = mixed_ref[outs, :]
        mixed_low = mixed.astype(BF16)
        tower_part = tower[:, units]
        act, slope = silu_parts(matmul_tn(tower_part, mixed_low) + tower_bias[units])
        score = jnp.sum(act * head_w[units], axis=0, keepdims=True) + head_b_ref[task]
        target = label_ref[task : task + 1, :].astype(F32)
        score_grad = (jax.nn.sigmoid(score) - target) * scale
        tower_grad = (score_grad * head_w[units] * slope).astype(BF16)
        act_sums.append(jnp.sum(score_grad * act, axis=1, keepdims=True))
        grad_sums.append(jnp.sum(tower_grad.astype(F32), axis=1, keepdims=True))
        head_sums.append(jnp.sum(score_grad, axis=1, keepdims=True))
        put_shared(slice(0, H2), units, matmul_nt(mixed_low, tower_grad))
        mixed_grad = matmul(tower_part, tower_grad).astype(BF16).astype(F32)
        mixed_grad_ref[outs, :] = mixed_grad
        dot_ref[task : task + 1, :] = jnp.sum(mixed_grad * mixed, axis=0, keepdims=True)
    column_sums = jnp.concatenate(
        [
            jnp.broadcast_to(jnp.concatenate(sums, axis=0), (LANES, LANES))
            for sums in (act_sums, grad_sums)
        ],
        axis=1,
    )
    put_shared(slice(H2, H2 + 8), whole, jnp.transpose(column_sums[:, :LANES])[0:8])
    put_shared(slice(H2 + 8, H2 + 16), whole, jnp.transpose(column_sums[:, LANES:])[0:8])
    head_line = jnp.zeros((8, LANES), F32)
    for task in range(TASKS):
        head_line = jnp.where(iota((8, LANES), 1) == task, head_sums[task], head_line)
    put_shared(slice(H2 + 16, H2 + 24), whole, head_line)

    input_ref[...] = jnp.zeros_like(input_ref)
    ones = jnp.ones((BIAS_ROWS, width), BF16)

    def backward(expert, carry):
        value = output_ref[expert]
        grad = jnp.zeros((H2, width), F32)
        for task in range(TASKS):
            mixed_grad = mixed_grad_ref[task * H2 : (task + 1) * H2, :]
            gate = gates_ref[pl.ds(task * experts + expert, 1), :]
            grad = grad + gate * mixed_grad
            along = jnp.sum(mixed_grad * value, axis=0, keepdims=True)
            logit_ref[pl.ds(task * experts + expert, 1), :] = gate * (
                along - dot_ref[task : task + 1, :]
            )
        output_grad = (grad * output_slope_ref[expert]).astype(BF16)
        hidden = hidden_ref[expert]
        put_weight(expert, slice(2 * D_IN, 2 * D_IN + H1), matmul_nt(hidden, output_grad))
        weights = weight_ref[expert, 2 * D_IN : 2 * D_IN + H1, :]
        hidden_grad = (matmul(weights, output_grad) * hidden_slope_ref[expert]).astype(BF16)
        turned = turned_ref[...]
        sums = []
        for half in range(H1 // LANES):
            half_grad = hidden_grad[half * LANES : (half + 1) * LANES]
            put_weight(
                expert, slice(half * D_IN, (half + 1) * D_IN), matmul_nt(turned, half_grad)
            )
            weights = weight_ref[expert, half * D_IN : (half + 1) * D_IN, :]
            input_ref[...] += matmul(weights, half_grad)
            sums.append(matmul_nt(ones, half_grad)[0:1])
        sums.append(matmul_nt(ones, output_grad)[0:1])
        sums.append(jnp.zeros((8 - 3, LANES), F32))
        grad_bias_ref[expert] = jnp.concatenate(sums, axis=0)
        return carry

    lax.fori_loop(0, experts, backward, 0, unroll=2)

    logit_grad = logit_ref[...].astype(BF16)
    gate_grad = matmul_nt(logit_grad, turned_ref[...])
    gate_base = H2 + 24
    pairs = TASKS * experts
    for lane_block in range(D_IN // LANES):
        put_shared(
            slice(gate_base + lane_block * pairs, gate_base + (lane_block + 1) * pairs),
            whole,
            gate_grad[:, lane_block * LANES : (lane_block + 1) * LANES],
        )
    low_ref[...] = (input_ref[...] + matmul_tn(gate_ref[...], logit_grad)).astype(BF16)
    bottom_grad = low_ref[EMB_WIDTH:, :]
    dense_base = gate_base + D_IN // LANES * pairs
    grad_dense_w = jnp.concatenate(
        [matmul_nt(dense, bottom_grad), jnp.zeros((DENSE, LANES - BOTTOM), F32)], axis=1
    )
    put_shared(
        slice(dense_base, dense_base + 16),
        whole,
        jnp.concatenate([grad_dense_w, jnp.zeros((16 - DENSE, LANES), F32)], axis=0),
    )
    grad_dense_ref[...] = matmul(dense_w, bottom_grad)

    def clear(step, carry):
        wide_ref[pl.ds(aligned(8 + step * LANES, 8), LANES), :] = jnp.zeros((LANES, LANES), F32)
        return carry

    chunk_rows = left_ref.shape[0] // FIELDS

    def permute(chunk, words):
        block = lax.div(chunk * chunk_rows, LANES)
        first = chunk * chunk_rows - block * LANES
        span = pl.ds(aligned(block * LANES, LANES), LANES)

        @pl.when(first == 0)
        def _():
            for field in range(FIELDS):
                piece = low_ref[field * EMB : (field + 1) * EMB, span]
                tiled_ref[field] = matmul_nt(eye, jnp.concatenate([piece] * GROUPS, axis=0))

        for step in range(chunk_rows // 8):
            start_row = aligned(first + step * 8, 8)
            for field in range(FIELDS):
                tile = tiled_ref[field, pl.ds(start_row, 8), :]
                for k in range(8):
                    start = words[(step * 8 + k) * FIELDS + field]
                    pltpu.store(wide_ref.at[pl.ds(start, 8), :], tile, mask=lines[k])

    def permute_place(at):
        each = part_rows // chunk_rows
        part = lax.div(at, each)
        return part * (out_ref.shape[0] // PARTS) + (at - part * each) * (chunk_rows * FIELDS)

    word_stream(
        out_ref,
        buffers,
        sems,
        permute_place,
        width // chunk_rows,
        permute,
        lambda: lax.fori_loop(0, slot_blocks, clear, 0, unroll=2),
    )

    def merge(block, carry):
        halves = []
        for half in range(2):
            piece = jnp.zeros((8, LANES), F32)
            for group in range(GROUPS):
                start = aligned(block * LANES + group * 16 + (half + 1) * 8, 8)
                piece = jnp.where(lanes[group], wide_ref[pl.ds(start, 8), :], piece)
            halves.append(piece)
        start = aligned(block * 16, 16)
        sent_ref[pl.ds(start, 16), :] = jnp.concatenate(halves, axis=0).astype(BF16)
        return carry

    lax.fori_loop(0, slot_blocks, merge, 0, unroll=4 if slot_blocks % 4 == 0 else 1)
    each = sent_ref.shape[0] // owners
    for one in range(owners):
        sent_refs[one][...] = sent_ref[one * each : (one + 1) * each, :]


def add_kernel(owners, packed, table_lanes, index_ref, request_ref, asked_ref, *refs):
    received_refs = refs[:owners]
    table_refs = refs[owners : owners + 2 * TABLE_CHUNKS]
    (
        received_ref,
        left_grad_ref,
        right_grad_ref,
        left_ref,
        right_ref,
        sems,
        *sums,
    ) = refs[owners + 2 * TABLE_CHUNKS :]
    rows = sums[0].shape[0] - 16
    core, batch = index_ref[0], index_ref[1]
    sources = received_ref.shape[0] // packed
    chunks = packed // 16
    lines, _ = masks()
    eye = identity()
    own_group = lax.shift_right_logical(iota((1, LANES), 1), 4)
    from_lane = iota((LANES, 2 * LANES), 0)
    to_lane = iota((LANES, 2 * LANES), 1)
    spread_names = []
    spread_grads = []
    for pair in range(GROUPS // 2):
        group = pair * 2 + lax.shift_right_logical(to_lane, 7)
        spread_names.append(
            jnp.where(lax.shift_right_logical(from_lane, 4) == group, 1.0, 0.0).astype(BF16)
        )
        wanted = group * EMB + (to_lane & (EMB - 1))
        spread_grads.append(jnp.where(from_lane == wanted, 1.0, 0.0).astype(BF16))

    def place(source):
        distance = lax.div(source, PARTS)
        return (distance ^ batch) * PARTS + source - distance * PARTS

    def spread(source, grad_ref):
        def step(first, count, pair):
            asked = asked_ref[pl.ds(place(source) * chunks + first, count), :]
            names = (own_group - lax.shift_right_logical(asked, table_lanes)) & (GROUPS - 1)
            start = aligned(source * packed + first * 16, 16)
            grads = received_ref[pl.ds(start, count * 16), :]
            lane_group = lax.shift_right_logical(iota((count * 16, LANES), 1), 4).astype(F32)
            wide_names = matmul(slot_lines(names.astype(F32)), spread_names[pair])
            wide_grads = matmul(grads, spread_grads[pair])
            for side in range(2):
                half = slice(side * LANES, (side + 1) * LANES)
                masked = jnp.where(wide_names[:, half] == lane_group, wide_grads[:, half], 0.0)
                for chunk in range(count):
                    start = (first + chunk) * LANES + (pair * 2 + side) * 16
                    grad_ref[start : start + 16, :] = masked[chunk * 16 : (chunk + 1) * 16]

        return [
            functools.partial(step, first, min(4, chunks - first), pair)
            for first in range(0, chunks, 4)
            for pair in range(GROUPS // 2)
        ]

    def clear(step, carry):
        for total in sums:
            total[pl.ds(aligned(8 + step * LANES, 8), LANES), :] = jnp.zeros((LANES, LANES), F32)
        return carry

    def before():
        for total in sums:
            total[0:8, :] = jnp.zeros((8, LANES), F32)
            total[8 + rows : 16 + rows, :] = jnp.zeros((8, LANES), F32)
        lax.fori_loop(0, rows // LANES, clear, 0)
        gather_blocks(received_refs, received_ref)
        for one in spread(0, left_grad_ref):
            one()

    def process(source, words):
        now, later = left_grad_ref, right_grad_ref
        if words is right_ref:
            now, later = later, now
        steps = spread(jnp.minimum(source + 1, sources - 1), later)
        rows = GROUPS * packed // 8
        for row in range(rows):
            if row * len(steps) // rows != (row - 1) * len(steps) // rows:
                steps[row * len(steps) // rows]()
            grads = now[row * 8 : (row + 1) * 8, :]
            for k in range(8):
                place = pl.ds(words[row * 8 + k], 8)
                total = sums[k % STREAMS]
                pltpu.store(total.at[place, :], total[place, :] + grads, mask=lines[k])

    size = GROUPS * packed
    word_stream(
        request_ref,
        (left_ref, right_ref),
        sems,
        lambda at: place(at) * size,
        sources,
        process,
        before,
    )

    def finish(kept, block, carry):
        start = aligned(8 + block * LANES, 8)
        total = functools.reduce(jnp.add, [one[pl.ds(start, LANES), :] for one in sums])
        turned = matmul_nt(eye, total.astype(BF16)).astype(BF16)
        each = GROUPS // (2 * TABLE_CHUNKS)
        for group in range(GROUPS):
            half, column = divmod(group, GROUPS // 2)
            chunk, column = divmod(column, each)
            table_ref = table_refs[chunk + (0 if half == kept else TABLE_CHUNKS)]
            column = aligned(column * rows + block * LANES, LANES)
            table_ref[:, pl.ds(column, LANES)] = turned[group * EMB : (group + 1) * EMB]
        return carry

    for kept in range(2):

        @pl.when(core == kept)
        def _():
            lax.fori_loop(0, rows // LANES, functools.partial(finish, kept), 0, unroll=8)


def unpack_kernel(weight_piece, extra_piece, pairs, piece_ref, *refs):
    (
        dense_w_ref,
        gate_ref,
        hidden_w_ref,
        hidden_b_ref,
        output_w_ref,
        output_b_ref,
        tower_w_ref,
        tower_b_ref,
        head_w_ref,
        head_b_ref,
        weight_ref,
        extra_ref,
    ) = refs
    for owner in range(piece_ref.shape[0]):
        weight_ref[owner * weight_piece : (owner + 1) * weight_piece, :] = piece_ref[
            owner, :weight_piece, :
        ].astype(F32)
        high = piece_ref[owner, weight_piece : weight_piece + extra_piece, :].astype(F32)
        low = piece_ref[owner, weight_piece + extra_piece :, :].astype(F32)
        extra_ref[owner * extra_piece : (owner + 1) * extra_piece, :] = high + low
    gate_rows = D_IN // LANES * pairs
    small = H2 + gate_rows + 16

    def small_line(row):
        return extra_ref[small + row : small + row + 1, :] + extra_ref[small + 6 + row : small + 7 + row, :]

    for half in range(H1 // LANES):
        span = slice(half * LANES, (half + 1) * LANES)
        hidden_w_ref[0, :, span] = weight_ref[half * D_IN : (half + 1) * D_IN, :]
        hidden_b_ref[:, span] = small_line(3 + half)
    output_w_ref[0] = weight_ref[2 * D_IN : GRAD_ROWS, :]
    output_b_ref[...] = small_line(5)
    tower_w_ref[...] = extra_ref[:H2, :]
    head_w_ref[...] = small_line(0)
    tower_b_ref[...] = small_line(1)
    head_b_ref[...] = small_line(2)[:, :TASKS]
    for block in range(D_IN // LANES):
        gate_ref[:, block * LANES : (block + 1) * LANES] = extra_ref[
            H2 + block * pairs : H2 + (block + 1) * pairs, :
        ]
    dense_w_ref[...] = extra_ref[H2 + gate_rows : H2 + gate_rows + DENSE, :BOTTOM]


SMEM = pl.BlockSpec(memory_space=pltpu.SMEM)
VMEM = pl.BlockSpec(memory_space=pltpu.VMEM)
ANY = pl.BlockSpec(memory_space=pl.ANY)


def call(kernel, outs, ins, scratch, name, micros, vmem=16):
    return pl.pallas_call(
        kernel,
        out_shape=outs,
        in_specs=ins,
        out_specs=jax.tree.map(lambda _: VMEM, outs),
        scratch_shapes=scratch,
        name=name,
        cost_estimate=pl.CostEstimate(
            flops=int(micros * 1.15e9), bytes_accessed=int(micros * 3e6), transcendentals=0
        ),
        compiler_params=pltpu.CompilerParams(vmem_limit_bytes=vmem << 20),
    )


def shards(
    emb_table,
    dense_feats,
    dense_w,
    gate_w,
    hidden_w,
    hidden_b,
    output_w,
    output_b,
    tower_w,
    tower_b,
    head_w,
    head_b,
    row_owner,
    local_row,
    labels,
):
    owners = lax.axis_size("batch")
    experts = lax.axis_size("expert")
    expert_index = lax.axis_index("expert")
    core = expert_index & 1
    row_total = dense_feats.shape[1]
    part_rows = row_total // PARTS
    lookups = row_total * FIELDS
    part_lookups = lookups // PARTS
    capacity = 2 * part_lookups // owners
    packed = -(-capacity // (GROUPS * 16)) * 16
    table_rows = emb_table.shape[0]
    table_packed = table_rows // GROUPS
    table_lanes = table_packed.bit_length() - 1
    scale = 1.0 / math.sqrt(row_total * owners * experts)
    slots = owners * PARTS * GROUPS * packed
    part_slots = owners * packed
    lookup_rows = lookups // LANES
    list_part = -(-lookup_rows // (PARTS * 24)) * 24
    list_rows = list_part * PARTS

    def tie(*values):
        return lax.optimization_barrier(values)

    def exchange(values, axis):
        return lax.all_to_all(values, axis, split_axis=0, concat_axis=0, tiled=True)

    def swap(values, axis, bits):
        size = lax.axis_size(axis)
        return lax.ppermute(values, axis, [(one, one ^ bits) for one in range(size)])

    def swap_all(blocks):
        return [blocks[0]] + [swap(blocks[bits], "batch", bits) for bits in range(1, owners)]

    owner_list = row_owner.reshape(lookup_rows, LANES)
    local_list = local_row.reshape(lookup_rows, LANES)
    slot_rows = slots // LANES
    list_shape = jax.ShapeDtypeStruct((list_rows, LANES), I32)
    batch_index = lax.axis_index("batch").reshape(1)
    requests, back, out = call(
        functools.partial(route_kernel, owners, part_lookups, packed, table_lanes),
        (jax.ShapeDtypeStruct((slot_rows, LANES), I32), list_shape, list_shape),
        [SMEM, VMEM, VMEM],
        [pltpu.VMEM((list_rows, LANES), I32)] * 3 + [pltpu.VMEM((PARTS, slot_rows // PARTS, 2 * LANES), F32)],
        "route",
        9,
    )(batch_index, owner_list, local_list)
    asked = exchange(requests.reshape(owners, slots // owners), "batch")
    asked = asked.reshape(slot_rows, LANES)
    offset = 8 - (jnp.arange(LANES, dtype=I32) & 7)
    words = ((asked & (table_packed - 1)) + offset).reshape(-1)
    back = back.reshape(-1)
    out = out.reshape(-1)

    hidden_b, out = tie(hidden_b, out)
    table, weights = call(
        pack_kernel,
        (
            jax.ShapeDtypeStruct((table_packed + 16, LANES), F32),
            jax.ShapeDtypeStruct((WEIGHT_ROWS, LANES), BF16),
        ),
        [VMEM] * 5,
        [],
        "pack",
        5,
        56,
    )(emb_table.T, hidden_w, output_w, hidden_b, output_b)
    weights = lax.all_gather(weights, "expert", axis=0, tiled=False)

    slot_words = [pltpu.SMEM((GROUPS * packed,), I32)] * 2 + [pltpu.SemaphoreType.DMA((2,))]
    row_words = [pltpu.SMEM((CHUNK_ROWS * FIELDS,), I32)] * 2 + [pltpu.SemaphoreType.DMA((2,))]
    returned = []
    for part in range(PARTS):
        found = call(
            functools.partial(fetch_kernel, owners, part, packed, table_lanes),
            jax.ShapeDtypeStruct((part_slots, LANES), BF16),
            [ANY, VMEM, ANY],
            [
                pltpu.VMEM((table_packed + 16, LANES), F32),
                pltpu.VMEM((part_slots, LANES), F32),
                pltpu.VMEM((GROUPS * packed, LANES), F32),
            ]
            + slot_words
            + [pltpu.SemaphoreType.DMA],
            "fetch",
            24 // PARTS,
            56,
        )(words, asked, table)
        found = exchange(found.reshape(owners, packed, LANES), "batch")
        returned.append(found.reshape(part_slots, LANES))
    early = []
    for part in range(PARTS - 1):
        early.append(
            call(
                functools.partial(unpermute_kernel, part, part_rows),
                jax.ShapeDtypeStruct((part_rows, D_IN), BF16),
                [ANY, VMEM],
                [pltpu.VMEM((GROUPS * part_slots + 16, LANES), F32), *row_words],
                "unpermute",
                15,
                56,
            )(back, returned[part])
        )

    pairs = TASKS * experts
    shared_rows = H2 + 24 + D_IN // LANES * pairs + 16
    vectors = jnp.stack([tower_b, head_w])
    *sent, grad_dense, grad_weight, grad_bias, grad_shared = call(
        functools.partial(dense_kernel, owners, part_rows, experts, scale),
        (
            *[jax.ShapeDtypeStruct((PARTS * packed, LANES), BF16)] * owners,
            jax.ShapeDtypeStruct((DENSE, row_total), F32),
            jax.ShapeDtypeStruct((experts, GRAD_ROWS, LANES), BF16),
            jax.ShapeDtypeStruct((experts, 8, LANES), F32),
            jax.ShapeDtypeStruct((shared_rows, LANES), F32),
        ),
        [ANY, ANY] + [VMEM] * 7 + [SMEM] + [VMEM] * PARTS,
        [
            pltpu.VMEM((slots + 16, LANES), F32),
            pltpu.VMEM((row_total, D_IN), BF16),
            pltpu.VMEM((D_IN, row_total), BF16),
            pltpu.VMEM((experts, H1, row_total), BF16),
            pltpu.VMEM((experts, H1, row_total), F32),
            pltpu.VMEM((experts, H2, row_total), F32),
            pltpu.VMEM((experts, H2, row_total), F32),
            pltpu.VMEM((pairs, row_total), F32),
            pltpu.VMEM((TASKS * H2, row_total), F32),
            pltpu.VMEM((TASKS * H2, row_total), F32),
            pltpu.VMEM((8, row_total), F32),
            pltpu.VMEM((pairs, row_total), F32),
            pltpu.VMEM((D_IN, row_total), F32),
            pltpu.VMEM((D_IN, row_total), BF16),
            pltpu.VMEM((FIELDS, LANES, LANES), F32),
            *row_words,
            pltpu.VMEM((PARTS * part_slots, LANES), BF16),
        ],
        "dense",
        45,
        56,
    )(
        back,
        out,
        returned[-1],
        weights,
        gate_w.T,
        dense_feats,
        dense_w,
        tower_w,
        vectors,
        head_b,
        labels,
        *early,
    )
    received = swap_all(sent)

    def split(values):
        high = lax.reduce_precision(values, exponent_bits=8, mantissa_bits=7)
        return high.astype(BF16), (values - high).astype(BF16)

    far = owners // 2
    received[far], grad_weight, grad_bias, grad_shared = tie(
        received[far], grad_weight, grad_bias, grad_shared
    )

    def spread_rows(values, piece):
        rows = values.shape[1]
        values = jnp.pad(values, ((0, 0), (0, piece * owners - rows), (0, 0)))
        return values.reshape(experts, owners, piece, LANES).transpose(1, 0, 2, 3)

    large = jnp.concatenate([grad_shared[:H2], grad_shared[H2 + 24 :]], axis=0).astype(BF16)
    small = jnp.concatenate([grad_shared[H2 + 8 * row : H2 + 8 * row + 1] for row in range(3)])
    small = jnp.concatenate(
        [jnp.broadcast_to(small[None], (experts, 3, LANES)), grad_bias[:, :3]], axis=1
    )
    extra = jnp.concatenate(
        [jnp.broadcast_to(large[None], (experts, *large.shape)), *split(small)], axis=1
    )
    weight_piece = -(-GRAD_ROWS // (16 * owners)) * 16
    extra_piece = -(-extra.shape[1] // (16 * owners)) * 16
    piece_rows = weight_piece + extra_piece
    pieces = jnp.concatenate(
        [spread_rows(grad_weight, weight_piece), spread_rows(extra, extra_piece)], axis=2
    )
    late = owners - 2
    *received[:late], pieces = tie(*received[:late], pieces)
    pieces = exchange(pieces.reshape(owners * experts, piece_rows, LANES), ("batch", "expert"))

    columns = table_rows // 2 // TABLE_CHUNKS
    table_part = call(
        functools.partial(add_kernel, owners, packed, table_lanes),
        (jax.ShapeDtypeStruct((EMB, columns), BF16),) * (2 * TABLE_CHUNKS),
        [SMEM, ANY, VMEM] + [VMEM] * owners,
        [pltpu.VMEM((PARTS * part_slots, LANES), BF16)]
        + [pltpu.VMEM((GROUPS * packed, LANES), F32)] * 2
        + slot_words
        + [pltpu.VMEM((table_packed + 16, LANES), F32)] * STREAMS,
        "add",
        60,
        48,
    )(jnp.concatenate([core.reshape(1), batch_index]), words, asked, *received)

    def add_low(left, right):
        return (left.astype(F32) + right.astype(F32)).astype(BF16)

    *table_part, pieces = tie(*table_part, pieces)
    kept = [
        add_low(one, swap(other, "expert", 1))
        for one, other in zip(table_part[:TABLE_CHUNKS], table_part[TABLE_CHUNKS:])
    ]
    *kept, pieces = tie(*kept, pieces)
    over = [swap(one, "expert", 2) for one in kept]
    sums = jnp.sum(pieces.astype(F32), axis=0)
    piece = jnp.concatenate([sums[:weight_piece].astype(BF16), *split(sums[weight_piece:])], axis=0)
    pieces = exchange(jnp.broadcast_to(piece[None], (owners, *piece.shape)), "batch")
    bit = 2
    while bit < experts:
        kept = [add_low(one, other) for one, other in zip(kept, over)]
        bit *= 2
        if bit < experts:
            over = [swap(one, "expert", bit) for one in kept]
    small = call(
        functools.partial(unpack_kernel, weight_piece, extra_piece, pairs),
        tuple(
            jax.ShapeDtypeStruct(shape, F32)
            for shape in (
                (DENSE, BOTTOM),
                (pairs, D_IN),
                (1, D_IN, H1),
                (1, H1),
                (1, H1, H2),
                (1, H2),
                (H2, TASKS * TOWER),
                (1, TASKS * TOWER),
                (1, TASKS * TOWER),
                (1, TASKS),
            )
        ),
        [VMEM],
        [
            pltpu.VMEM((owners * weight_piece, LANES), F32),
            pltpu.VMEM((owners * extra_piece, LANES), F32),
        ],
        "unpack",
        3,
    )(pieces)
    others = [swap(one, "expert", 1) for one in kept]
    *others, small = tie(*others, small)
    lower = [jnp.where(core == 0, one, other) for one, other in zip(kept, others)]
    upper = [jnp.where(core == 0, other, one) for one, other in zip(kept, others)]
    table_total = jnp.concatenate(lower + upper, axis=1).astype(F32).T
    grad_dense_w, gate, hidden, hidden_bias, output, output_bias, tower, tower_bias, head, head_bias = (
        small
    )
    return (
        table_total,
        grad_dense,
        grad_dense_w,
        gate.T,
        hidden,
        hidden_bias,
        output,
        output_bias,
        tower,
        tower_bias.reshape(-1),
        head.reshape(-1),
        head_bias.reshape(-1),
    )


def solution(mesh):
    in_specs = (
        P("batch", None),
        P(None, ("batch", "expert")),
        P(),
        P(),
        P("expert", None, None),
        P("expert", None),
        P("expert", None, None),
        P("expert", None),
        P(),
        P(),
        P(),
        P(),
        P(("batch", "expert"), None),
        P(("batch", "expert")),
        P(None, ("batch", "expert")),
    )
    out_specs = (
        P("batch", None),
        P(None, ("batch", "expert")),
        P(),
        P(),
        P("expert", None, None),
        P("expert", None),
        P("expert", None, None),
        P("expert", None),
        P(),
        P(),
        P(),
        P(),
    )
    return jax.shard_map(shards, mesh=mesh, in_specs=in_specs, out_specs=out_specs, check_vma=False)
```

```python
import functools
import math

import jax
import jax.numpy as jnp
from jax import lax
from jax.experimental import pallas as pl
from jax.experimental.pallas import tpu as pltpu
from jax.sharding import PartitionSpec as P

FIELDS = 26
EMB = 16
DENSE = 13
BOTTOM = 96
D_IN = 512
H1 = 256
H2 = 128
TOWER = 64
TASKS = 2
LANES = 128
GROUPS = LANES // EMB
EMB_WIDTH = FIELDS * EMB
BIAS_ROWS = 16
GRAD_ROWS = 2 * D_IN + H1
WEIGHT_ROWS = GRAD_ROWS + BIAS_ROWS
STREAMS = 8
PARTS = 2
CHUNK_ROWS = 64
TABLE_CHUNKS = 2

F32 = jnp.float32
BF16 = jnp.bfloat16
I32 = jnp.int32


def iota(shape, axis):
    return lax.broadcasted_iota(I32, shape, axis)


def matmul(a, b):
    return lax.dot_general(a, b, (((1,), (0,)), ((), ())), preferred_element_type=F32)


def matmul_nt(a, b):
    return lax.dot_general(a, b, (((1,), (1,)), ((), ())), preferred_element_type=F32)


def matmul_tn(a, b):
    return lax.dot_general(a, b, (((0,), (0,)), ((), ())), preferred_element_type=F32)


def identity():
    return (iota((LANES, LANES), 0) == iota((LANES, LANES), 1)).astype(BF16)


def aligned(value, step):
    return pl.multiple_of(value, step)


def silu_parts(values):
    sig = jax.nn.sigmoid(values)
    return values * sig, sig * (1.0 + values * (1.0 - sig))


def route_kernel(
    owners, part_lookups, packed, table_lanes, batch_ref, owner_ref, local_ref, request_ref,
    back_ref, out_ref, high_ref, low_ref, value_ref, total_ref
):
    rows = high_ref.shape[0]
    part_rows = rows // PARTS
    filled = part_lookups // LANES
    slot_rows = request_ref.shape[0]
    shape = (rows, LANES)
    high_ref[...] = jnp.full(shape, -1, I32)
    low_ref[...] = jnp.zeros(shape, I32)
    for part in range(PARTS):
        lines = slice(part * part_rows, part * part_rows + filled)
        taken = slice(part * filled, (part + 1) * filled)
        high_ref[lines, :] = owner_ref[taken, :]
        low_ref[lines, :] = local_ref[taken, :]
    owner = high_ref[...]
    local = low_ref[...]
    row_id = iota(shape, 0)
    tri = (iota((LANES, LANES), 0) <= iota((LANES, LANES), 1)).astype(BF16)
    ones = jnp.ones((LANES, LANES), BF16)
    before = (iota((part_rows, part_rows), 1) < iota((part_rows, part_rows), 0)).astype(BF16)
    ranks = []
    for part in range(PARTS):
        own = owner[part * part_rows : (part + 1) * part_rows]
        rank = jnp.zeros((part_rows, LANES), F32)
        for one in range(owners):
            hit = own == one
            hits = jnp.where(hit, 1.0, 0.0).astype(BF16)
            upto = matmul(hits, tri)
            ahead = matmul(before, matmul(hits, ones).astype(BF16))
            rank = jnp.where(hit, upto + ahead - 1.0, rank)
        ranks.append(rank)
    rank = jnp.concatenate(ranks, axis=0)
    part_id = jnp.zeros(shape, I32)
    for part in range(1, PARTS):
        part_id = part_id + jnp.where(row_id >= part * part_rows, 1, 0)
    rank = rank.astype(I32)
    group = jnp.zeros(shape, I32)
    for step in range(1, GROUPS):
        group = group + jnp.where(rank >= step * packed, 1, 0)
    place = rank - group * packed
    held = jnp.maximum(owner, 0)
    chunks = packed // 16
    chunk = lax.shift_right_logical(place, 4)
    block = (held * PARTS + part_id) * chunks + chunk
    inside = group * 16 + (place & 15)
    table_group = lax.shift_right_logical(local, table_lanes)
    table_row = local & ((1 << table_lanes) - 1)
    high_ref[...] = jnp.where(owner < 0, -1, held * chunks + chunk)
    low_ref[...] = inside
    value_ref[...] = table_row + (((group - table_group) & (GROUPS - 1)) << table_lanes)
    lookup = (row_id - part_id * part_rows) * LANES + iota(shape, 1)
    quotient = jnp.floor((lookup.astype(F32) + 0.5) * (1.0 / FIELDS)).astype(I32)
    field_group = (lookup - quotient * FIELDS) & (GROUPS - 1)
    offset = 8 - (quotient & 7)
    turn = (field_group - group) & (GROUPS - 1)
    back_ref[...] = (turn * owners + held) * packed + place + offset
    away = ((held ^ batch_ref[0]) - held) * (PARTS * GROUPS * packed)
    out_ref[...] = block * LANES + inside + offset + away
    total_ref[...] = jnp.zeros_like(total_ref)
    own_rows = slot_rows // PARTS

    def gather_requests(part, step, carry):
        base = aligned(part * part_rows + step * 8, 8)
        high = high_ref[pl.ds(base, 8), :]
        low = low_ref[pl.ds(base, 8), :]
        values = value_ref[pl.ds(base, 8), :]
        upper = lax.shift_right_logical(values, 8).astype(F32)
        lower = (values & 255).astype(F32)
        at_high = []
        at_low = []
        for k in range(8):
            line = slice(k, k + 1)
            at_high.append(jnp.where(iota((own_rows, LANES), 0) == high[line], 1.0, 0.0).astype(BF16))
            same = iota((LANES, LANES), 0) == low[line]
            at_low.append(
                jnp.concatenate(
                    [jnp.where(same, upper[line], 0.0), jnp.where(same, lower[line], 0.0)], axis=0
                ).astype(BF16)
            )
        total_ref[part] += matmul_nt(
            jnp.concatenate(at_high, axis=1), jnp.concatenate(at_low, axis=1)
        )
        return carry

    for part in range(PARTS):
        lax.fori_loop(0, part_rows // 8, functools.partial(gather_requests, part), 0, unroll=3)
        total = (total_ref[part, :, :LANES] * 256.0 + total_ref[part, :, LANES:]).astype(I32)
        for one in range(owners):
            start = (one * PARTS + part) * chunks
            request_ref[start : start + chunks, :] = total[one * chunks : (one + 1) * chunks]


def pack_kernel(
    table_ref, hidden_w_ref, output_w_ref, hidden_b_ref, output_b_ref, packed_ref, weight_ref
):
    lines = []
    for values in (hidden_b_ref[:, :LANES], hidden_b_ref[:, LANES:], output_b_ref[...]):
        for _ in range(3):
            term = values.astype(BF16).astype(F32)
            lines.append(term)
            values = values - term
    lines.append(jnp.zeros((BIAS_ROWS - len(lines), LANES), F32))
    for half in range(H1 // LANES):
        weight_ref[half * D_IN : (half + 1) * D_IN, :] = hidden_w_ref[
            0, :, half * LANES : (half + 1) * LANES
        ]
    weight_ref[2 * D_IN : 2 * D_IN + H1, :] = output_w_ref[0]
    weight_ref[2 * D_IN + H1 :, :] = jnp.concatenate(lines, axis=0).astype(BF16)
    rows = table_ref.shape[1] // GROUPS
    eye = identity()

    def step(block, carry):
        pieces = []
        for group in range(GROUPS):
            start = aligned(group * rows + block * LANES, LANES)
            pieces.append(table_ref[:, pl.ds(start, LANES)])
        packed_ref[pl.ds(aligned(8 + block * LANES, 8), LANES), :] = matmul_nt(
            eye, jnp.concatenate(pieces, axis=0)
        )
        return carry

    packed_ref[0:8, :] = jnp.zeros((8, LANES), F32)
    packed_ref[8 + rows : 16 + rows, :] = jnp.zeros((8, LANES), F32)

    lax.fori_loop(0, rows // LANES, step, 0, unroll=8)


def masks():
    line = iota((8, LANES), 0)
    group = lax.shift_right_logical(iota((8, LANES), 1), 4)
    return [line == k for k in range(8)], [group == one for one in range(GROUPS)]


def turn_copies(rows_ref, wide_ref):
    rows = rows_ref.shape[0]
    half = GROUPS // 2
    from_lane = iota((LANES, half * LANES), 0)
    to_lane = iota((LANES, half * LANES), 1)
    turn = (lax.shift_right_logical(to_lane, 7) + half) * EMB
    turns = jnp.where(((from_lane + turn - to_lane) & (LANES - 1)) == 0, 1.0, 0.0).astype(BF16)

    def step(block, carry):
        start = aligned(block * LANES, LANES)
        piece = rows_ref[pl.ds(start, LANES), :]
        moved = matmul(piece, turns)
        piece = piece.astype(F32)
        for turn in range(GROUPS):
            if turn >= half:
                one = moved[:, (turn - half) * LANES : (turn - half + 1) * LANES]
            else:
                one = pltpu.roll(piece, turn * EMB, 1) if turn else piece
            wide_ref[pl.ds(aligned(8 + turn * rows + start, 8), LANES), :] = one
        return carry

    blocks = rows // LANES
    unroll = [count for count in (4, 3, 2, 1) if blocks % count == 0][0]
    lax.fori_loop(0, blocks, step, 0, unroll=unroll)


def assemble(wide_ref, word, groups, lines, lanes):
    block = jnp.zeros((8, LANES), F32)
    for place, group in groups:
        piece = wide_ref[pl.ds(word(0, place), 8), :]
        for k in range(1, 8):
            piece = jnp.where(lines[k], wide_ref[pl.ds(word(k, place), 8), :], piece)
        block = jnp.where(lanes[group], piece, block)
    return block


def word_stream(word_ref, buffers, sems, place, count, process, before=None):
    slots = len(buffers)
    size = buffers[0].shape[0]

    def copy(at, slot):
        start = aligned(place(at), LANES)
        return pltpu.make_async_copy(
            word_ref.at[pl.ds(start, size)], buffers[slot], sems.at[slot]
        )

    for slot in range(min(slots, count)):
        copy(slot, slot).start()
    if before is not None:
        before()

    def step(turn, carry):
        for slot in range(slots):
            at = turn * slots + slot
            copy(at, slot).wait()
            process(at, buffers[slot])

            @pl.when(at + slots < count)
            def _():
                copy(at + slots, slot).start()

        return carry

    lax.fori_loop(0, count // slots, step, 0)
    for slot in range(count % slots):
        at = count // slots * slots + slot
        copy(at, slot).wait()
        process(at, buffers[slot])


def slot_lines(numbers):
    own = (iota((16, LANES), 1) & 15) == iota((16, LANES), 0)
    return jnp.concatenate(
        [jnp.where(own, numbers[row : row + 1], 0.0) for row in range(numbers.shape[0])], axis=0
    ).astype(BF16)


def same_group():
    return (
        lax.shift_right_logical(iota((LANES, LANES), 0), 4)
        == lax.shift_right_logical(iota((LANES, LANES), 1), 4)
    ).astype(BF16)


def fetch_kernel(
    owners, part, packed, table_lanes, request_ref, asked_ref, table_ref, found_ref, turn_ref,
    piece_ref, left_ref, right_ref, sems
):
    lines, _ = masks()
    chunks = packed // 16
    within = same_group()
    group = lax.shift_right_logical(iota((8, LANES), 1), 4)
    bits = [(group & (1 << bit)) != 0 for bit in range(3)]

    def make_turns(source, first, count):
        at = (source * PARTS + part) * chunks + first
        numbers = lax.shift_right_logical(asked_ref[pl.ds(at, count), :], table_lanes)
        start = aligned(source * packed + first * 16, 16)
        turn_ref[pl.ds(start, count * 16), :] = matmul(slot_lines(numbers.astype(F32)), within)

    def before():
        make_turns(0, 0, chunks)

    def process(source, words):
        later = jnp.minimum(source + 1, owners - 1)
        for chunk in range(chunks):
            if chunk % 4 == 0:
                make_turns(later, chunk, min(4, chunks - chunk))
            for line in range(LANES):
                base = chunk * LANES + line // 8 * 8
                pltpu.store(
                    piece_ref.at[base : base + 8, :],
                    table_ref[pl.ds(words[chunk * LANES + line], 8), :],
                    mask=lines[line % 8],
                )
            start = aligned(source * packed + chunk * 16, 16)
            turns = turn_ref[pl.ds(start, 16), :]
            halves = []
            for half in range(2):
                mixed = []
                for group in range(GROUPS):
                    base = chunk * LANES + group * 16 + half * 8
                    mixed.append(piece_ref[base : base + 8, :])
                for bit in range(3):
                    mixed = [
                        jnp.where(bits[bit], mixed[(turn + (1 << bit)) % GROUPS], mixed[turn])
                        for turn in range(GROUPS)
                    ]
                wanted = turns[half * 8 : (half + 1) * 8]
                block = mixed[0]
                for turn in range(1, GROUPS):
                    moved = pltpu.roll(mixed[turn], turn * EMB, 1)
                    block = jnp.where(wanted == float(turn), moved, block)
                halves.append(block)
            found_ref[pl.ds(start, 16), :] = jnp.concatenate(halves, axis=0).astype(BF16)

    size = chunks * LANES
    word_stream(
        request_ref,
        (left_ref, right_ref),
        sems,
        lambda at: (at * PARTS + part) * size,
        owners,
        process,
        before,
    )


def unpermute(
    part, part_rows, back_ref, returned_ref, feature_ref, first_row, wide_ref, buffers, sems
):
    lines, lanes = masks()
    size = buffers[0].shape[0]
    chunk_rows = size // FIELDS

    def process(chunk, words):
        for block in range(chunk_rows // 16):
            start_row = aligned(first_row + chunk * chunk_rows + block * 16, 16)
            for lane_block in range(D_IN // LANES):
                fields = range(lane_block * GROUPS, min((lane_block + 1) * GROUPS, FIELDS))
                halves = [
                    assemble(
                        wide_ref,
                        lambda k, field, half=half: words[
                            (block * 16 + half * 8 + k) * FIELDS + field
                        ],
                        [(field, field % GROUPS) for field in fields],
                        lines,
                        lanes,
                    )
                    for half in range(2)
                ]
                feature_ref[
                    pl.ds(start_row, 16), lane_block * LANES : (lane_block + 1) * LANES
                ] = jnp.concatenate(halves, axis=0).astype(BF16)

    first = part * back_ref.shape[0] // PARTS
    word_stream(
        back_ref,
        buffers,
        sems,
        lambda at: first + at * size,
        part_rows // chunk_rows,
        process,
        lambda: turn_copies(returned_ref, wide_ref),
    )


def gather_blocks(block_refs, whole_ref):
    rows = block_refs[0].shape[0]
    for one, block_ref in enumerate(block_refs):
        whole_ref[one * rows : (one + 1) * rows, :] = block_ref[...]


def unpermute_kernel(
    part, part_rows, back_ref, returned_ref, feature_ref, wide_ref, left_ref, right_ref, sems
):
    unpermute(
        part,
        part_rows,
        back_ref,
        returned_ref,
        feature_ref,
        0,
        wide_ref,
        (left_ref, right_ref),
        sems,
    )


def dense_kernel(
    owners,
    part_rows,
    experts,
    scale,
    back_ref,
    out_ref,
    returned_ref,
    weight_ref,
    gate_ref,
    dense_ref,
    dense_w_ref,
    tower_ref,
    vector_ref,
    head_b_ref,
    label_ref,
    *refs,
):
    early = refs[: PARTS - 1]
    refs = refs[PARTS - 1 :]
    sent_refs = refs[:owners]
    (
        grad_dense_ref,
        grad_weight_ref,
        grad_bias_ref,
        grad_shared_ref,
        wide_ref,
        feature_ref,
        turned_ref,
        hidden_ref,
        hidden_slope_ref,
        output_ref,
        output_slope_ref,
        gates_ref,
        mixed_ref,
        mixed_grad_ref,
        dot_ref,
        logit_ref,
        input_ref,
        low_ref,
        tiled_ref,
        left_ref,
        right_ref,
        sems,
        sent_ref,
    ) = refs[owners:]
    buffers = (left_ref, right_ref)
    width = turned_ref.shape[1]
    blocks = width // LANES
    slot_blocks = sent_ref.shape[0] // 16
    eye = identity()
    lines, lanes = masks()

    def put_weight(expert, cut, value):
        grad_weight_ref[expert, cut, :] = value.astype(BF16)

    def put_shared(rows, cut, value):
        grad_shared_ref[rows, cut] = value

    whole = slice(None)
    for part in range(PARTS - 1):
        feature_ref[part * part_rows : (part + 1) * part_rows, :] = early[part][...]
    unpermute(
        PARTS - 1,
        part_rows,
        back_ref,
        returned_ref,
        feature_ref,
        (PARTS - 1) * part_rows,
        wide_ref,
        buffers,
        sems,
    )

    for lane_block in range(D_IN // LANES):
        for block in range(blocks):
            piece = feature_ref[
                block * LANES : (block + 1) * LANES, lane_block * LANES : (lane_block + 1) * LANES
            ]
            turned_ref[
                lane_block * LANES : (lane_block + 1) * LANES, block * LANES : (block + 1) * LANES
            ] = matmul_nt(eye, piece).astype(BF16)
    dense = dense_ref[...]
    dense_w = dense_w_ref[...]
    turned_ref[EMB_WIDTH:, :] = matmul_tn(dense_w, dense).astype(BF16)

    features = turned_ref[...]
    logits = matmul(gate_ref[...], features)
    for task in range(TASKS):
        part_logits = logits[task * experts : (task + 1) * experts]
        powers = jnp.exp(part_logits - jnp.max(part_logits, axis=0, keepdims=True))
        gates_ref[task * experts : (task + 1) * experts, :] = powers / jnp.sum(
            powers, axis=0, keepdims=True
        )

    mixed_ref[...] = jnp.zeros_like(mixed_ref)

    def column(line):
        tall = jnp.transpose(jnp.broadcast_to(line, (LANES, LANES)))
        return jnp.concatenate([tall] * blocks, axis=1)

    def bias_line(expert, rows):
        lines = [weight_ref[expert, 2 * D_IN + H1 :, :].astype(F32)[row : row + 1] for row in rows]
        return functools.reduce(jnp.add, lines)

    def forward(expert, carry):
        turned = turned_ref[...]
        for half in range(H1 // LANES):
            weights = weight_ref[expert, half * D_IN : (half + 1) * D_IN, :]
            bias = column(bias_line(expert, range(half * 3, half * 3 + 3)))
            value, slope = silu_parts(matmul_tn(weights, turned) + bias)
            hidden_ref[expert, half * LANES : (half + 1) * LANES, :] = value.astype(BF16)
            hidden_slope_ref[expert, half * LANES : (half + 1) * LANES, :] = slope
        weights = weight_ref[expert, 2 * D_IN : 2 * D_IN + H1, :]
        bias = column(bias_line(expert, (6, 7, 8)))
        value, slope = silu_parts(matmul_tn(weights, hidden_ref[expert]) + bias)
        output_ref[expert] = value
        output_slope_ref[expert] = slope
        for task in range(TASKS):
            mixed_ref[task * H2 : (task + 1) * H2, :] += (
                gates_ref[pl.ds(task * experts + expert, 1), :] * value
            )
        return carry

    lax.fori_loop(0, experts, forward, 0, unroll=2)

    tower_bias = column(vector_ref[0:1, :])
    head_w = column(vector_ref[1:2, :])
    tower = tower_ref[...]
    act_sums = []
    grad_sums = []
    head_sums = []
    for task in range(TASKS):
        units = slice(task * TOWER, (task + 1) * TOWER)
        outs = slice(task * H2, (task + 1) * H2)
        mixed = mixed_ref[outs, :]
        mixed_low = mixed.astype(BF16)
        tower_part = tower[:, units]
        act, slope = silu_parts(matmul_tn(tower_part, mixed_low) + tower_bias[units])
        score = jnp.sum(act * head_w[units], axis=0, keepdims=True) + head_b_ref[task]
        target = label_ref[task : task + 1, :].astype(F32)
        score_grad = (jax.nn.sigmoid(score) - target) * scale
        tower_grad = (score_grad * head_w[units] * slope).astype(BF16)
        act_sums.append(jnp.sum(score_grad * act, axis=1, keepdims=True))
        grad_sums.append(jnp.sum(tower_grad.astype(F32), axis=1, keepdims=True))
        head_sums.append(jnp.sum(score_grad, axis=1, keepdims=True))
        put_shared(slice(0, H2), units, matmul_nt(mixed_low, tower_grad))
        mixed_grad = matmul(tower_part, tower_grad).astype(BF16).astype(F32)
        mixed_grad_ref[outs, :] = mixed_grad
        dot_ref[task : task + 1, :] = jnp.sum(mixed_grad * mixed, axis=0, keepdims=True)
    column_sums = jnp.concatenate(
        [
            jnp.broadcast_to(jnp.concatenate(sums, axis=0), (LANES, LANES))
            for sums in (act_sums, grad_sums)
        ],
        axis=1,
    )
    put_shared(slice(H2, H2 + 8), whole, jnp.transpose(column_sums[:, :LANES])[0:8])
    put_shared(slice(H2 + 8, H2 + 16), whole, jnp.transpose(column_sums[:, LANES:])[0:8])
    head_line = jnp.zeros((8, LANES), F32)
    for task in range(TASKS):
        head_line = jnp.where(iota((8, LANES), 1) == task, head_sums[task], head_line)
    put_shared(slice(H2 + 16, H2 + 24), whole, head_line)

    input_ref[...] = jnp.zeros_like(input_ref)
    ones = jnp.ones((BIAS_ROWS, width), BF16)

    def backward(expert, carry):
        value = output_ref[expert]
        grad = jnp.zeros((H2, width), F32)
        for task in range(TASKS):
            mixed_grad = mixed_grad_ref[task * H2 : (task + 1) * H2, :]
            gate = gates_ref[pl.ds(task * experts + expert, 1), :]
            grad = grad + gate * mixed_grad
            along = jnp.sum(mixed_grad * value, axis=0, keepdims=True)
            logit_ref[pl.ds(task * experts + expert, 1), :] = gate * (
                along - dot_ref[task : task + 1, :]
            )
        output_grad = (grad * output_slope_ref[expert]).astype(BF16)
        hidden = hidden_ref[expert]
        put_weight(expert, slice(2 * D_IN, 2 * D_IN + H1), matmul_nt(hidden, output_grad))
        weights = weight_ref[expert, 2 * D_IN : 2 * D_IN + H1, :]
        hidden_grad = (matmul(weights, output_grad) * hidden_slope_ref[expert]).astype(BF16)
        turned = turned_ref[...]
        sums = []
        for half in range(H1 // LANES):
            half_grad = hidden_grad[half * LANES : (half + 1) * LANES]
            put_weight(
                expert, slice(half * D_IN, (half + 1) * D_IN), matmul_nt(turned, half_grad)
            )
            weights = weight_ref[expert, half * D_IN : (half + 1) * D_IN, :]
            input_ref[...] += matmul(weights, half_grad)
            sums.append(matmul_nt(ones, half_grad)[0:1])
        sums.append(matmul_nt(ones, output_grad)[0:1])
        sums.append(jnp.zeros((8 - 3, LANES), F32))
        grad_bias_ref[expert] = jnp.concatenate(sums, axis=0)
        return carry

    lax.fori_loop(0, experts, backward, 0, unroll=2)

    logit_grad = logit_ref[...].astype(BF16)
    gate_grad = matmul_nt(logit_grad, turned_ref[...])
    gate_base = H2 + 24
    pairs = TASKS * experts
    for lane_block in range(D_IN // LANES):
        put_shared(
            slice(gate_base + lane_block * pairs, gate_base + (lane_block + 1) * pairs),
            whole,
            gate_grad[:, lane_block * LANES : (lane_block + 1) * LANES],
        )
    low_ref[...] = (input_ref[...] + matmul_tn(gate_ref[...], logit_grad)).astype(BF16)
    bottom_grad = low_ref[EMB_WIDTH:, :]
    dense_base = gate_base + D_IN // LANES * pairs
    grad_dense_w = jnp.concatenate(
        [matmul_nt(dense, bottom_grad), jnp.zeros((DENSE, LANES - BOTTOM), F32)], axis=1
    )
    put_shared(
        slice(dense_base, dense_base + 16),
        whole,
        jnp.concatenate([grad_dense_w, jnp.zeros((16 - DENSE, LANES), F32)], axis=0),
    )
    grad_dense_ref[...] = matmul(dense_w, bottom_grad)

    def clear(step, carry):
        wide_ref[pl.ds(aligned(8 + step * LANES, 8), LANES), :] = jnp.zeros((LANES, LANES), F32)
        return carry

    chunk_rows = left_ref.shape[0] // FIELDS

    def permute(chunk, words):
        block = lax.div(chunk * chunk_rows, LANES)
        first = chunk * chunk_rows - block * LANES
        span = pl.ds(aligned(block * LANES, LANES), LANES)

        @pl.when(first == 0)
        def _():
            for field in range(FIELDS):
                piece = low_ref[field * EMB : (field + 1) * EMB, span]
                tiled_ref[field] = matmul_nt(eye, jnp.concatenate([piece] * GROUPS, axis=0))

        for step in range(chunk_rows // 8):
            start_row = aligned(first + step * 8, 8)
            for field in range(FIELDS):
                tile = tiled_ref[field, pl.ds(start_row, 8), :]
                for k in range(8):
                    start = words[(step * 8 + k) * FIELDS + field]
                    pltpu.store(wide_ref.at[pl.ds(start, 8), :], tile, mask=lines[k])

    def permute_place(at):
        each = part_rows // chunk_rows
        part = lax.div(at, each)
        return part * (out_ref.shape[0] // PARTS) + (at - part * each) * (chunk_rows * FIELDS)

    word_stream(
        out_ref,
        buffers,
        sems,
        permute_place,
        width // chunk_rows,
        permute,
        lambda: lax.fori_loop(0, slot_blocks, clear, 0, unroll=2),
    )

    def merge(block, carry):
        halves = []
        for half in range(2):
            piece = jnp.zeros((8, LANES), F32)
            for group in range(GROUPS):
                start = aligned(block * LANES + group * 16 + (half + 1) * 8, 8)
                piece = jnp.where(lanes[group], wide_ref[pl.ds(start, 8), :], piece)
            halves.append(piece)
        start = aligned(block * 16, 16)
        sent_ref[pl.ds(start, 16), :] = jnp.concatenate(halves, axis=0).astype(BF16)
        return carry

    lax.fori_loop(0, slot_blocks, merge, 0, unroll=4 if slot_blocks % 4 == 0 else 1)
    each = sent_ref.shape[0] // owners
    for one in range(owners):
        sent_refs[one][...] = sent_ref[one * each : (one + 1) * each, :]


def add_kernel(owners, packed, table_lanes, index_ref, request_ref, asked_ref, *refs):
    received_refs = refs[:owners]
    table_refs = refs[owners : owners + 2 * TABLE_CHUNKS]
    (
        received_ref,
        left_grad_ref,
        right_grad_ref,
        left_ref,
        right_ref,
        sems,
        *sums,
    ) = refs[owners + 2 * TABLE_CHUNKS :]
    rows = sums[0].shape[0] - 16
    core, batch = index_ref[0], index_ref[1]
    sources = received_ref.shape[0] // packed
    chunks = packed // 16
    lines, _ = masks()
    eye = identity()
    own_group = lax.shift_right_logical(iota((1, LANES), 1), 4)
    from_lane = iota((LANES, 2 * LANES), 0)
    to_lane = iota((LANES, 2 * LANES), 1)
    spread_names = []
    spread_grads = []
    for pair in range(GROUPS // 2):
        group = pair * 2 + lax.shift_right_logical(to_lane, 7)
        spread_names.append(
            jnp.where(lax.shift_right_logical(from_lane, 4) == group, 1.0, 0.0).astype(BF16)
        )
        wanted = group * EMB + (to_lane & (EMB - 1))
        spread_grads.append(jnp.where(from_lane == wanted, 1.0, 0.0).astype(BF16))

    def place(source):
        distance = lax.div(source, PARTS)
        return (distance ^ batch) * PARTS + source - distance * PARTS

    def spread(source, grad_ref):
        def step(first, count, pair):
            asked = asked_ref[pl.ds(place(source) * chunks + first, count), :]
            names = (own_group - lax.shift_right_logical(asked, table_lanes)) & (GROUPS - 1)
            start = aligned(source * packed + first * 16, 16)
            grads = received_ref[pl.ds(start, count * 16), :]
            lane_group = lax.shift_right_logical(iota((count * 16, LANES), 1), 4).astype(F32)
            wide_names = matmul(slot_lines(names.astype(F32)), spread_names[pair])
            wide_grads = matmul(grads, spread_grads[pair])
            for side in range(2):
                half = slice(side * LANES, (side + 1) * LANES)
                masked = jnp.where(wide_names[:, half] == lane_group, wide_grads[:, half], 0.0)
                for chunk in range(count):
                    start = (first + chunk) * LANES + (pair * 2 + side) * 16
                    grad_ref[start : start + 16, :] = masked[chunk * 16 : (chunk + 1) * 16]

        return [
            functools.partial(step, first, min(4, chunks - first), pair)
            for first in range(0, chunks, 4)
            for pair in range(GROUPS // 2)
        ]

    def clear(step, carry):
        for total in sums:
            total[pl.ds(aligned(8 + step * LANES, 8), LANES), :] = jnp.zeros((LANES, LANES), F32)
        return carry

    def before():
        for total in sums:
            total[0:8, :] = jnp.zeros((8, LANES), F32)
            total[8 + rows : 16 + rows, :] = jnp.zeros((8, LANES), F32)
        lax.fori_loop(0, rows // LANES, clear, 0)
        gather_blocks(received_refs, received_ref)
        for one in spread(0, left_grad_ref):
            one()

    def process(source, words):
        now, later = left_grad_ref, right_grad_ref
        if words is right_ref:
            now, later = later, now
        steps = spread(jnp.minimum(source + 1, sources - 1), later)
        rows = GROUPS * packed // 8
        for row in range(rows):
            if row * len(steps) // rows != (row - 1) * len(steps) // rows:
                steps[row * len(steps) // rows]()
            grads = now[row * 8 : (row + 1) * 8, :]
            for k in range(8):
                place = pl.ds(words[row * 8 + k], 8)
                total = sums[k % STREAMS]
                pltpu.store(total.at[place, :], total[place, :] + grads, mask=lines[k])

    size = GROUPS * packed
    word_stream(
        request_ref,
        (left_ref, right_ref),
        sems,
        lambda at: place(at) * size,
        sources,
        process,
        before,
    )

    def finish(kept, block, carry):
        start = aligned(8 + block * LANES, 8)
        total = functools.reduce(jnp.add, [one[pl.ds(start, LANES), :] for one in sums])
        turned = matmul_nt(eye, total.astype(BF16)).astype(BF16)
        each = GROUPS // (2 * TABLE_CHUNKS)
        for group in range(GROUPS):
            half, column = divmod(group, GROUPS // 2)
            chunk, column = divmod(column, each)
            table_ref = table_refs[chunk + (0 if half == kept else TABLE_CHUNKS)]
            column = aligned(column * rows + block * LANES, LANES)
            table_ref[:, pl.ds(column, LANES)] = turned[group * EMB : (group + 1) * EMB]
        return carry

    for kept in range(2):

        @pl.when(core == kept)
        def _():
            lax.fori_loop(0, rows // LANES, functools.partial(finish, kept), 0, unroll=8)


def unpack_kernel(weight_piece, extra_piece, pairs, piece_ref, *refs):
    (
        dense_w_ref,
        gate_ref,
        hidden_w_ref,
        hidden_b_ref,
        output_w_ref,
        output_b_ref,
        tower_w_ref,
        tower_b_ref,
        head_w_ref,
        head_b_ref,
        weight_ref,
        extra_ref,
    ) = refs
    for owner in range(piece_ref.shape[0]):
        weight_ref[owner * weight_piece : (owner + 1) * weight_piece, :] = piece_ref[
            owner, :weight_piece, :
        ].astype(F32)
        high = piece_ref[owner, weight_piece : weight_piece + extra_piece, :].astype(F32)
        low = piece_ref[owner, weight_piece + extra_piece :, :].astype(F32)
        extra_ref[owner * extra_piece : (owner + 1) * extra_piece, :] = high + low
    gate_rows = D_IN // LANES * pairs
    small = H2 + gate_rows + 16

    def small_line(row):
        return extra_ref[small + row : small + row + 1, :] + extra_ref[small + 6 + row : small + 7 + row, :]

    for half in range(H1 // LANES):
        span = slice(half * LANES, (half + 1) * LANES)
        hidden_w_ref[0, :, span] = weight_ref[half * D_IN : (half + 1) * D_IN, :]
        hidden_b_ref[:, span] = small_line(3 + half)
    output_w_ref[0] = weight_ref[2 * D_IN : GRAD_ROWS, :]
    output_b_ref[...] = small_line(5)
    tower_w_ref[...] = extra_ref[:H2, :]
    head_w_ref[...] = small_line(0)
    tower_b_ref[...] = small_line(1)
    head_b_ref[...] = small_line(2)[:, :TASKS]
    for block in range(D_IN // LANES):
        gate_ref[:, block * LANES : (block + 1) * LANES] = extra_ref[
            H2 + block * pairs : H2 + (block + 1) * pairs, :
        ]
    dense_w_ref[...] = extra_ref[H2 + gate_rows : H2 + gate_rows + DENSE, :BOTTOM]


SMEM = pl.BlockSpec(memory_space=pltpu.SMEM)
VMEM = pl.BlockSpec(memory_space=pltpu.VMEM)
ANY = pl.BlockSpec(memory_space=pl.ANY)


def call(kernel, outs, ins, scratch, name, micros, vmem=16):
    return pl.pallas_call(
        kernel,
        out_shape=outs,
        in_specs=ins,
        out_specs=jax.tree.map(lambda _: VMEM, outs),
        scratch_shapes=scratch,
        name=name,
        cost_estimate=pl.CostEstimate(
            flops=int(micros * 1.15e9), bytes_accessed=int(micros * 3e6), transcendentals=0
        ),
        compiler_params=pltpu.CompilerParams(vmem_limit_bytes=vmem << 20),
    )


def shards(
    emb_table,
    dense_feats,
    dense_w,
    gate_w,
    hidden_w,
    hidden_b,
    output_w,
    output_b,
    tower_w,
    tower_b,
    head_w,
    head_b,
    row_owner,
    local_row,
    labels,
):
    owners = lax.axis_size("batch")
    experts = lax.axis_size("expert")
    expert_index = lax.axis_index("expert")
    core = expert_index & 1
    row_total = dense_feats.shape[1]
    part_rows = row_total // PARTS
    lookups = row_total * FIELDS
    part_lookups = lookups // PARTS
    capacity = 2 * part_lookups // owners
    packed = -(-capacity // (GROUPS * 16)) * 16
    table_rows = emb_table.shape[0]
    table_packed = table_rows // GROUPS
    table_lanes = table_packed.bit_length() - 1
    scale = 1.0 / math.sqrt(row_total * owners * experts)
    slots = owners * PARTS * GROUPS * packed
    part_slots = owners * packed
    lookup_rows = lookups // LANES
    list_part = -(-lookup_rows // (PARTS * 24)) * 24
    list_rows = list_part * PARTS

    def tie(*values):
        return lax.optimization_barrier(values)

    def exchange(values, axis):
        return lax.all_to_all(values, axis, split_axis=0, concat_axis=0, tiled=True)

    def swap(values, axis, bits):
        size = lax.axis_size(axis)
        return lax.ppermute(values, axis, [(one, one ^ bits) for one in range(size)])

    def swap_all(blocks):
        return [blocks[0]] + [swap(blocks[bits], "batch", bits) for bits in range(1, owners)]

    owner_list = row_owner.reshape(lookup_rows, LANES)
    local_list = local_row.reshape(lookup_rows, LANES)
    slot_rows = slots // LANES
    list_shape = jax.ShapeDtypeStruct((list_rows, LANES), I32)
    batch_index = lax.axis_index("batch").reshape(1)
    requests, back, out = call(
        functools.partial(route_kernel, owners, part_lookups, packed, table_lanes),
        (jax.ShapeDtypeStruct((slot_rows, LANES), I32), list_shape, list_shape),
        [SMEM, VMEM, VMEM],
        [pltpu.VMEM((list_rows, LANES), I32)] * 3 + [pltpu.VMEM((PARTS, slot_rows // PARTS, 2 * LANES), F32)],
        "route",
        9,
    )(batch_index, owner_list, local_list)
    asked = exchange(requests.reshape(owners, slots // owners), "batch")
    asked = asked.reshape(slot_rows, LANES)
    offset = 8 - (jnp.arange(LANES, dtype=I32) & 7)
    words = ((asked & (table_packed - 1)) + offset).reshape(-1)
    back = back.reshape(-1)
    out = out.reshape(-1)

    hidden_b, out = tie(hidden_b, out)
    table, weights = call(
        pack_kernel,
        (
            pltpu.VMEM((table_packed + 16, LANES), F32),
            jax.ShapeDtypeStruct((WEIGHT_ROWS, LANES), BF16),
        ),
        [VMEM] * 5,
        [],
        "pack",
        5,
    )(emb_table.T, hidden_w, output_w, hidden_b, output_b)
    table = pltpu.with_memory_space_constraint(table, pltpu.VMEM)
    weights = lax.all_gather(weights, "expert", axis=0, tiled=False)

    slot_words = [pltpu.SMEM((GROUPS * packed,), I32)] * 2 + [pltpu.SemaphoreType.DMA((2,))]
    row_words = [pltpu.SMEM((CHUNK_ROWS * FIELDS,), I32)] * 2 + [pltpu.SemaphoreType.DMA((2,))]
    returned = []
    for part in range(PARTS):
        found = call(
            functools.partial(fetch_kernel, owners, part, packed, table_lanes),
            jax.ShapeDtypeStruct((part_slots, LANES), BF16),
            [ANY, VMEM, VMEM],
            [
                pltpu.VMEM((part_slots, LANES), F32),
                pltpu.VMEM((GROUPS * packed, LANES), F32),
            ]
            + slot_words,
            "fetch",
            24 // PARTS,
        )(words, asked, table)
        found = exchange(found.reshape(owners, packed, LANES), "batch")
        returned.append(found.reshape(part_slots, LANES))
    early = []
    for part in range(PARTS - 1):
        early.append(
            call(
                functools.partial(unpermute_kernel, part, part_rows),
                jax.ShapeDtypeStruct((part_rows, D_IN), BF16),
                [ANY, VMEM],
                [pltpu.VMEM((GROUPS * part_slots + 16, LANES), F32), *row_words],
                "unpermute",
                15,
            )(back, returned[part])
        )

    pairs = TASKS * experts
    shared_rows = H2 + 24 + D_IN // LANES * pairs + 16
    vectors = jnp.stack([tower_b, head_w])
    *sent, grad_dense, grad_weight, grad_bias, grad_shared = call(
        functools.partial(dense_kernel, owners, part_rows, experts, scale),
        (
            *[jax.ShapeDtypeStruct((PARTS * packed, LANES), BF16)] * owners,
            jax.ShapeDtypeStruct((DENSE, row_total), F32),
            jax.ShapeDtypeStruct((experts, GRAD_ROWS, LANES), BF16),
            jax.ShapeDtypeStruct((experts, 8, LANES), F32),
            jax.ShapeDtypeStruct((shared_rows, LANES), F32),
        ),
        [ANY, ANY] + [VMEM] * 7 + [SMEM] + [VMEM] * PARTS,
        [
            pltpu.VMEM((slots + 16, LANES), F32),
            pltpu.VMEM((row_total, D_IN), BF16),
            pltpu.VMEM((D_IN, row_total), BF16),
            pltpu.VMEM((experts, H1, row_total), BF16),
            pltpu.VMEM((experts, H1, row_total), F32),
            pltpu.VMEM((experts, H2, row_total), F32),
            pltpu.VMEM((experts, H2, row_total), F32),
            pltpu.VMEM((pairs, row_total), F32),
            pltpu.VMEM((TASKS * H2, row_total), F32),
            pltpu.VMEM((TASKS * H2, row_total), F32),
            pltpu.VMEM((8, row_total), F32),
            pltpu.VMEM((pairs, row_total), F32),
            pltpu.VMEM((D_IN, row_total), F32),
            pltpu.VMEM((D_IN, row_total), BF16),
            pltpu.VMEM((FIELDS, LANES, LANES), F32),
            *row_words,
            pltpu.VMEM((PARTS * part_slots, LANES), BF16),
        ],
        "dense",
        45,
        56,
    )(
        back,
        out,
        returned[-1],
        weights,
        gate_w.T,
        dense_feats,
        dense_w,
        tower_w,
        vectors,
        head_b,
        labels,
        *early,
    )
    received = swap_all(sent)

    def split(values):
        high = lax.reduce_precision(values, exponent_bits=8, mantissa_bits=7)
        return high.astype(BF16), (values - high).astype(BF16)

    far = owners // 2
    received[far], grad_weight, grad_bias, grad_shared = tie(
        received[far], grad_weight, grad_bias, grad_shared
    )

    def spread_rows(values, piece):
        rows = values.shape[1]
        values = jnp.pad(values, ((0, 0), (0, piece * owners - rows), (0, 0)))
        return values.reshape(experts, owners, piece, LANES).transpose(1, 0, 2, 3)

    large = jnp.concatenate([grad_shared[:H2], grad_shared[H2 + 24 :]], axis=0).astype(BF16)
    small = jnp.concatenate([grad_shared[H2 + 8 * row : H2 + 8 * row + 1] for row in range(3)])
    small = jnp.concatenate(
        [jnp.broadcast_to(small[None], (experts, 3, LANES)), grad_bias[:, :3]], axis=1
    )
    extra = jnp.concatenate(
        [jnp.broadcast_to(large[None], (experts, *large.shape)), *split(small)], axis=1
    )
    weight_piece = -(-GRAD_ROWS // (16 * owners)) * 16
    extra_piece = -(-extra.shape[1] // (16 * owners)) * 16
    piece_rows = weight_piece + extra_piece
    pieces = jnp.concatenate(
        [spread_rows(grad_weight, weight_piece), spread_rows(extra, extra_piece)], axis=2
    )
    late = owners - 2
    *received[:late], pieces = tie(*received[:late], pieces)
    pieces = exchange(pieces.reshape(owners * experts, piece_rows, LANES), ("batch", "expert"))

    columns = table_rows // 2 // TABLE_CHUNKS
    table_part = call(
        functools.partial(add_kernel, owners, packed, table_lanes),
        (jax.ShapeDtypeStruct((EMB, columns), BF16),) * (2 * TABLE_CHUNKS),
        [SMEM, ANY, VMEM] + [VMEM] * owners,
        [pltpu.VMEM((PARTS * part_slots, LANES), BF16)]
        + [pltpu.VMEM((GROUPS * packed, LANES), F32)] * 2
        + slot_words
        + [pltpu.VMEM((table_packed + 16, LANES), F32)] * STREAMS,
        "add",
        60,
        48,
    )(jnp.concatenate([core.reshape(1), batch_index]), words, asked, *received)

    def add_low(left, right):
        return (left.astype(F32) + right.astype(F32)).astype(BF16)

    *table_part, pieces = tie(*table_part, pieces)
    kept = [
        add_low(one, swap(other, "expert", 1))
        for one, other in zip(table_part[:TABLE_CHUNKS], table_part[TABLE_CHUNKS:])
    ]
    *kept, pieces = tie(*kept, pieces)
    over = [swap(one, "expert", 2) for one in kept]
    sums = jnp.sum(pieces.astype(F32), axis=0)
    piece = jnp.concatenate([sums[:weight_piece].astype(BF16), *split(sums[weight_piece:])], axis=0)
    pieces = exchange(jnp.broadcast_to(piece[None], (owners, *piece.shape)), "batch")
    bit = 2
    while bit < experts:
        kept = [add_low(one, other) for one, other in zip(kept, over)]
        bit *= 2
        if bit < experts:
            over = [swap(one, "expert", bit) for one in kept]
    small = call(
        functools.partial(unpack_kernel, weight_piece, extra_piece, pairs),
        tuple(
            jax.ShapeDtypeStruct(shape, F32)
            for shape in (
                (DENSE, BOTTOM),
                (pairs, D_IN),
                (1, D_IN, H1),
                (1, H1),
                (1, H1, H2),
                (1, H2),
                (H2, TASKS * TOWER),
                (1, TASKS * TOWER),
                (1, TASKS * TOWER),
                (1, TASKS),
            )
        ),
        [VMEM],
        [
            pltpu.VMEM((owners * weight_piece, LANES), F32),
            pltpu.VMEM((owners * extra_piece, LANES), F32),
        ],
        "unpack",
        3,
    )(pieces)
    others = [swap(one, "expert", 1) for one in kept]
    *others, small = tie(*others, small)
    lower = [jnp.where(core == 0, one, other) for one, other in zip(kept, others)]
    upper = [jnp.where(core == 0, other, one) for one, other in zip(kept, others)]
    table_total = jnp.concatenate(lower + upper, axis=1).astype(F32).T
    grad_dense_w, gate, hidden, hidden_bias, output, output_bias, tower, tower_bias, head, head_bias = (
        small
    )
    return (
        table_total,
        grad_dense,
        grad_dense_w,
        gate.T,
        hidden,
        hidden_bias,
        output,
        output_bias,
        tower,
        tower_bias.reshape(-1),
        head.reshape(-1),
        head_bias.reshape(-1),
    )


def solution(mesh):
    in_specs = (
        P("batch", None),
        P(None, ("batch", "expert")),
        P(),
        P(),
        P("expert", None, None),
        P("expert", None),
        P("expert", None, None),
        P("expert", None),
        P(),
        P(),
        P(),
        P(),
        P(("batch", "expert"), None),
        P(("batch", "expert")),
        P(None, ("batch", "expert")),
    )
    out_specs = (
        P("batch", None),
        P(None, ("batch", "expert")),
        P(),
        P(),
        P("expert", None, None),
        P("expert", None),
        P("expert", None, None),
        P("expert", None),
        P(),
        P(),
        P(),
        P(),
    )
    return jax.shard_map(shards, mesh=mesh, in_specs=in_specs, out_specs=out_specs, check_vma=False)
```

```python
import functools
import math

import jax
import jax.numpy as jnp
from jax import lax
from jax.experimental import pallas as pl
from jax.experimental.pallas import tpu as pltpu
from jax.sharding import PartitionSpec as P

FIELDS = 26
EMB = 16
DENSE = 13
BOTTOM = 96
D_IN = 512
H1 = 256
H2 = 128
TOWER = 64
TASKS = 2
LANES = 128
GROUPS = LANES // EMB
EMB_WIDTH = FIELDS * EMB
BIAS_ROWS = 16
GRAD_ROWS = 2 * D_IN + H1
WEIGHT_ROWS = GRAD_ROWS + BIAS_ROWS
STREAMS = 8
PARTS = 2
CHUNK_ROWS = 64
SLOT_BUFFERS = 4
ROW_BUFFERS = 5
TABLE_CHUNKS = 2

F32 = jnp.float32
BF16 = jnp.bfloat16
I32 = jnp.int32


def iota(shape, axis):
    return lax.broadcasted_iota(I32, shape, axis)


def matmul(a, b):
    return lax.dot_general(a, b, (((1,), (0,)), ((), ())), preferred_element_type=F32)


def matmul_nt(a, b):
    return lax.dot_general(a, b, (((1,), (1,)), ((), ())), preferred_element_type=F32)


def matmul_tn(a, b):
    return lax.dot_general(a, b, (((0,), (0,)), ((), ())), preferred_element_type=F32)


def identity():
    return (iota((LANES, LANES), 0) == iota((LANES, LANES), 1)).astype(BF16)


def aligned(value, step):
    return pl.multiple_of(value, step)


def silu_parts(values):
    sig = jax.nn.sigmoid(values)
    return values * sig, sig * (1.0 + values * (1.0 - sig))


def route_kernel(
    owners, part_lookups, packed, table_lanes, batch_ref, owner_ref, local_ref, request_ref,
    back_ref, out_ref, high_ref, low_ref, value_ref, total_ref
):
    rows = high_ref.shape[0]
    part_rows = rows // PARTS
    filled = part_lookups // LANES
    slot_rows = request_ref.shape[0]
    shape = (rows, LANES)
    high_ref[...] = jnp.full(shape, -1, I32)
    low_ref[...] = jnp.zeros(shape, I32)
    for part in range(PARTS):
        lines = slice(part * part_rows, part * part_rows + filled)
        taken = slice(part * filled, (part + 1) * filled)
        high_ref[lines, :] = owner_ref[taken, :]
        low_ref[lines, :] = local_ref[taken, :]
    owner = high_ref[...]
    local = low_ref[...]
    row_id = iota(shape, 0)
    tri = (iota((LANES, LANES), 0) <= iota((LANES, LANES), 1)).astype(BF16)
    ones = jnp.ones((LANES, LANES), BF16)
    before = (iota((part_rows, part_rows), 1) < iota((part_rows, part_rows), 0)).astype(BF16)
    ranks = []
    for part in range(PARTS):
        own = owner[part * part_rows : (part + 1) * part_rows]
        rank = jnp.zeros((part_rows, LANES), F32)
        for one in range(owners):
            hit = own == one
            hits = jnp.where(hit, 1.0, 0.0).astype(BF16)
            upto = matmul(hits, tri)
            ahead = matmul(before, matmul(hits, ones).astype(BF16))
            rank = jnp.where(hit, upto + ahead - 1.0, rank)
        ranks.append(rank)
    rank = jnp.concatenate(ranks, axis=0)
    part_id = jnp.zeros(shape, I32)
    for part in range(1, PARTS):
        part_id = part_id + jnp.where(row_id >= part * part_rows, 1, 0)
    rank = rank.astype(I32)
    group = jnp.zeros(shape, I32)
    for step in range(1, GROUPS):
        group = group + jnp.where(rank >= step * packed, 1, 0)
    place = rank - group * packed
    held = jnp.maximum(owner, 0)
    chunks = packed // 16
    chunk = lax.shift_right_logical(place, 4)
    block = (held * PARTS + part_id) * chunks + chunk
    inside = group * 16 + (place & 15)
    table_group = lax.shift_right_logical(local, table_lanes)
    table_row = local & ((1 << table_lanes) - 1)
    high_ref[...] = jnp.where(owner < 0, -1, held * chunks + chunk)
    low_ref[...] = inside
    value_ref[...] = table_row + (((group - table_group) & (GROUPS - 1)) << table_lanes)
    lookup = (row_id - part_id * part_rows) * LANES + iota(shape, 1)
    quotient = jnp.floor((lookup.astype(F32) + 0.5) * (1.0 / FIELDS)).astype(I32)
    field_group = (lookup - quotient * FIELDS) & (GROUPS - 1)
    offset = 8 - (quotient & 7)
    turn = (field_group - group) & (GROUPS - 1)
    back_ref[...] = (turn * owners + held) * packed + place + offset
    away = ((held ^ batch_ref[0]) - held) * (PARTS * GROUPS * packed)
    out_ref[...] = block * LANES + inside + offset + away
    total_ref[...] = jnp.zeros_like(total_ref)
    own_rows = slot_rows // PARTS

    def gather_requests(part, step, carry):
        base = aligned(part * part_rows + step * 8, 8)
        high = high_ref[pl.ds(base, 8), :]
        low = low_ref[pl.ds(base, 8), :]
        values = value_ref[pl.ds(base, 8), :]
        upper = lax.shift_right_logical(values, 8).astype(F32)
        lower = (values & 255).astype(F32)
        at_high = []
        at_low = []
        for k in range(8):
            line = slice(k, k + 1)
            at_high.append(jnp.where(iota((own_rows, LANES), 0) == high[line], 1.0, 0.0).astype(BF16))
            same = iota((LANES, LANES), 0) == low[line]
            at_low.append(
                jnp.concatenate(
                    [jnp.where(same, upper[line], 0.0), jnp.where(same, lower[line], 0.0)], axis=0
                ).astype(BF16)
            )
        total_ref[part] += matmul_nt(
            jnp.concatenate(at_high, axis=1), jnp.concatenate(at_low, axis=1)
        )
        return carry

    for part in range(PARTS):
        lax.fori_loop(0, part_rows // 8, functools.partial(gather_requests, part), 0, unroll=3)
        total = (total_ref[part, :, :LANES] * 256.0 + total_ref[part, :, LANES:]).astype(I32)
        for one in range(owners):
            start = (one * PARTS + part) * chunks
            request_ref[start : start + chunks, :] = total[one * chunks : (one + 1) * chunks]


def pack_kernel(
    table_ref, hidden_w_ref, output_w_ref, hidden_b_ref, output_b_ref, packed_ref, weight_ref
):
    lines = []
    for values in (hidden_b_ref[:, :LANES], hidden_b_ref[:, LANES:], output_b_ref[...]):
        for _ in range(3):
            term = values.astype(BF16).astype(F32)
            lines.append(term)
            values = values - term
    lines.append(jnp.zeros((BIAS_ROWS - len(lines), LANES), F32))
    for half in range(H1 // LANES):
        weight_ref[half * D_IN : (half + 1) * D_IN, :] = hidden_w_ref[
            0, :, half * LANES : (half + 1) * LANES
        ]
    weight_ref[2 * D_IN : 2 * D_IN + H1, :] = output_w_ref[0]
    weight_ref[2 * D_IN + H1 :, :] = jnp.concatenate(lines, axis=0).astype(BF16)
    rows = table_ref.shape[1] // GROUPS
    eye = identity()

    def step(block, carry):
        pieces = []
        for group in range(GROUPS):
            start = aligned(group * rows + block * LANES, LANES)
            pieces.append(table_ref[:, pl.ds(start, LANES)])
        packed_ref[pl.ds(aligned(8 + block * LANES, 8), LANES), :] = matmul_nt(
            eye, jnp.concatenate(pieces, axis=0)
        )
        return carry

    packed_ref[0:8, :] = jnp.zeros((8, LANES), F32)
    packed_ref[8 + rows : 16 + rows, :] = jnp.zeros((8, LANES), F32)

    lax.fori_loop(0, rows // LANES, step, 0, unroll=8)


def masks():
    line = iota((8, LANES), 0)
    group = lax.shift_right_logical(iota((8, LANES), 1), 4)
    return [line == k for k in range(8)], [group == one for one in range(GROUPS)]


def turn_copies(rows_ref, wide_ref):
    rows = rows_ref.shape[0]
    half = GROUPS // 2
    from_lane = iota((LANES, half * LANES), 0)
    to_lane = iota((LANES, half * LANES), 1)
    turn = (lax.shift_right_logical(to_lane, 7) + half) * EMB
    turns = jnp.where(((from_lane + turn - to_lane) & (LANES - 1)) == 0, 1.0, 0.0).astype(BF16)

    def step(block, carry):
        start = aligned(block * LANES, LANES)
        piece = rows_ref[pl.ds(start, LANES), :]
        moved = matmul(piece, turns)
        piece = piece.astype(F32)
        for turn in range(GROUPS):
            if turn >= half:
                one = moved[:, (turn - half) * LANES : (turn - half + 1) * LANES]
            else:
                one = pltpu.roll(piece, turn * EMB, 1) if turn else piece
            wide_ref[pl.ds(aligned(8 + turn * rows + start, 8), LANES), :] = one
        return carry

    blocks = rows // LANES
    unroll = [count for count in (4, 3, 2, 1) if blocks % count == 0][0]
    lax.fori_loop(0, blocks, step, 0, unroll=unroll)


def assemble(wide_ref, word, groups, lines, lanes):
    block = jnp.zeros((8, LANES), F32)
    for place, group in groups:
        piece = wide_ref[pl.ds(word(0, place), 8), :]
        for k in range(1, 8):
            piece = jnp.where(lines[k], wide_ref[pl.ds(word(k, place), 8), :], piece)
        block = jnp.where(lanes[group], piece, block)
    return block


def word_stream(word_ref, buffers, sems, place, count, process, before=None):
    slots = len(buffers)
    size = buffers[0].shape[0]

    def copy(at, slot):
        start = aligned(place(at), LANES)
        return pltpu.make_async_copy(
            word_ref.at[pl.ds(start, size)], buffers[slot], sems.at[slot]
        )

    for slot in range(min(slots, count)):
        copy(slot, slot).start()
    if before is not None:
        before()

    def step(turn, carry):
        for slot in range(slots):
            at = turn * slots + slot
            copy(at, slot).wait()
            process(at, buffers[slot], slot)

            @pl.when(at + slots < count)
            def _():
                copy(at + slots, slot).start()

        return carry

    lax.fori_loop(0, count // slots, step, 0)
    for slot in range(count % slots):
        at = count // slots * slots + slot
        copy(at, slot).wait()
        process(at, buffers[slot], slot)


def slot_lines(numbers):
    own = (iota((16, LANES), 1) & 15) == iota((16, LANES), 0)
    return jnp.concatenate(
        [jnp.where(own, numbers[row : row + 1], 0.0) for row in range(numbers.shape[0])], axis=0
    ).astype(BF16)


def same_group():
    return (
        lax.shift_right_logical(iota((LANES, LANES), 0), 4)
        == lax.shift_right_logical(iota((LANES, LANES), 1), 4)
    ).astype(BF16)


def fetch_kernel(
    owners, part, packed, table_lanes, request_ref, asked_ref, table_ref, found_ref, turn_ref,
    piece_ref, *stream
):
    *buffers, sems = stream
    lines, _ = masks()
    chunks = packed // 16
    within = same_group()
    group = lax.shift_right_logical(iota((8, LANES), 1), 4)
    bits = [(group & (1 << bit)) != 0 for bit in range(3)]

    def make_turns(source, first, count):
        at = (source * PARTS + part) * chunks + first
        numbers = lax.shift_right_logical(asked_ref[pl.ds(at, count), :], table_lanes)
        start = aligned(source * packed + first * 16, 16)
        turn_ref[pl.ds(start, count * 16), :] = matmul(slot_lines(numbers.astype(F32)), within)

    def before():
        make_turns(0, 0, chunks)

    def process(source, words, slot):
        later = jnp.minimum(source + 1, owners - 1)
        for chunk in range(chunks):
            if chunk % 4 == 0:
                make_turns(later, chunk, min(4, chunks - chunk))
            for line in range(LANES):
                base = chunk * LANES + line // 8 * 8
                pltpu.store(
                    piece_ref.at[base : base + 8, :],
                    table_ref[pl.ds(words[chunk * LANES + line], 8), :],
                    mask=lines[line % 8],
                )
            start = aligned(source * packed + chunk * 16, 16)
            turns = turn_ref[pl.ds(start, 16), :]
            halves = []
            for half in range(2):
                mixed = []
                for group in range(GROUPS):
                    base = chunk * LANES + group * 16 + half * 8
                    mixed.append(piece_ref[base : base + 8, :])
                for bit in range(3):
                    mixed = [
                        jnp.where(bits[bit], mixed[(turn + (1 << bit)) % GROUPS], mixed[turn])
                        for turn in range(GROUPS)
                    ]
                wanted = turns[half * 8 : (half + 1) * 8]
                block = mixed[0]
                for turn in range(1, GROUPS):
                    moved = pltpu.roll(mixed[turn], turn * EMB, 1)
                    block = jnp.where(wanted == float(turn), moved, block)
                halves.append(block)
            found_ref[pl.ds(start, 16), :] = jnp.concatenate(halves, axis=0).astype(BF16)

    size = chunks * LANES
    word_stream(
        request_ref,
        buffers,
        sems,
        lambda at: (at * PARTS + part) * size,
        owners,
        process,
        before,
    )


def unpermute(
    part, part_rows, back_ref, returned_ref, feature_ref, first_row, wide_ref, buffers, sems
):
    lines, lanes = masks()
    size = buffers[0].shape[0]
    chunk_rows = size // FIELDS

    def process(chunk, words, slot):
        for block in range(chunk_rows // 16):
            start_row = aligned(first_row + chunk * chunk_rows + block * 16, 16)
            for lane_block in range(D_IN // LANES):
                fields = range(lane_block * GROUPS, min((lane_block + 1) * GROUPS, FIELDS))
                halves = [
                    assemble(
                        wide_ref,
                        lambda k, field, half=half: words[
                            (block * 16 + half * 8 + k) * FIELDS + field
                        ],
                        [(field, field % GROUPS) for field in fields],
                        lines,
                        lanes,
                    )
                    for half in range(2)
                ]
                feature_ref[
                    pl.ds(start_row, 16), lane_block * LANES : (lane_block + 1) * LANES
                ] = jnp.concatenate(halves, axis=0).astype(BF16)

    first = part * back_ref.shape[0] // PARTS
    word_stream(
        back_ref,
        buffers,
        sems,
        lambda at: first + at * size,
        part_rows // chunk_rows,
        process,
        lambda: turn_copies(returned_ref, wide_ref),
    )


def gather_blocks(block_refs, whole_ref):
    rows = block_refs[0].shape[0]
    for one, block_ref in enumerate(block_refs):
        whole_ref[one * rows : (one + 1) * rows, :] = block_ref[...]


def unpermute_kernel(
    part, part_rows, back_ref, returned_ref, feature_ref, wide_ref, *stream
):
    *buffers, sems = stream
    unpermute(
        part,
        part_rows,
        back_ref,
        returned_ref,
        feature_ref,
        0,
        wide_ref,
        buffers,
        sems,
    )


def dense_kernel(
    owners,
    part_rows,
    experts,
    scale,
    back_ref,
    out_ref,
    returned_ref,
    weight_ref,
    gate_ref,
    dense_ref,
    dense_w_ref,
    tower_ref,
    vector_ref,
    head_b_ref,
    label_ref,
    *refs,
):
    early = refs[: PARTS - 1]
    refs = refs[PARTS - 1 :]
    sent_refs = refs[:owners]
    (
        grad_dense_ref,
        grad_weight_ref,
        grad_bias_ref,
        grad_shared_ref,
        wide_ref,
        feature_ref,
        turned_ref,
        hidden_ref,
        hidden_slope_ref,
        output_ref,
        output_slope_ref,
        gates_ref,
        mixed_ref,
        mixed_grad_ref,
        dot_ref,
        logit_ref,
        input_ref,
        low_ref,
        tiled_ref,
        sent_ref,
        *buffers,
        sems,
    ) = refs[owners:]
    width = turned_ref.shape[1]
    blocks = width // LANES
    slot_blocks = sent_ref.shape[0] // 16
    eye = identity()
    lines, lanes = masks()

    def put_weight(expert, cut, value):
        grad_weight_ref[expert, cut, :] = value.astype(BF16)

    def put_shared(rows, cut, value):
        grad_shared_ref[rows, cut] = value

    whole = slice(None)
    for part in range(PARTS - 1):
        feature_ref[part * part_rows : (part + 1) * part_rows, :] = early[part][...]
    unpermute(
        PARTS - 1,
        part_rows,
        back_ref,
        returned_ref,
        feature_ref,
        (PARTS - 1) * part_rows,
        wide_ref,
        buffers,
        sems,
    )

    for lane_block in range(D_IN // LANES):
        for block in range(blocks):
            piece = feature_ref[
                block * LANES : (block + 1) * LANES, lane_block * LANES : (lane_block + 1) * LANES
            ]
            turned_ref[
                lane_block * LANES : (lane_block + 1) * LANES, block * LANES : (block + 1) * LANES
            ] = matmul_nt(eye, piece).astype(BF16)
    dense = dense_ref[...]
    dense_w = dense_w_ref[...]
    turned_ref[EMB_WIDTH:, :] = matmul_tn(dense_w, dense).astype(BF16)

    features = turned_ref[...]
    logits = matmul(gate_ref[...], features)
    for task in range(TASKS):
        part_logits = logits[task * experts : (task + 1) * experts]
        powers = jnp.exp(part_logits - jnp.max(part_logits, axis=0, keepdims=True))
        gates_ref[task * experts : (task + 1) * experts, :] = powers / jnp.sum(
            powers, axis=0, keepdims=True
        )

    mixed_ref[...] = jnp.zeros_like(mixed_ref)

    def column(line):
        tall = jnp.transpose(jnp.broadcast_to(line, (LANES, LANES)))
        return jnp.concatenate([tall] * blocks, axis=1)

    def bias_line(expert, rows):
        lines = [weight_ref[expert, 2 * D_IN + H1 :, :].astype(F32)[row : row + 1] for row in rows]
        return functools.reduce(jnp.add, lines)

    def forward(expert, carry):
        turned = turned_ref[...]
        for half in range(H1 // LANES):
            weights = weight_ref[expert, half * D_IN : (half + 1) * D_IN, :]
            bias = column(bias_line(expert, range(half * 3, half * 3 + 3)))
            value, slope = silu_parts(matmul_tn(weights, turned) + bias)
            hidden_ref[expert, half * LANES : (half + 1) * LANES, :] = value.astype(BF16)
            hidden_slope_ref[expert, half * LANES : (half + 1) * LANES, :] = slope
        weights = weight_ref[expert, 2 * D_IN : 2 * D_IN + H1, :]
        bias = column(bias_line(expert, (6, 7, 8)))
        value, slope = silu_parts(matmul_tn(weights, hidden_ref[expert]) + bias)
        output_ref[expert] = value
        output_slope_ref[expert] = slope
        for task in range(TASKS):
            mixed_ref[task * H2 : (task + 1) * H2, :] += (
                gates_ref[pl.ds(task * experts + expert, 1), :] * value
            )
        return carry

    lax.fori_loop(0, experts, forward, 0, unroll=2)

    tower_bias = column(vector_ref[0:1, :])
    head_w = column(vector_ref[1:2, :])
    tower = tower_ref[...]
    act_sums = []
    grad_sums = []
    head_sums = []
    for task in range(TASKS):
        units = slice(task * TOWER, (task + 1) * TOWER)
        outs = slice(task * H2, (task + 1) * H2)
        mixed = mixed_ref[outs, :]
        mixed_low = mixed.astype(BF16)
        tower_part = tower[:, units]
        act, slope = silu_parts(matmul_tn(tower_part, mixed_low) + tower_bias[units])
        score = jnp.sum(act * head_w[units], axis=0, keepdims=True) + head_b_ref[task]
        target = label_ref[task : task + 1, :].astype(F32)
        score_grad = (jax.nn.sigmoid(score) - target) * scale
        tower_grad = (score_grad * head_w[units] * slope).astype(BF16)
        act_sums.append(jnp.sum(score_grad * act, axis=1, keepdims=True))
        grad_sums.append(jnp.sum(tower_grad.astype(F32), axis=1, keepdims=True))
        head_sums.append(jnp.sum(score_grad, axis=1, keepdims=True))
        put_shared(slice(0, H2), units, matmul_nt(mixed_low, tower_grad))
        mixed_grad = matmul(tower_part, tower_grad).astype(BF16).astype(F32)
        mixed_grad_ref[outs, :] = mixed_grad
        dot_ref[task : task + 1, :] = jnp.sum(mixed_grad * mixed, axis=0, keepdims=True)
    column_sums = jnp.concatenate(
        [
            jnp.broadcast_to(jnp.concatenate(sums, axis=0), (LANES, LANES))
            for sums in (act_sums, grad_sums)
        ],
        axis=1,
    )
    put_shared(slice(H2, H2 + 8), whole, jnp.transpose(column_sums[:, :LANES])[0:8])
    put_shared(slice(H2 + 8, H2 + 16), whole, jnp.transpose(column_sums[:, LANES:])[0:8])
    head_line = jnp.zeros((8, LANES), F32)
    for task in range(TASKS):
        head_line = jnp.where(iota((8, LANES), 1) == task, head_sums[task], head_line)
    put_shared(slice(H2 + 16, H2 + 24), whole, head_line)

    input_ref[...] = jnp.zeros_like(input_ref)
    ones = jnp.ones((BIAS_ROWS, width), BF16)

    def backward(expert, carry):
        value = output_ref[expert]
        grad = jnp.zeros((H2, width), F32)
        for task in range(TASKS):
            mixed_grad = mixed_grad_ref[task * H2 : (task + 1) * H2, :]
            gate = gates_ref[pl.ds(task * experts + expert, 1), :]
            grad = grad + gate * mixed_grad
            along = jnp.sum(mixed_grad * value, axis=0, keepdims=True)
            logit_ref[pl.ds(task * experts + expert, 1), :] = gate * (
                along - dot_ref[task : task + 1, :]
            )
        output_grad = (grad * output_slope_ref[expert]).astype(BF16)
        hidden = hidden_ref[expert]
        put_weight(expert, slice(2 * D_IN, 2 * D_IN + H1), matmul_nt(hidden, output_grad))
        weights = weight_ref[expert, 2 * D_IN : 2 * D_IN + H1, :]
        hidden_grad = (matmul(weights, output_grad) * hidden_slope_ref[expert]).astype(BF16)
        turned = turned_ref[...]
        sums = []
        for half in range(H1 // LANES):
            half_grad = hidden_grad[half * LANES : (half + 1) * LANES]
            put_weight(
                expert, slice(half * D_IN, (half + 1) * D_IN), matmul_nt(turned, half_grad)
            )
            weights = weight_ref[expert, half * D_IN : (half + 1) * D_IN, :]
            input_ref[...] += matmul(weights, half_grad)
            sums.append(matmul_nt(ones, half_grad)[0:1])
        sums.append(matmul_nt(ones, output_grad)[0:1])
        sums.append(jnp.zeros((8 - 3, LANES), F32))
        grad_bias_ref[expert] = jnp.concatenate(sums, axis=0)
        return carry

    lax.fori_loop(0, experts, backward, 0, unroll=2)

    logit_grad = logit_ref[...].astype(BF16)
    gate_grad = matmul_nt(logit_grad, turned_ref[...])
    gate_base = H2 + 24
    pairs = TASKS * experts
    for lane_block in range(D_IN // LANES):
        put_shared(
            slice(gate_base + lane_block * pairs, gate_base + (lane_block + 1) * pairs),
            whole,
            gate_grad[:, lane_block * LANES : (lane_block + 1) * LANES],
        )
    low_ref[...] = (input_ref[...] + matmul_tn(gate_ref[...], logit_grad)).astype(BF16)
    bottom_grad = low_ref[EMB_WIDTH:, :]
    dense_base = gate_base + D_IN // LANES * pairs
    grad_dense_w = jnp.concatenate(
        [matmul_nt(dense, bottom_grad), jnp.zeros((DENSE, LANES - BOTTOM), F32)], axis=1
    )
    put_shared(
        slice(dense_base, dense_base + 16),
        whole,
        jnp.concatenate([grad_dense_w, jnp.zeros((16 - DENSE, LANES), F32)], axis=0),
    )
    grad_dense_ref[...] = matmul(dense_w, bottom_grad)

    def clear(step, carry):
        wide_ref[pl.ds(aligned(8 + step * LANES, 8), LANES), :] = jnp.zeros((LANES, LANES), F32)
        return carry

    chunk_rows = buffers[0].shape[0] // FIELDS

    def permute(chunk, words, slot):
        block = lax.div(chunk * chunk_rows, LANES)
        first = chunk * chunk_rows - block * LANES
        span = pl.ds(aligned(block * LANES, LANES), LANES)

        @pl.when(first == 0)
        def _():
            for field in range(FIELDS):
                piece = low_ref[field * EMB : (field + 1) * EMB, span]
                tiled_ref[field] = matmul_nt(eye, jnp.concatenate([piece] * GROUPS, axis=0))

        for step in range(chunk_rows // 8):
            start_row = aligned(first + step * 8, 8)
            for field in range(FIELDS):
                tile = tiled_ref[field, pl.ds(start_row, 8), :]
                for k in range(8):
                    start = words[(step * 8 + k) * FIELDS + field]
                    pltpu.store(wide_ref.at[pl.ds(start, 8), :], tile, mask=lines[k])

    def permute_place(at):
        each = part_rows // chunk_rows
        part = lax.div(at, each)
        return part * (out_ref.shape[0] // PARTS) + (at - part * each) * (chunk_rows * FIELDS)

    word_stream(
        out_ref,
        buffers,
        sems,
        permute_place,
        width // chunk_rows,
        permute,
        lambda: lax.fori_loop(0, slot_blocks, clear, 0, unroll=2),
    )

    def merge(block, carry):
        halves = []
        for half in range(2):
            piece = jnp.zeros((8, LANES), F32)
            for group in range(GROUPS):
                start = aligned(block * LANES + group * 16 + (half + 1) * 8, 8)
                piece = jnp.where(lanes[group], wide_ref[pl.ds(start, 8), :], piece)
            halves.append(piece)
        start = aligned(block * 16, 16)
        sent_ref[pl.ds(start, 16), :] = jnp.concatenate(halves, axis=0).astype(BF16)
        return carry

    lax.fori_loop(0, slot_blocks, merge, 0, unroll=4 if slot_blocks % 4 == 0 else 1)
    each = sent_ref.shape[0] // owners
    for one in range(owners):
        sent_refs[one][...] = sent_ref[one * each : (one + 1) * each, :]


def add_kernel(owners, packed, table_lanes, index_ref, request_ref, asked_ref, *refs):
    received_refs = refs[:owners]
    table_refs = refs[owners : owners + 2 * TABLE_CHUNKS]
    (
        received_ref,
        left_grad_ref,
        right_grad_ref,
        *rest,
    ) = refs[owners + 2 * TABLE_CHUNKS :]
    *buffers, sems = rest[: SLOT_BUFFERS + 1]
    sums = rest[SLOT_BUFFERS + 1 :]
    rows = sums[0].shape[0] - 16
    core, batch = index_ref[0], index_ref[1]
    sources = received_ref.shape[0] // packed
    chunks = packed // 16
    lines, _ = masks()
    eye = identity()
    own_group = lax.shift_right_logical(iota((1, LANES), 1), 4)
    from_lane = iota((LANES, 2 * LANES), 0)
    to_lane = iota((LANES, 2 * LANES), 1)
    spread_names = []
    spread_grads = []
    for pair in range(GROUPS // 2):
        group = pair * 2 + lax.shift_right_logical(to_lane, 7)
        spread_names.append(
            jnp.where(lax.shift_right_logical(from_lane, 4) == group, 1.0, 0.0).astype(BF16)
        )
        wanted = group * EMB + (to_lane & (EMB - 1))
        spread_grads.append(jnp.where(from_lane == wanted, 1.0, 0.0).astype(BF16))

    def place(source):
        distance = lax.div(source, PARTS)
        return (distance ^ batch) * PARTS + source - distance * PARTS

    def spread(source, grad_ref):
        def step(first, count, pair):
            asked = asked_ref[pl.ds(place(source) * chunks + first, count), :]
            names = (own_group - lax.shift_right_logical(asked, table_lanes)) & (GROUPS - 1)
            start = aligned(source * packed + first * 16, 16)
            grads = received_ref[pl.ds(start, count * 16), :]
            lane_group = lax.shift_right_logical(iota((count * 16, LANES), 1), 4).astype(F32)
            wide_names = matmul(slot_lines(names.astype(F32)), spread_names[pair])
            wide_grads = matmul(grads, spread_grads[pair])
            for side in range(2):
                half = slice(side * LANES, (side + 1) * LANES)
                masked = jnp.where(wide_names[:, half] == lane_group, wide_grads[:, half], 0.0)
                for chunk in range(count):
                    start = (first + chunk) * LANES + (pair * 2 + side) * 16
                    grad_ref[start : start + 16, :] = masked[chunk * 16 : (chunk + 1) * 16]

        return [
            functools.partial(step, first, min(4, chunks - first), pair)
            for first in range(0, chunks, 4)
            for pair in range(GROUPS // 2)
        ]

    def clear(step, carry):
        for total in sums:
            total[pl.ds(aligned(8 + step * LANES, 8), LANES), :] = jnp.zeros((LANES, LANES), F32)
        return carry

    def before():
        for total in sums:
            total[0:8, :] = jnp.zeros((8, LANES), F32)
            total[8 + rows : 16 + rows, :] = jnp.zeros((8, LANES), F32)
        lax.fori_loop(0, rows // LANES, clear, 0)
        gather_blocks(received_refs, received_ref)
        for one in spread(0, left_grad_ref):
            one()

    def process(source, words, slot):
        now, later = left_grad_ref, right_grad_ref
        if slot % 2:
            now, later = later, now
        steps = spread(jnp.minimum(source + 1, sources - 1), later)
        rows = GROUPS * packed // 8
        for row in range(rows):
            if row * len(steps) // rows != (row - 1) * len(steps) // rows:
                steps[row * len(steps) // rows]()
            grads = now[row * 8 : (row + 1) * 8, :]
            for k in range(8):
                place = pl.ds(words[row * 8 + k], 8)
                total = sums[k % STREAMS]
                pltpu.store(total.at[place, :], total[place, :] + grads, mask=lines[k])

    size = GROUPS * packed
    word_stream(
        request_ref,
        buffers,
        sems,
        lambda at: place(at) * size,
        sources,
        process,
        before,
    )

    def finish(kept, block, carry):
        start = aligned(8 + block * LANES, 8)
        total = functools.reduce(jnp.add, [one[pl.ds(start, LANES), :] for one in sums])
        turned = matmul_nt(eye, total.astype(BF16)).astype(BF16)
        each = GROUPS // (2 * TABLE_CHUNKS)
        for group in range(GROUPS):
            half, column = divmod(group, GROUPS // 2)
            chunk, column = divmod(column, each)
            table_ref = table_refs[chunk + (0 if half == kept else TABLE_CHUNKS)]
            column = aligned(column * rows + block * LANES, LANES)
            table_ref[:, pl.ds(column, LANES)] = turned[group * EMB : (group + 1) * EMB]
        return carry

    for kept in range(2):

        @pl.when(core == kept)
        def _():
            lax.fori_loop(0, rows // LANES, functools.partial(finish, kept), 0, unroll=8)


def unpack_kernel(weight_piece, extra_piece, pairs, piece_ref, *refs):
    (
        dense_w_ref,
        gate_ref,
        hidden_w_ref,
        hidden_b_ref,
        output_w_ref,
        output_b_ref,
        tower_w_ref,
        tower_b_ref,
        head_w_ref,
        head_b_ref,
        weight_ref,
        extra_ref,
    ) = refs
    for owner in range(piece_ref.shape[0]):
        weight_ref[owner * weight_piece : (owner + 1) * weight_piece, :] = piece_ref[
            owner, :weight_piece, :
        ].astype(F32)
        high = piece_ref[owner, weight_piece : weight_piece + extra_piece, :].astype(F32)
        low = piece_ref[owner, weight_piece + extra_piece :, :].astype(F32)
        extra_ref[owner * extra_piece : (owner + 1) * extra_piece, :] = high + low
    gate_rows = D_IN // LANES * pairs
    small = H2 + gate_rows + 16

    def small_line(row):
        return extra_ref[small + row : small + row + 1, :] + extra_ref[small + 6 + row : small + 7 + row, :]

    for half in range(H1 // LANES):
        span = slice(half * LANES, (half + 1) * LANES)
        hidden_w_ref[0, :, span] = weight_ref[half * D_IN : (half + 1) * D_IN, :]
        hidden_b_ref[:, span] = small_line(3 + half)
    output_w_ref[0] = weight_ref[2 * D_IN : GRAD_ROWS, :]
    output_b_ref[...] = small_line(5)
    tower_w_ref[...] = extra_ref[:H2, :]
    head_w_ref[...] = small_line(0)
    tower_b_ref[...] = small_line(1)
    head_b_ref[...] = small_line(2)[:, :TASKS]
    for block in range(D_IN // LANES):
        gate_ref[:, block * LANES : (block + 1) * LANES] = extra_ref[
            H2 + block * pairs : H2 + (block + 1) * pairs, :
        ]
    dense_w_ref[...] = extra_ref[H2 + gate_rows : H2 + gate_rows + DENSE, :BOTTOM]


SMEM = pl.BlockSpec(memory_space=pltpu.SMEM)
VMEM = pl.BlockSpec(memory_space=pltpu.VMEM)
ANY = pl.BlockSpec(memory_space=pl.ANY)


def call(kernel, outs, ins, scratch, name, micros, vmem=16):
    return pl.pallas_call(
        kernel,
        out_shape=outs,
        in_specs=ins,
        out_specs=jax.tree.map(lambda _: VMEM, outs),
        scratch_shapes=scratch,
        name=name,
        cost_estimate=pl.CostEstimate(
            flops=int(micros * 1.15e9), bytes_accessed=int(micros * 3e6), transcendentals=0
        ),
        compiler_params=pltpu.CompilerParams(vmem_limit_bytes=vmem << 20),
    )


def shards(
    emb_table,
    dense_feats,
    dense_w,
    gate_w,
    hidden_w,
    hidden_b,
    output_w,
    output_b,
    tower_w,
    tower_b,
    head_w,
    head_b,
    row_owner,
    local_row,
    labels,
):
    owners = lax.axis_size("batch")
    experts = lax.axis_size("expert")
    expert_index = lax.axis_index("expert")
    core = expert_index & 1
    row_total = dense_feats.shape[1]
    part_rows = row_total // PARTS
    lookups = row_total * FIELDS
    part_lookups = lookups // PARTS
    capacity = 2 * part_lookups // owners
    packed = -(-capacity // (GROUPS * 16)) * 16
    table_rows = emb_table.shape[0]
    table_packed = table_rows // GROUPS
    table_lanes = table_packed.bit_length() - 1
    scale = 1.0 / math.sqrt(row_total * owners * experts)
    slots = owners * PARTS * GROUPS * packed
    part_slots = owners * packed
    lookup_rows = lookups // LANES
    list_part = -(-lookup_rows // (PARTS * 24)) * 24
    list_rows = list_part * PARTS

    def tie(*values):
        return lax.optimization_barrier(values)

    def exchange(values, axis):
        return lax.all_to_all(values, axis, split_axis=0, concat_axis=0, tiled=True)

    def swap(values, axis, bits):
        size = lax.axis_size(axis)
        return lax.ppermute(values, axis, [(one, one ^ bits) for one in range(size)])

    def swap_all(blocks):
        return [blocks[0]] + [swap(blocks[bits], "batch", bits) for bits in range(1, owners)]

    owner_list = row_owner.reshape(lookup_rows, LANES)
    local_list = local_row.reshape(lookup_rows, LANES)
    slot_rows = slots // LANES
    list_shape = jax.ShapeDtypeStruct((list_rows, LANES), I32)
    batch_index = lax.axis_index("batch").reshape(1)
    requests, back, out = call(
        functools.partial(route_kernel, owners, part_lookups, packed, table_lanes),
        (jax.ShapeDtypeStruct((slot_rows, LANES), I32), list_shape, list_shape),
        [SMEM, VMEM, VMEM],
        [pltpu.VMEM((list_rows, LANES), I32)] * 3 + [pltpu.VMEM((PARTS, slot_rows // PARTS, 2 * LANES), F32)],
        "route",
        9,
    )(batch_index, owner_list, local_list)
    asked = exchange(requests.reshape(owners, slots // owners), "batch")
    asked = asked.reshape(slot_rows, LANES)
    offset = 8 - (jnp.arange(LANES, dtype=I32) & 7)
    words = ((asked & (table_packed - 1)) + offset).reshape(-1)
    back = back.reshape(-1)
    out = out.reshape(-1)

    hidden_b, out = tie(hidden_b, out)
    table, weights = call(
        pack_kernel,
        (
            pltpu.VMEM((table_packed + 16, LANES), F32),
            jax.ShapeDtypeStruct((WEIGHT_ROWS, LANES), BF16),
        ),
        [VMEM] * 5,
        [],
        "pack",
        5,
    )(emb_table.T, hidden_w, output_w, hidden_b, output_b)
    table = pltpu.with_memory_space_constraint(table, pltpu.VMEM)
    weights = lax.all_gather(weights, "expert", axis=0, tiled=False)

    slot_words = [pltpu.SMEM((GROUPS * packed,), I32)] * SLOT_BUFFERS
    slot_words.append(pltpu.SemaphoreType.DMA((SLOT_BUFFERS,)))
    row_words = [pltpu.SMEM((CHUNK_ROWS * FIELDS,), I32)] * ROW_BUFFERS
    row_words.append(pltpu.SemaphoreType.DMA((ROW_BUFFERS,)))
    returned = []
    for part in range(PARTS):
        found = call(
            functools.partial(fetch_kernel, owners, part, packed, table_lanes),
            jax.ShapeDtypeStruct((part_slots, LANES), BF16),
            [ANY, VMEM, VMEM],
            [
                pltpu.VMEM((part_slots, LANES), F32),
                pltpu.VMEM((GROUPS * packed, LANES), F32),
            ]
            + slot_words,
            "fetch",
            24 // PARTS,
        )(words, asked, table)
        found = exchange(found.reshape(owners, packed, LANES), "batch")
        returned.append(found.reshape(part_slots, LANES))
    early = []
    for part in range(PARTS - 1):
        early.append(
            call(
                functools.partial(unpermute_kernel, part, part_rows),
                jax.ShapeDtypeStruct((part_rows, D_IN), BF16),
                [ANY, VMEM],
                [pltpu.VMEM((GROUPS * part_slots + 16, LANES), F32), *row_words],
                "unpermute",
                15,
            )(back, returned[part])
        )

    pairs = TASKS * experts
    shared_rows = H2 + 24 + D_IN // LANES * pairs + 16
    vectors = jnp.stack([tower_b, head_w])
    *sent, grad_dense, grad_weight, grad_bias, grad_shared = call(
        functools.partial(dense_kernel, owners, part_rows, experts, scale),
        (
            *[jax.ShapeDtypeStruct((PARTS * packed, LANES), BF16)] * owners,
            jax.ShapeDtypeStruct((DENSE, row_total), F32),
            jax.ShapeDtypeStruct((experts, GRAD_ROWS, LANES), BF16),
            jax.ShapeDtypeStruct((experts, 8, LANES), F32),
            jax.ShapeDtypeStruct((shared_rows, LANES), F32),
        ),
        [ANY, ANY] + [VMEM] * 7 + [SMEM] + [VMEM] * PARTS,
        [
            pltpu.VMEM((slots + 16, LANES), F32),
            pltpu.VMEM((row_total, D_IN), BF16),
            pltpu.VMEM((D_IN, row_total), BF16),
            pltpu.VMEM((experts, H1, row_total), BF16),
            pltpu.VMEM((experts, H1, row_total), F32),
            pltpu.VMEM((experts, H2, row_total), F32),
            pltpu.VMEM((experts, H2, row_total), F32),
            pltpu.VMEM((pairs, row_total), F32),
            pltpu.VMEM((TASKS * H2, row_total), F32),
            pltpu.VMEM((TASKS * H2, row_total), F32),
            pltpu.VMEM((8, row_total), F32),
            pltpu.VMEM((pairs, row_total), F32),
            pltpu.VMEM((D_IN, row_total), F32),
            pltpu.VMEM((D_IN, row_total), BF16),
            pltpu.VMEM((FIELDS, LANES, LANES), F32),
            pltpu.VMEM((PARTS * part_slots, LANES), BF16),
            *row_words,
        ],
        "dense",
        45,
        56,
    )(
        back,
        out,
        returned[-1],
        weights,
        gate_w.T,
        dense_feats,
        dense_w,
        tower_w,
        vectors,
        head_b,
        labels,
        *early,
    )
    received = swap_all(sent)

    def split(values):
        high = lax.reduce_precision(values, exponent_bits=8, mantissa_bits=7)
        return high.astype(BF16), (values - high).astype(BF16)

    far = owners // 2
    received[far], grad_weight, grad_bias, grad_shared = tie(
        received[far], grad_weight, grad_bias, grad_shared
    )

    def spread_rows(values, piece):
        rows = values.shape[1]
        values = jnp.pad(values, ((0, 0), (0, piece * owners - rows), (0, 0)))
        return values.reshape(experts, owners, piece, LANES).transpose(1, 0, 2, 3)

    large = jnp.concatenate([grad_shared[:H2], grad_shared[H2 + 24 :]], axis=0).astype(BF16)
    small = jnp.concatenate([grad_shared[H2 + 8 * row : H2 + 8 * row + 1] for row in range(3)])
    small = jnp.concatenate(
        [jnp.broadcast_to(small[None], (experts, 3, LANES)), grad_bias[:, :3]], axis=1
    )
    extra = jnp.concatenate(
        [jnp.broadcast_to(large[None], (experts, *large.shape)), *split(small)], axis=1
    )
    weight_piece = -(-GRAD_ROWS // (16 * owners)) * 16
    extra_piece = -(-extra.shape[1] // (16 * owners)) * 16
    piece_rows = weight_piece + extra_piece
    pieces = jnp.concatenate(
        [spread_rows(grad_weight, weight_piece), spread_rows(extra, extra_piece)], axis=2
    )
    late = owners - 2
    *received[:late], pieces = tie(*received[:late], pieces)
    pieces = exchange(pieces.reshape(owners * experts, piece_rows, LANES), ("batch", "expert"))

    columns = table_rows // 2 // TABLE_CHUNKS
    table_part = call(
        functools.partial(add_kernel, owners, packed, table_lanes),
        (jax.ShapeDtypeStruct((EMB, columns), BF16),) * (2 * TABLE_CHUNKS),
        [SMEM, ANY, VMEM] + [VMEM] * owners,
        [pltpu.VMEM((PARTS * part_slots, LANES), BF16)]
        + [pltpu.VMEM((GROUPS * packed, LANES), F32)] * 2
        + slot_words
        + [pltpu.VMEM((table_packed + 16, LANES), F32)] * STREAMS,
        "add",
        60,
        48,
    )(jnp.concatenate([core.reshape(1), batch_index]), words, asked, *received)

    def add_low(left, right):
        return (left.astype(F32) + right.astype(F32)).astype(BF16)

    *table_part, pieces = tie(*table_part, pieces)
    kept = [
        add_low(one, swap(other, "expert", 1))
        for one, other in zip(table_part[:TABLE_CHUNKS], table_part[TABLE_CHUNKS:])
    ]
    *kept, pieces = tie(*kept, pieces)
    over = [swap(one, "expert", 2) for one in kept]
    sums = jnp.sum(pieces.astype(F32), axis=0)
    piece = jnp.concatenate([sums[:weight_piece].astype(BF16), *split(sums[weight_piece:])], axis=0)
    pieces = exchange(jnp.broadcast_to(piece[None], (owners, *piece.shape)), "batch")
    bit = 2
    while bit < experts:
        kept = [add_low(one, other) for one, other in zip(kept, over)]
        bit *= 2
        if bit < experts:
            over = [swap(one, "expert", bit) for one in kept]
    small = call(
        functools.partial(unpack_kernel, weight_piece, extra_piece, pairs),
        tuple(
            jax.ShapeDtypeStruct(shape, F32)
            for shape in (
                (DENSE, BOTTOM),
                (pairs, D_IN),
                (1, D_IN, H1),
                (1, H1),
                (1, H1, H2),
                (1, H2),
                (H2, TASKS * TOWER),
                (1, TASKS * TOWER),
                (1, TASKS * TOWER),
                (1, TASKS),
            )
        ),
        [VMEM],
        [
            pltpu.VMEM((owners * weight_piece, LANES), F32),
            pltpu.VMEM((owners * extra_piece, LANES), F32),
        ],
        "unpack",
        3,
    )(pieces)
    others = [swap(one, "expert", 1) for one in kept]
    *others, small = tie(*others, small)
    lower = [jnp.where(core == 0, one, other) for one, other in zip(kept, others)]
    upper = [jnp.where(core == 0, other, one) for one, other in zip(kept, others)]
    table_total = jnp.concatenate(lower + upper, axis=1).astype(F32).T
    grad_dense_w, gate, hidden, hidden_bias, output, output_bias, tower, tower_bias, head, head_bias = (
        small
    )
    return (
        table_total,
        grad_dense,
        grad_dense_w,
        gate.T,
        hidden,
        hidden_bias,
        output,
        output_bias,
        tower,
        tower_bias.reshape(-1),
        head.reshape(-1),
        head_bias.reshape(-1),
    )


def solution(mesh):
    in_specs = (
        P("batch", None),
        P(None, ("batch", "expert")),
        P(),
        P(),
        P("expert", None, None),
        P("expert", None),
        P("expert", None, None),
        P("expert", None),
        P(),
        P(),
        P(),
        P(),
        P(("batch", "expert"), None),
        P(("batch", "expert")),
        P(None, ("batch", "expert")),
    )
    out_specs = (
        P("batch", None),
        P(None, ("batch", "expert")),
        P(),
        P(),
        P("expert", None, None),
        P("expert", None),
        P("expert", None, None),
        P("expert", None),
        P(),
        P(),
        P(),
        P(),
    )
    return jax.shard_map(shards, mesh=mesh, in_specs=in_specs, out_specs=out_specs, check_vma=False)
```
